32 devices in a mesh: grp: 2 (over x), gx: 8 (over z, y), gy: 2 (over core).
Axes of the slice: x: 2, y: 2, z: 4, core: 2. Of those that a mesh axis runs over, the one named last changes fastest.
Arguments:
- tokens: bfloat16 [256, 18432], P(('grp', 'gy'), 'gx'), parts along dimension 0, may hold values from -6 to 6
- query_weight: bfloat16 [18432, 6144], P('gx', 'gy'), may hold values from -0.046875 to 0.046875
- kv_weight: bfloat16 [18432, 512], P('gx'), may hold values from -0.046875 to 0.046875
- out_weight: bfloat16 [6144, 18432], P('gy', 'gx'), may hold values from -0.078125 to 0.078125
- key_cache: bfloat16 [256, 1024, 256], P(('grp', 'gx', 'gy')), parts along dimension 0, may hold values from -640 to 640
- value_cache: bfloat16 [256, 1024, 256], P(('grp', 'gx', 'gy')), parts along dimension 0, may hold values from -6 to 6
- lengths: int32 [256], P(('grp', 'gx', 'gy')), parts along dimension 0, may hold values from 256 to 1024, as said below
Outputs:
- mixed: bfloat16 [256, 18432], P(('grp', 'gy'), 'gx'), parts along dimension 0
The draws below stay inside these ranges and needn't reach their ends.
There are 2 independent parts, one for each index of `grp`. The reference program is written for one: setup_inputs(seed, part) draws one part's arguments, and reference() takes and returns one part's arrays. A program takes and returns all parts, laid end to end along the dimension named above; an argument that names none is the same for every part. Nothing has to cross between parts.
Inputs may be any that keep to these rules, and one draw needn't show every extreme that they name: `lengths`: one batch row holds exactly 1024 valid positions and one exactly 256.
All inputs are finite; a program needn't handle non-finite values.
Results may differ from the reference program's by a relative error of at most 0.012.
The reference program's roundings to bfloat16 on the way count: a program that leaves them out, or rounds other values in their place, can miss the bound.
Values may be sent and summed in bfloat16 or wider, within the bound.
No kernel may reach another device: no remote copies, remote signals or barrier semaphores. Data moves between devices by JAX's collectives and lax.ppermute only.
A program may use at most 128 MiB of HBM per device.

```python
import jax
import jax.numpy as jnp
from jax import lax

D = 18432
H = 24
DH = 256
L = 1024
B = 128


def draw_key_cache(key, part):
    key = jax.random.fold_in(key, 11)
    key_base = jax.random.fold_in(key, 0)
    base = jax.random.truncated_normal(key_base, -4.5, 4.5, (B, L, DH), jnp.float32)
    return base.astype(jnp.bfloat16)


def draw_lengths(key, part):
    key = jax.random.fold_in(key, 23)
    key_len, key_pick = jax.random.split(key)
    drawn = jax.random.randint(key_len, (B,), L // 4, L + 1)
    order = jax.random.permutation(key_pick, B)
    drawn = drawn.at[order[0]].set(L)
    drawn = drawn.at[order[1]].set(L // 4)
    return drawn.astype(jnp.int32)


def with_spikes(array, rng, source, target, shards_of, factor):
    def block_of(position):
        return (jnp.arange(array.shape[position]) // (array.shape[position] // shards_of)).reshape((-1,) + (1,) * (array.ndim - 1 - position))

    first = jax.random.permutation(rng, shards_of)[block_of(target)]
    other_side = (block_of(target) + shards_of // 2) % shards_of
    return jnp.where((block_of(source) == first) | (block_of(source) == other_side), factor * array, array)


def shard_levels(own_key, dims, cuts, low, top_value):
    def one(dim, shards_of):
        draws = jax.random.uniform(jax.random.fold_in(jax.random.fold_in(own_key, 6), dim), (shards_of,), jnp.float32, low / len(cuts), top_value / len(cuts))
        return jnp.repeat(jnp.exp(draws), dims[dim] // shards_of).reshape((-1,) + (1,) * (len(dims) - dim - 1))

    loudness = one(*cuts[0])
    for cut in cuts[1:]:
        loudness = loudness * one(*cut)
    return loudness


def bell_draw(own_key, shape, spread, reach, pieces=(), kind=jnp.bfloat16):
    loudness = shard_levels(own_key, shape, pieces, -0.22, 0.18) if pieces else 1.0
    entries = jax.random.normal(own_key, shape, jnp.float32) * spread * loudness
    return jnp.minimum(jnp.maximum(entries, -reach), reach).astype(kind)


def noise_with(stream_key, dims, width, most, cuts, heavy, kind=jnp.bfloat16):
    entries = width * jax.random.normal(stream_key, dims, jnp.float32)
    if cuts:
        entries = entries * shard_levels(stream_key, dims, cuts, -0.22, 0.18)
    return jnp.clip(with_spikes(entries, jax.random.fold_in(stream_key, 3), *heavy), -most, most).astype(kind)


def setup_inputs(seed: int = 0, part: int = 0) -> dict:
    streams_of = jax.random.split(jax.random.key(seed), 8)
    part_keys = jax.random.split(jax.random.fold_in(streams_of[7], part), 8)
    tokens = noise_with(part_keys[0], (B, D), 1.0, 6.0, ((0, 2), (1, 8)), (1, 0, 8, 2.0))
    query_weight = bell_draw(streams_of[1], (D, H * DH), D ** -0.5, 0.046875, ((0, 8), (1, 2)))
    kv_weight = bell_draw(streams_of[2], (D, 2 * DH), D ** -0.5, 0.046875, ((0, 8),))
    out_weight = bell_draw(streams_of[3], (H * DH, D), (H * DH) ** -0.5, 0.078125, ((0, 2), (1, 8)))
    key_cache = draw_key_cache(jax.random.fold_in(jax.random.fold_in(streams_of[7], part), 71), part)
    value_cache = bell_draw(part_keys[5], (B, L, DH), 1.0, 6.0, ((0, 16),))
    lengths = draw_lengths(jax.random.fold_in(jax.random.fold_in(streams_of[7], part), 71), part)
    return {"tokens": tokens, "query_weight": query_weight, "kv_weight": kv_weight, "out_weight": out_weight, "key_cache": key_cache, "value_cache": value_cache, "lengths": lengths}


def attend_row(items):
    query, keys, values, length, fresh_row = items
    score_scale = DH ** -0.5
    query_float = query.astype(jnp.float32)
    scores = jnp.dot(query_float, keys.astype(jnp.float32).T, precision=lax.Precision.HIGHEST) * score_scale
    new_key = fresh_row[:DH].astype(jnp.float32)
    new_value = fresh_row[DH:].astype(jnp.float32)
    self_score = jnp.dot(query_float, new_key, precision=lax.Precision.HIGHEST) * score_scale
    visible = jnp.arange(L, dtype=jnp.int32) < length
    masked = jnp.where(visible[None, :], scores, jnp.float32(-1e30))
    peak_score = jnp.maximum(jnp.max(masked, axis=1), self_score)
    raised = jnp.where(visible[None, :], jnp.exp(masked - peak_score[:, None]), jnp.float32(0.0))
    self_raised = jnp.exp(self_score - peak_score)
    denominator = jnp.sum(raised, axis=1) + self_raised
    weights = (raised / denominator[:, None]).astype(jnp.bfloat16)
    self_weight = (self_raised / denominator).astype(jnp.bfloat16)
    summed = jnp.dot(weights.astype(jnp.float32), values.astype(jnp.float32), precision=lax.Precision.HIGHEST)
    summed = summed + self_weight.astype(jnp.float32)[:, None] * new_value[None, :]
    return summed.astype(jnp.bfloat16).reshape(H * DH)


def reference(tokens, query_weight, kv_weight, out_weight, key_cache, value_cache, lengths):
    queries = jnp.dot(tokens, query_weight, preferred_element_type=jnp.float32).astype(jnp.bfloat16)
    queries = queries.reshape(B, H, DH)
    fresh = jnp.dot(tokens, kv_weight, preferred_element_type=jnp.float32).astype(jnp.bfloat16)
    attended = lax.map(attend_row, (queries, key_cache, value_cache, lengths, fresh))
    return jnp.dot(attended, out_weight, preferred_element_type=jnp.float32).astype(jnp.bfloat16)
```

```python
import functools

import jax
import jax.numpy as jnp
from jax import lax
from jax.experimental import pallas as pl
from jax.experimental.pallas import tpu as pltpu
from jax.sharding import PartitionSpec as P

H = 24
DH = 256
CHUNKS = 4
GROUPS = 2
VMEM_LIMIT = 40 * 1024 * 1024


def tile_of(width, wanted):
    while wanted >= 128:
        if width % wanted == 0:
            return wanted
        wanted -= 128
    return width


def build_rows(n, rows, ids_ref, own_ref, other_ref, xs_ref):
    me, core = ids_ref[0], ids_ref[1]
    half = n // 2
    for m in range(half):
        for bit, base in ((1, 0), (0, half)):
            block = jnp.bitwise_xor(me, 2 * m + bit)
            source = pl.ds(pl.multiple_of((block % half) * rows, rows), rows)
            target = pl.ds((base + m) * rows, rows)
            mine = block // half == core

            @pl.when(mine)
            def _():
                xs_ref[target, :] = own_ref[source, :]

            @pl.when(jnp.logical_not(mine))
            def _():
                xs_ref[target, :] = other_ref[source, :]


def project_kernel(n, rows, with_kv, ids_ref, own_ref, other_ref, w_ref, *refs):
    if with_kv:
        kv_ref, send_ref, keep_ref, xs_ref = refs
    else:
        send_ref, keep_ref, xs_ref = refs
    step = pl.program_id(0)

    @pl.when(step == 0)
    def _():
        build_rows(n, rows, ids_ref, own_ref, other_ref, xs_ref)

    def put(weight):
        total = jnp.dot(xs_ref[...], weight, preferred_element_type=jnp.float32)
        half = total.shape[0] // 2
        send_ref[...] = total[:half]
        keep_ref[...] = total[half:]

    if with_kv:

        @pl.when(step == 0)
        def _():
            put(kv_ref[...])

        @pl.when(step > 0)
        def _():
            put(w_ref[...])
    else:
        put(w_ref[...])


def project(n, rows, ids, own, other, query_weight, kv_weight, chunk, width):
    features = own.shape[1]
    tile = DH
    first = chunk * width // tile
    steps = width // tile
    with_kv = kv_weight is not None
    extra = 1 if with_kv else 0
    whole = pl.BlockSpec(own.shape, lambda i, ids: (0, 0))
    in_specs = [
        whole,
        whole,
        pl.BlockSpec((features, tile), lambda i, ids: (0, first + jnp.maximum(i - extra, 0))),
    ]
    operands = [own, other, query_weight]
    if with_kv:
        in_specs.append(pl.BlockSpec((features, tile), lambda i, ids: (0, ids[1])))
        operands.append(kv_weight)
    half_rows = n * rows // 2
    columns = width + extra * tile
    out = jax.ShapeDtypeStruct((half_rows, columns), jnp.float32)
    return pl.pallas_call(
        functools.partial(project_kernel, n, rows, with_kv),
        out_shape=(out, out),
        grid_spec=pltpu.PrefetchScalarGridSpec(
            num_scalar_prefetch=1,
            grid=(steps + extra,),
            in_specs=in_specs,
            out_specs=[pl.BlockSpec((half_rows, tile), lambda i, ids: (0, i))] * 2,
            scratch_shapes=[pltpu.VMEM((n * rows, features), own.dtype)],
        ),
        compiler_params=pltpu.CompilerParams(vmem_limit_bytes=VMEM_LIMIT),
        cost_estimate=pl.CostEstimate(
            flops=2 * n * rows * features * columns,
            bytes_accessed=2 * features * columns + 4 * n * rows * columns,
            transcendentals=0,
        ),
        name="project",
    )(ids, *operands)


def attend_kernel(parts, per_part, offset, scalars_ref, *refs):
    own_q = refs[:parts]
    other_q = refs[parts : 2 * parts]
    kv_own, kv_other, k_ref, v_ref, own_out, other_out, q_scr, o_scr, kv_scr = refs[2 * parts :]
    row = pl.program_id(0)
    heads = 2 * parts * per_part
    core = scalars_ref[0]

    @pl.when(row == 0)
    def _():
        q_scr[...] = jnp.zeros_like(q_scr)
        first, second = kv_own[...].astype(jnp.float32), kv_other[...].astype(jnp.float32)
        kv_scr[0] = jnp.where(core == 0, first, second)
        kv_scr[1] = jnp.where(core == 0, second, first)
        for part in range(2 * parts):
            ref = (own_q + other_q)[part]
            skip = offset if part % parts == 0 else 0
            for head in range(per_part):
                at = skip + head * DH
                q_scr[:, part * per_part + head, :] = ref[:, at : at + DH].astype(jnp.float32)

    scale = DH**-0.5
    query = q_scr[row]
    keys = k_ref[0]
    scores = scale * lax.dot_general(
        query.astype(jnp.bfloat16), keys, (((1,), (1,)), ((), ())), preferred_element_type=jnp.float32
    )
    new_key = kv_scr[0, pl.ds(row, 1), :]
    new_value = kv_scr[1, pl.ds(row, 1), :]
    self_score = scale * jnp.sum(query * new_key, axis=1, keepdims=True)
    visible = lax.broadcasted_iota(jnp.int32, scores.shape, 1) < scalars_ref[1 + row]
    masked = jnp.where(visible, scores, jnp.float32(-1e30))
    peak = jnp.maximum(jnp.max(masked, axis=1, keepdims=True), self_score)
    raised = jnp.where(visible, jnp.exp(masked - peak), jnp.float32(0.0))
    self_raised = jnp.exp(self_score - peak)
    denominator = jnp.sum(raised, axis=1, keepdims=True) + self_raised
    weights = (raised / denominator).astype(jnp.bfloat16)
    self_weight = (self_raised / denominator).astype(jnp.bfloat16).astype(jnp.float32)
    total = jnp.dot(weights, v_ref[0], preferred_element_type=jnp.float32)
    o_scr[row] = total + self_weight * new_value

    @pl.when(row == pl.num_programs(0) - 1)
    def _():
        for head in range(heads):
            ref = own_out if head < heads // 2 else other_out
            at = (head % (heads // 2)) * DH
            ref[:, at : at + DH] = o_scr[:, head, :].astype(jnp.bfloat16)


def attend(core, lengths, own_q, other_q, offset, kv_own, kv_other, keys, values):
    parts = len(own_q)
    rows, positions, _ = keys.shape
    per_part = (own_q[0].shape[1] - offset) // DH
    heads = 2 * parts * per_part
    padded = -(-heads // 16) * 16

    def whole(array):
        return pl.BlockSpec(array.shape, lambda b, s: (0, 0))

    cache = pl.BlockSpec((1, positions, DH), lambda b, s: (b, 0, 0))
    out = jax.ShapeDtypeStruct((rows, heads * DH // 2), jnp.bfloat16)
    scalars = jnp.concatenate([core[None], lengths])
    return pl.pallas_call(
        functools.partial(attend_kernel, parts, per_part, offset),
        out_shape=(out, out),
        grid_spec=pltpu.PrefetchScalarGridSpec(
            num_scalar_prefetch=1,
            grid=(rows,),
            in_specs=[whole(a) for a in (*own_q, *other_q, kv_own, kv_other)] + [cache, cache],
            out_specs=[whole(out), whole(out)],
            scratch_shapes=[
                pltpu.VMEM((rows, padded, DH), jnp.float32),
                pltpu.VMEM((rows, padded, DH), jnp.float32),
                pltpu.VMEM((2, rows, DH), jnp.float32),
            ],
        ),
        compiler_params=pltpu.CompilerParams(vmem_limit_bytes=VMEM_LIMIT),
        cost_estimate=pl.CostEstimate(
            flops=4 * rows * padded * positions * DH,
            bytes_accessed=4 * rows * positions * DH,
            transcendentals=rows * padded * positions,
        ),
        name="attend",
    )(scalars, *own_q, *other_q, kv_own, kv_other, keys, values)


def output_kernel(n, rows, with_prior, ids_ref, *refs):
    blocks = refs[:n]
    if with_prior:
        w_ref, send_in, keep_in, send_ref, keep_ref, xs_ref = refs[n:]
    else:
        w_ref, send_ref, keep_ref, xs_ref = refs[n:]
    me, core = ids_ref[0], ids_ref[1]
    half = n // 2

    @pl.when(pl.program_id(0) == 0)
    def _():
        for j in range(n):
            block = jnp.bitwise_xor(me, j)
            place = block % half + jnp.where(block // half == core, half, 0)
            xs_ref[pl.ds(pl.multiple_of(place * rows, rows), rows), :] = blocks[j][...]

    total = jnp.dot(xs_ref[...], w_ref[...], preferred_element_type=jnp.float32)
    cut = half * rows
    if with_prior:
        send_ref[...] = send_in[...] + total[:cut]
        keep_ref[...] = keep_in[...] + total[cut:]
    else:
        send_ref[...] = total[:cut]
        keep_ref[...] = total[cut:]


def project_out(n, rows, ids, blocks, out_weight, group, prior):
    depth = blocks[0].shape[1]
    columns = out_weight.shape[1]
    tile = tile_of(columns, 768)
    half_rows = n * rows // 2
    out = jax.ShapeDtypeStruct((half_rows, columns), jnp.float32)
    piece = pl.BlockSpec((half_rows, tile), lambda i, ids: (0, i))
    in_specs = [pl.BlockSpec(b.shape, lambda i, ids: (0, 0)) for b in blocks]
    in_specs.append(pl.BlockSpec((depth, tile), lambda i, ids: (group, i)))
    operands = [*blocks, out_weight]
    if prior is not None:
        in_specs += [piece, piece]
        operands += list(prior)
    return pl.pallas_call(
        functools.partial(output_kernel, n, rows, prior is not None),
        out_shape=(out, out),
        grid_spec=pltpu.PrefetchScalarGridSpec(
            num_scalar_prefetch=1,
            grid=(columns // tile,),
            in_specs=in_specs,
            out_specs=[piece, piece],
            scratch_shapes=[pltpu.VMEM((n * rows, depth), jnp.bfloat16)],
        ),
        compiler_params=pltpu.CompilerParams(vmem_limit_bytes=VMEM_LIMIT),
        cost_estimate=pl.CostEstimate(
            flops=2 * n * rows * depth * columns,
            bytes_accessed=2 * depth * columns + 4 * n * rows * columns,
            transcendentals=0,
        ),
        name="project_out",
    )(ids, *operands)


def local(tokens, query_weight, kv_weight, out_weight, key_cache, value_cache, lengths):
    n = lax.axis_size("gx")
    me = lax.axis_index("gx").astype(jnp.int32)
    core = lax.axis_index("gy").astype(jnp.int32)
    ids = jnp.stack([me, core])
    own_rows = key_cache.shape[0]
    rows = 2 * own_rows
    half = n // 2

    def swap(array):
        return lax.ppermute(array, "gy", [(0, 1), (1, 0)])

    def across(array, mask):
        return lax.ppermute(array, "gx", [(g, g ^ mask) for g in range(n)])

    other_tokens = swap(tokens)
    width = query_weight.shape[1] // CHUNKS

    mine, theirs = [], []
    for chunk in range(CHUNKS):
        send, keep = project(
            n, rows, ids, tokens, other_tokens, query_weight, kv_weight if chunk == 0 else None, chunk, width
        )
        received = across(send, 1)
        parts = [keep[m * rows : (m + 1) * rows] + received[m * rows : (m + 1) * rows] for m in range(half)]
        total = parts[0]
        for m in range(1, half):
            total = total + across(parts[m], 2 * m)
        mine.append(lax.dynamic_slice_in_dim(total, core * own_rows, own_rows, 0).astype(jnp.bfloat16))
        give = lax.dynamic_slice_in_dim(total, (1 - core) * own_rows, own_rows, 0).astype(jnp.bfloat16)
        theirs.append(swap(give))

    kv_own, kv_other = mine[0][:, :DH], theirs[0][:, :DH]
    mine[0], theirs[0] = mine[0][:, DH:], theirs[0][:, DH:]

    per_group = CHUNKS // GROUPS
    prior = None
    for group in range(GROUPS):
        at = slice(group * per_group, (group + 1) * per_group)
        own, other = attend(
            core, lengths, mine[at], theirs[at], 0, kv_own, kv_other, key_cache, value_cache
        )
        got = swap(other)
        block = jnp.where(core == 0, jnp.concatenate([own, got]), jnp.concatenate([got, own]))
        near = [block] + [across(block, 2 * m) for m in range(1, half)]
        far = [across(b, 1) for b in near]
        blocks = [b for pair in zip(near, far) for b in pair]
        prior = project_out(n, rows, ids, blocks, out_weight, group, prior)
    send, keep = prior
    return (keep + swap(send)).astype(jnp.bfloat16)


def solution(mesh):
    return jax.shard_map(
        local,
        mesh=mesh,
        in_specs=(
            P(("grp", "gy"), "gx"),
            P("gx", "gy"),
            P("gx", None),
            P("gy", "gx"),
            P(("grp", "gx", "gy"), None, None),
            P(("grp", "gx", "gy"), None, None),
            P(("grp", "gx", "gy")),
        ),
        out_specs=P(("grp", "gy"), "gx"),
        check_vma=False,
    )
```

```python
import functools

import jax
import jax.numpy as jnp
from jax import lax
from jax.experimental import pallas as pl
from jax.experimental.pallas import tpu as pltpu
from jax.sharding import PartitionSpec as P

H = 24
DH = 256
MIB = 1024 * 1024
ANY = pl.BlockSpec(memory_space=pl.ANY)
VMEM = pl.BlockSpec(memory_space=pltpu.VMEM)
SMEM = pl.BlockSpec(memory_space=pltpu.SMEM)


def tile_of(width, wanted):
    while wanted >= 128:
        if width % wanted == 0:
            return wanted
        wanted -= 128
    return width


def order_of(bits):
    order = [0]
    for bit in reversed(bits):
        order = order + [j + bit for j in order]
    return order


def project_kernel(order, rows, first, tile, kv_width, ids_ref, own_ref, other_ref, w_ref, *refs):
    if kv_width:
        kv_ref, send_ref, keep_ref, xs_ref, ws_ref, kvs_ref, row_sem, w_sem, kv_sem = refs
    else:
        send_ref, keep_ref, xs_ref, ws_ref, row_sem, w_sem = refs
    n = len(order)
    half = n // 2
    tiles = ws_ref.shape[0]
    me, core = ids_ref[0], ids_ref[1]

    def row_copy(source_ref, p):
        block = jnp.bitwise_xor(me, order[p])
        source = pl.ds(pl.multiple_of((block % half) * rows, rows), rows)
        return pltpu.make_async_copy(
            source_ref.at[source, :], xs_ref.at[pl.ds(p * rows, rows), :], row_sem.at[p]
        )

    def weight_copy(t):
        return pltpu.make_async_copy(
            w_ref.at[:, pl.ds(first + t * tile, tile)], ws_ref.at[t], w_sem.at[t]
        )

    for p in range(n):
        mine = jnp.bitwise_xor(me, order[p]) // half == core

        @pl.when(mine)
        def _():
            row_copy(own_ref, p).start()

        @pl.when(jnp.logical_not(mine))
        def _():
            row_copy(other_ref, p).start()

    if kv_width:
        kv_copy = pltpu.make_async_copy(
            kv_ref.at[:, pl.ds(pl.multiple_of(core * kv_width, kv_width), kv_width)], kvs_ref, kv_sem
        )
        kv_copy.start()
    for t in range(tiles):
        weight_copy(t).start()
    for p in range(n):
        row_copy(own_ref, p).wait()

    cut = half * rows

    def put(weight, at, width):
        total = jnp.dot(xs_ref[...], weight, preferred_element_type=jnp.float32)
        keep_ref[:, at : at + width] = total[:cut]
        send_ref[:, at : at + width] = total[cut:]

    if kv_width:
        kv_copy.wait()
        put(kvs_ref[...], 0, kv_width)
    for t in range(tiles):
        weight_copy(t).wait()
        put(ws_ref[t], kv_width + t * tile, tile)


def project(bits, rows, ids, own, other, query_weight, kv_weight, first, width):
    features = own.shape[1]
    order = order_of(bits)
    n = len(order)
    tile = tile_of(width, 512)
    kv_width = kv_weight.shape[1] // 2 if kv_weight is not None else 0
    columns = width + kv_width
    out = jax.ShapeDtypeStruct((n * rows // 2, columns), jnp.float32)
    scratch = [
        pltpu.VMEM((n * rows, features), own.dtype),
        pltpu.VMEM((width // tile, features, tile), own.dtype),
    ]
    sems = [pltpu.SemaphoreType.DMA((n,)), pltpu.SemaphoreType.DMA((width // tile,))]
    operands = [ids, own, other, query_weight]
    if kv_width:
        scratch.append(pltpu.VMEM((features, kv_width), own.dtype))
        sems.append(pltpu.SemaphoreType.DMA)
        operands.append(kv_weight)
    return pl.pallas_call(
        functools.partial(project_kernel, order, rows, first, tile, kv_width),
        out_shape=(out, out),
        in_specs=[SMEM] + [ANY] * (len(operands) - 1),
        out_specs=(VMEM, VMEM),
        scratch_shapes=scratch + sems,
        compiler_params=pltpu.CompilerParams(vmem_limit_bytes=16 * MIB),
        cost_estimate=pl.CostEstimate(
            flops=2 * n * rows * features * columns,
            bytes_accessed=2 * features * columns + 4 * n * rows * columns,
            transcendentals=0,
        ),
        name="project",
    )(*operands)


def attend_kernel(parts, scalars_ref, *refs):
    own_q, other_q = refs[: len(parts)], refs[len(parts) : 2 * len(parts)]
    k_ref, v_ref, own_out, other_out, q_scr, o_scr = refs[2 * len(parts) :]
    core = scalars_ref[0]
    rows, positions, _ = k_ref.shape
    at = 0
    for side in (own_q, other_q):
        for ref, (heads, skip) in zip(side, parts):
            for head in range(heads):
                column = skip + head * DH
                q_scr[:, at, :] = ref[:, column : column + DH].astype(jnp.float32)
                at += 1
    total_heads = at
    first = own_q[0][:, :DH].astype(jnp.float32)
    second = other_q[0][:, :DH].astype(jnp.float32)
    new_keys = jnp.where(core == 0, first, second)
    new_values = jnp.where(core == 0, second, first)
    scale = DH**-0.5
    for row in range(rows):
        query = q_scr[row]
        scores = scale * lax.dot_general(
            query.astype(jnp.bfloat16),
            k_ref[row],
            (((1,), (1,)), ((), ())),
            preferred_element_type=jnp.float32,
        )
        self_score = scale * jnp.sum(query * new_keys[row : row + 1], axis=1, keepdims=True)
        visible = lax.broadcasted_iota(jnp.int32, scores.shape, 1) < scalars_ref[1 + row]
        masked = jnp.where(visible, scores, jnp.float32(-1e30))
        peak = jnp.maximum(jnp.max(masked, axis=1, keepdims=True), self_score)
        raised = jnp.where(visible, jnp.exp(masked - peak), jnp.float32(0.0))
        self_raised = jnp.exp(self_score - peak)
        denominator = jnp.sum(raised, axis=1, keepdims=True) + self_raised
        weights = (raised / denominator).astype(jnp.bfloat16)
        self_weight = (self_raised / denominator).astype(jnp.bfloat16).astype(jnp.float32)
        total = jnp.dot(weights, v_ref[row], preferred_element_type=jnp.float32)
        o_scr[row] = total + self_weight * new_values[row : row + 1]
    half = total_heads // 2
    for head in range(total_heads):
        ref = own_out if head < half else other_out
        column = (head % half) * DH
        ref[:, column : column + DH] = o_scr[:, head, :].astype(jnp.bfloat16)


def attend(core, lengths, own_q, other_q, parts, keys, values):
    rows, positions, _ = keys.shape
    heads = 2 * sum(part[0] for part in parts)
    out = jax.ShapeDtypeStruct((rows, heads * DH // 2), jnp.bfloat16)
    scalars = jnp.concatenate([core[None], lengths])
    return pl.pallas_call(
        functools.partial(attend_kernel, parts),
        out_shape=(out, out),
        in_specs=[SMEM] + [VMEM] * (2 * len(parts) + 2),
        out_specs=(VMEM, VMEM),
        scratch_shapes=[pltpu.VMEM((rows, heads, DH), jnp.float32)] * 2,
        compiler_params=pltpu.CompilerParams(vmem_limit_bytes=16 * MIB),
        cost_estimate=pl.CostEstimate(
            flops=4 * rows * heads * positions * DH,
            bytes_accessed=4 * rows * positions * DH,
            transcendentals=rows * heads * positions,
        ),
        name="attend",
    )(scalars, *own_q, *other_q, keys, values)


def output_kernel(order, rows, first, tile, with_prior, ids_ref, near_ref, far_ref, w_ref, *refs):
    if with_prior:
        send_in, keep_in, send_ref, keep_ref, xs_ref = refs
    else:
        send_ref, keep_ref, xs_ref = refs
    me, core = ids_ref[0], ids_ref[1]
    n = len(order)
    half = n // 2
    for p, j in enumerate(order):
        block = jnp.bitwise_xor(me, j)
        place = block % half + jnp.where(block // half == core, half, 0)
        source = near_ref if p < half else far_ref
        at = (p % half) * rows
        xs_ref[pl.ds(pl.multiple_of(place * rows, rows), rows), :] = source[at : at + rows, :]
    depth = xs_ref.shape[1]
    cut = half * rows
    for column in range(0, w_ref.shape[1], tile):
        span = slice(column, column + tile)
        total = jnp.dot(
            xs_ref[...], w_ref[first : first + depth, span], preferred_element_type=jnp.float32
        )
        if with_prior:
            send_ref[:, span] = send_in[:, span] + total[:cut]
            keep_ref[:, span] = keep_in[:, span] + total[cut:]
        else:
            send_ref[:, span] = total[:cut]
            keep_ref[:, span] = total[cut:]


def project_out(order, rows, ids, near, far, out_weight, first, prior):
    depth = near.shape[1]
    columns = out_weight.shape[1]
    n = len(order)
    tile = tile_of(columns, 768)
    out = jax.ShapeDtypeStruct((n * rows // 2, columns), jnp.float32)
    operands = [ids, near, far, out_weight] + ([] if prior is None else list(prior))
    return pl.pallas_call(
        functools.partial(output_kernel, order, rows, first, tile, prior is not None),
        out_shape=(out, out),
        in_specs=[SMEM] + [VMEM] * (len(operands) - 1),
        out_specs=(VMEM, VMEM),
        scratch_shapes=[pltpu.VMEM((n * rows, depth), jnp.bfloat16)],
        compiler_params=pltpu.CompilerParams(vmem_limit_bytes=16 * MIB),
        cost_estimate=pl.CostEstimate(
            flops=2 * n * rows * depth * columns,
            bytes_accessed=2 * depth * columns + 4 * n * rows * columns,
            transcendentals=0,
        ),
        name="project_out",
    )(*operands)


def local(tokens, query_weight, kv_weight, out_weight, key_cache, value_cache, lengths):
    n = lax.axis_size("gx")
    me = lax.axis_index("gx").astype(jnp.int32)
    core = lax.axis_index("gy").astype(jnp.int32)
    ids = jnp.stack([me, core])
    own_rows = key_cache.shape[0]
    rows = 2 * own_rows
    bits = [1 << i for i in range(n.bit_length() - 1)]

    def swap(array):
        return lax.ppermute(array, "gy", [(0, 1), (1, 0)])

    def across(array, mask):
        return lax.ppermute(array, "gx", [(g, g ^ mask) for g in range(n)])

    other_tokens = swap(tokens)
    width = query_weight.shape[1] // 2
    heads = width // DH

    orders = [bits, bits[1:] + bits[:1]]
    state = [
        project(orders[0], rows, ids, tokens, other_tokens, query_weight, kv_weight, 0, width),
        project(orders[1], rows, ids, tokens, other_tokens, query_weight, None, width, width),
    ]
    moving = [across(state[i][0], orders[i][0]) for i in range(2)]
    for step in range(len(bits)):
        for i in range(2):
            total = state[i][1] + moving[i]
            if step + 1 < len(bits):
                cut = total.shape[0] // 2
                state[i] = (total[cut:], total[:cut])
                moving[i] = across(state[i][0], orders[i][step + 1])
            else:
                state[i] = total
    mine, theirs = [], []
    for total in state:
        mine.append(lax.dynamic_slice_in_dim(total, core * own_rows, own_rows, 0).astype(jnp.bfloat16))
        give = lax.dynamic_slice_in_dim(total, (1 - core) * own_rows, own_rows, 0).astype(jnp.bfloat16)
        theirs.append(swap(give))

    own, other = attend(
        core, lengths, mine, theirs, ((heads, kv_weight.shape[1] // 2), (heads, 0)), key_cache, value_cache
    )
    got = swap(other)
    block = jnp.where(core == 0, jnp.concatenate([own, got]), jnp.concatenate([got, own]))

    near = [block[:, :width], block[:, width:]]
    far = [None, None]
    paths = [bits[::-1], bits[:1] + bits[:0:-1]]
    for step in range(len(bits)):
        for i in range(2):
            if step:
                near[i] = jnp.concatenate([near[i], far[i]])
            far[i] = across(near[i], paths[i][step])
    prior = None
    for i in range(2):
        prior = project_out(order_of(paths[i][::-1]), rows, ids, near[i], far[i], out_weight, i * width, prior)
    send, keep = prior
    return (keep + swap(send)).astype(jnp.bfloat16)


def solution(mesh):
    return jax.shard_map(
        local,
        mesh=mesh,
        in_specs=(
            P(("grp", "gy"), "gx"),
            P("gx", "gy"),
            P("gx", None),
            P("gy", "gx"),
            P(("grp", "gx", "gy"), None, None),
            P(("grp", "gx", "gy"), None, None),
            P(("grp", "gx", "gy")),
        ),
        out_specs=P(("grp", "gy"), "gx"),
        check_vma=False,
    )
```

```python
import functools

import jax
import jax.numpy as jnp
from jax import lax
from jax.experimental import pallas as pl
from jax.experimental.pallas import tpu as pltpu
from jax.sharding import PartitionSpec as P

H = 24
DH = 256
MIB = 1024 * 1024
TURNS = (0, 1, 2, 3, 2, 1, 0, 3, 2, 1, 0, 3)
VMEM = pl.BlockSpec(memory_space=pltpu.VMEM)
ANY = pl.BlockSpec(memory_space=pl.ANY)
HBM = pl.BlockSpec(memory_space=pltpu.HBM)
SMEM = pl.BlockSpec(memory_space=pltpu.SMEM)


def tile_of(width, wanted):
    while wanted >= 128:
        if width % wanted == 0:
            return wanted
        wanted -= 128
    return width


def order_of(bits):
    order = [0]
    for bit in reversed(bits):
        order = order + [j + bit for j in order]
    return order


def slabs_of(depth):
    return depth // 768 if depth % 768 == 0 else 1


def load_kernel(sources, pieces, *refs):
    count = len(sources)
    ids_ref, in_refs, out_refs, sems = refs[0], refs[1 : 1 + count], refs[-1 - count : -1], refs[-1]
    copies = []
    for at, (source, in_ref, out_ref) in enumerate(zip(sources, in_refs, out_refs)):
        step = out_ref.shape[0] // pieces
        for piece in range(pieces):
            span = pl.ds(piece * step, step)
            if source is None:
                view = in_ref.at[span]
            elif isinstance(source, tuple):
                view = in_ref.at[span, pl.ds(source[0], source[1])]
            else:
                view = in_ref.at[span, pl.ds(pl.multiple_of(ids_ref[1] * source, source), source)]
            copies.append(pltpu.make_async_copy(view, out_ref.at[span], sems.at[at, piece]))
    for copy in copies:
        copy.start()
    for copy in copies:
        copy.wait()


def load(ids, arrays, sources, pieces):
    shapes, total = [], 0
    for array, source in zip(arrays, sources):
        shape = array.shape
        if source is not None:
            shape = (shape[0], source[1] if isinstance(source, tuple) else source)
        shapes.append(jax.ShapeDtypeStruct(shape, array.dtype))
        total += 2 * array.size if source is None else 2 * shape[0] * shape[1]
    return pl.pallas_call(
        functools.partial(load_kernel, sources, pieces),
        out_shape=shapes,
        in_specs=[SMEM] + [HBM] * len(arrays),
        out_specs=[VMEM] * len(arrays),
        scratch_shapes=[pltpu.SemaphoreType.DMA((len(arrays), pieces))],
        compiler_params=pltpu.CompilerParams(vmem_limit_bytes=46 * MIB),
        cost_estimate=pl.CostEstimate(flops=0, bytes_accessed=total, transcendentals=0),
        name="load",
    )(ids, *arrays)


def project_kernel(order, rows, first, held, after, ids_ref, own_ref, other_ref, *refs):
    refs = refs[:1 + held] + refs[1 + held + after :]
    if held:
        w_ref, kv_ref, send_ref, keep_ref, xs_ref, row_sem = refs
    else:
        w_ref, send_ref, keep_ref, xs_ref, ws_ref, row_sem, w_sem = refs
    n = len(order)
    half = n // 2
    me, core = ids_ref[0], ids_ref[1]
    depth = xs_ref.shape[1]
    slabs = slabs_of(depth)
    slab = depth // slabs

    def row_copy(source_ref, p):
        block = jnp.bitwise_xor(me, order[p])
        source = pl.ds(pl.multiple_of((block % half) * rows, rows), rows)
        return pltpu.make_async_copy(
            source_ref.at[source, :], xs_ref.at[pl.ds(p * rows, rows), :], row_sem.at[p]
        )

    def weight_copy(k):
        span = pl.ds(k * slab, slab)
        width = ws_ref.shape[1]
        return pltpu.make_async_copy(w_ref.at[span, pl.ds(first, width)], ws_ref.at[span], w_sem.at[k])

    for p in range(n):
        mine = jnp.bitwise_xor(me, order[p]) // half == core

        @pl.when(mine)
        def _():
            row_copy(own_ref, p).start()

        @pl.when(jnp.logical_not(mine))
        def _():
            row_copy(other_ref, p).start()

    if not held:
        for k in range(slabs):
            weight_copy(k).start()
    for p in range(n):
        row_copy(own_ref, p).wait()

    cut = half * rows

    def put(total, at):
        keep_ref[:, at : at + total.shape[1]] = total[:cut]
        send_ref[:, at : at + total.shape[1]] = total[cut:]

    if held:
        kv_width = kv_ref.shape[1]
        put(jnp.dot(xs_ref[...], kv_ref[...], preferred_element_type=jnp.float32), 0)
        put(jnp.dot(xs_ref[...], w_ref[...], preferred_element_type=jnp.float32), kv_width)
    else:
        total = None
        for k in range(slabs):
            weight_copy(k).wait()
            span = slice(k * slab, (k + 1) * slab)
            part = jnp.dot(xs_ref[:, span], ws_ref[span, :], preferred_element_type=jnp.float32)
            total = part if total is None else total + part
        put(total, 0)


def project(bits, rows, ids, own, other, weights, first, width, after):
    features = own.shape[1]
    order = order_of(bits)
    n = len(order)
    slabs = slabs_of(features)
    held = len(weights) > 1
    columns = sum(w.shape[1] for w in weights) if held else width
    out = jax.ShapeDtypeStruct((n * rows // 2, columns), jnp.float32)
    scratch = [pltpu.VMEM((n * rows, features), own.dtype)]
    sems = [pltpu.SemaphoreType.DMA((n,))]
    if not held:
        scratch.append(pltpu.VMEM((features, width), own.dtype))
        sems.append(pltpu.SemaphoreType.DMA((slabs,)))
    return pl.pallas_call(
        functools.partial(project_kernel, order, rows, first, held, len(after)),
        out_shape=(out, out),
        in_specs=[SMEM, VMEM, VMEM] + [VMEM if held else HBM] * len(weights) + [ANY] * len(after),
        out_specs=(VMEM, VMEM),
        scratch_shapes=scratch + sems,
        compiler_params=pltpu.CompilerParams(vmem_limit_bytes=48 * MIB),
        cost_estimate=pl.CostEstimate(
            flops=2 * n * rows * columns,
            bytes_accessed=4 * n * rows,
            transcendentals=0,
        ),
        name="project",
    )(ids, own, other, *weights, *after)


def combine_kernel(last, ids_ref, keep_ref, got_ref, after_ref, send_ref, left_ref):
    total = keep_ref[...] + got_ref[...]
    cut = total.shape[0] // 2
    if last:
        mine = ids_ref[1] == 0
        send_ref[...] = jnp.where(mine, total[cut:], total[:cut]).astype(jnp.bfloat16)
        left_ref[...] = jnp.where(mine, total[:cut], total[cut:]).astype(jnp.bfloat16)
    else:
        send_ref[...] = total[cut:]
        left_ref[...] = total[:cut]


def combine(ids, keep, got, last, after):
    rows, columns = keep.shape
    out = jax.ShapeDtypeStruct((rows // 2, columns), jnp.bfloat16 if last else jnp.float32)
    return pl.pallas_call(
        functools.partial(combine_kernel, last),
        out_shape=(out, out),
        in_specs=[SMEM, VMEM, VMEM, ANY],
        out_specs=(VMEM, VMEM),
        compiler_params=pltpu.CompilerParams(vmem_limit_bytes=4 * MIB),
        cost_estimate=pl.CostEstimate(
            flops=rows * columns, bytes_accessed=12 * rows * columns, transcendentals=0
        ),
        name="combine",
    )(ids, keep, got, after)


def attend_kernel(parts, scalars_ref, *refs):
    own_q, other_q = refs[: len(parts)], refs[len(parts) : 2 * len(parts)]
    k_hbm, v_hbm, own_out, other_out, k_ref, v_ref, q_scr, o_scr, sems = refs[2 * len(parts) :]
    core = scalars_ref[0]
    rows, positions, _ = k_ref.shape
    copies = []
    for row in range(rows):
        copies.append(pltpu.make_async_copy(k_hbm.at[row], k_ref.at[row], sems.at[0, row]))
        copies.append(pltpu.make_async_copy(v_hbm.at[row], v_ref.at[row], sems.at[1, row]))
    for copy in copies:
        copy.start()
    at = 0
    for side in (own_q, other_q):
        for ref, (heads, skip) in zip(side, parts):
            for head in range(heads):
                column = skip + head * DH
                q_scr[:, at, :] = ref[:, column : column + DH].astype(jnp.float32)
                at += 1
    total_heads = at
    first = own_q[0][:, :DH].astype(jnp.float32)
    second = other_q[0][:, :DH].astype(jnp.float32)
    new_keys = jnp.where(core == 0, first, second)
    new_values = jnp.where(core == 0, second, first)
    scale = DH**-0.5
    for row in range(rows):
        query = q_scr[row]
        copies[2 * row].wait()
        scores = scale * lax.dot_general(
            query.astype(jnp.bfloat16),
            k_ref[row],
            (((1,), (1,)), ((), ())),
            preferred_element_type=jnp.float32,
        )
        self_score = scale * jnp.sum(query * new_keys[row : row + 1], axis=1, keepdims=True)
        visible = lax.broadcasted_iota(jnp.int32, scores.shape, 1) < scalars_ref[1 + row]
        masked = jnp.where(visible, scores, jnp.float32(-1e30))
        peak = jnp.maximum(jnp.max(masked, axis=1, keepdims=True), self_score)
        raised = jnp.where(visible, jnp.exp(masked - peak), jnp.float32(0.0))
        self_raised = jnp.exp(self_score - peak)
        denominator = jnp.sum(raised, axis=1, keepdims=True) + self_raised
        weights = (raised / denominator).astype(jnp.bfloat16)
        self_weight = (self_raised / denominator).astype(jnp.bfloat16).astype(jnp.float32)
        copies[2 * row + 1].wait()
        total = jnp.dot(weights, v_ref[row], preferred_element_type=jnp.float32)
        o_scr[row] = total + self_weight * new_values[row : row + 1]
    half = total_heads // 2
    for head in range(total_heads):
        ref = own_out if head < half else other_out
        column = (head % half) * DH
        ref[:, column : column + DH] = o_scr[:, head, :].astype(jnp.bfloat16)


def attend(core, lengths, own_q, other_q, parts, keys, values):
    rows, positions, _ = keys.shape
    heads = 2 * sum(part[0] for part in parts)
    out = jax.ShapeDtypeStruct((rows, heads * DH // 2), jnp.bfloat16)
    scalars = jnp.concatenate([core[None], lengths])
    return pl.pallas_call(
        functools.partial(attend_kernel, parts),
        out_shape=(out, out),
        in_specs=[SMEM] + [VMEM] * (2 * len(parts)) + [HBM, HBM],
        out_specs=(VMEM, VMEM),
        scratch_shapes=[pltpu.VMEM(keys.shape, keys.dtype)] * 2
        + [pltpu.VMEM((rows, heads, DH), jnp.float32)] * 2
        + [pltpu.SemaphoreType.DMA((2, rows))],
        compiler_params=pltpu.CompilerParams(vmem_limit_bytes=55 * MIB),
        cost_estimate=pl.CostEstimate(
            flops=4 * rows * heads * positions * DH,
            bytes_accessed=4 * rows * positions * DH,
            transcendentals=rows * heads * positions,
        ),
        name="attend",
    )(scalars, *own_q, *other_q, keys, values)


def spans_of(columns):
    if columns % 768:
        return [(0, columns)]
    spans = [(at, 768) for at in range(0, columns - 768, 768)]
    return spans + [(columns - 768, 512), (columns - 256, 256)]


def output_kernel(order, rows, first, spans, with_prior, ids_ref, near_ref, far_ref, w_hbm, *refs):
    if with_prior:
        send_in, keep_in, send_ref, keep_ref, xs_ref, w_ref, sems, row_sems, prior_ref, prior_sems = refs
    else:
        send_ref, keep_ref, xs_ref, w_ref, sems, row_sems = refs
    depth = xs_ref.shape[1]
    me, core = ids_ref[0], ids_ref[1]
    n = len(order)
    half = n // 2
    row_copies = []
    for p, j in enumerate(order):
        block = jnp.bitwise_xor(me, j)
        place = block % half + jnp.where(block // half == core, half, 0)
        source = near_ref if p < half else far_ref
        row_copies.append(
            pltpu.make_async_copy(
                source.at[pl.ds((p % half) * rows, rows), :],
                xs_ref.at[pl.ds(pl.multiple_of(place * rows, rows), rows), :],
                row_sems.at[p],
            )
        )
    for copy in row_copies:
        copy.start()
    copies = []
    for at, (column, width) in enumerate(spans):
        span = pl.ds(column, width)
        copies.append(
            pltpu.make_async_copy(w_hbm.at[pl.ds(first, depth), span], w_ref.at[:, span], sems.at[at])
        )
    for copy in copies:
        copy.start()
    if with_prior:
        prior_copies = [
            pltpu.make_async_copy(ref, prior_ref.at[at], prior_sems.at[at])
            for at, ref in enumerate((send_in, keep_in))
        ]
        for copy in prior_copies:
            copy.start()
    for copy in row_copies:
        copy.wait()
    if with_prior:
        for copy in prior_copies:
            copy.wait()
    cut = half * rows
    for copy, (column, width) in zip(copies, spans):
        copy.wait()
        span = slice(column, column + width)
        total = jnp.dot(xs_ref[...], w_ref[:, span], preferred_element_type=jnp.float32)
        if with_prior:
            send_ref[:, span] = prior_ref[0, :, span] + total[:cut]
            keep_ref[:, span] = prior_ref[1, :, span] + total[cut:]
        else:
            send_ref[:, span] = total[:cut]
            keep_ref[:, span] = total[cut:]


def project_out(order, rows, ids, near, far, out_weight, first, prior):
    depth = near.shape[1]
    columns = out_weight.shape[1]
    n = len(order)
    spans = spans_of(columns)
    out = jax.ShapeDtypeStruct((n * rows // 2, columns), jnp.float32)
    operands = [ids, near, far, out_weight] + ([] if prior is None else list(prior))
    return pl.pallas_call(
        functools.partial(output_kernel, order, rows, first, spans, prior is not None),
        out_shape=(out, out),
        in_specs=[SMEM, ANY, ANY, HBM] + [ANY] * (len(operands) - 4),
        out_specs=(VMEM, VMEM),
        scratch_shapes=[
            pltpu.VMEM((n * rows, depth), jnp.bfloat16),
            pltpu.VMEM((depth, columns), jnp.bfloat16),
            pltpu.SemaphoreType.DMA((len(spans),)),
            pltpu.SemaphoreType.DMA((n,)),
        ]
        + (
            []
            if prior is None
            else [pltpu.VMEM((2, *out.shape), jnp.float32), pltpu.SemaphoreType.DMA((2,))]
        ),
        compiler_params=pltpu.CompilerParams(vmem_limit_bytes=52 * MIB),
        cost_estimate=pl.CostEstimate(
            flops=2 * n * rows * depth * columns,
            bytes_accessed=2 * depth * columns + 4 * n * rows * columns,
            transcendentals=0,
        ),
        name="project_out",
    )(*operands)


def local(tokens, query_weight, kv_weight, out_weight, key_cache, value_cache, lengths):
    n = lax.axis_size("gx")
    me = lax.axis_index("gx").astype(jnp.int32)
    core = lax.axis_index("gy").astype(jnp.int32)
    ids = jnp.stack([me, core])
    own_rows = key_cache.shape[0]
    rows = 2 * own_rows
    bits = [1 << i for i in range(n.bit_length() - 1)]

    def swap(array):
        return lax.ppermute(array, "gy", [(0, 1), (1, 0)])

    def across(array, mask):
        return lax.ppermute(array, "gx", [(g, g ^ mask) for g in range(n)])

    width = query_weight.shape[1] // 2
    kv_width = kv_weight.shape[1] // 2

    y, z = bits[:1], bits[1:]
    unit = query_weight.shape[1] // 12
    plan = [(4 * unit, z + y), (4 * unit, y + z), (2 * unit, z[:1] + y + z[1:]), (2 * unit, y + z)]
    *held, own_tokens = load(ids, [query_weight, kv_weight, tokens], [(0, plan[0][0]), kv_width, None], 4)
    other_tokens = swap(tokens)
    state, moving, first, after = [], [], 0, []
    for i, (columns, order) in enumerate(plan):
        weights = held if i == 0 else [query_weight]
        send, keep = project(order, rows, ids, own_tokens, other_tokens, weights, first, columns, after)
        after = [send]
        state.append((send, keep))
        moving.append(across(send, order[0]))
        first += columns
    mine, theirs = [None] * len(plan), [None] * len(plan)
    turns = [i for _ in bits for i in range(len(plan))]
    if len(bits) == 3:
        turns = TURNS
    steps = [0] * len(plan)
    after = after[0]
    for i in turns:
        steps[i] += 1
        last = steps[i] == len(bits)
        send, keep = combine(ids, state[i][1], moving[i], last, after)
        after = keep
        if last:
            mine[i], theirs[i] = keep, swap(send)
        else:
            state[i] = (send, keep)
            moving[i] = across(send, plan[i][1][steps[i]])

    parts = tuple((columns // DH, 0 if i else kv_width) for i, (columns, _) in enumerate(plan))
    own, other = attend(core, lengths, mine, theirs, parts, key_cache, value_cache)
    got = swap(other)
    block = jnp.where(core == 0, jnp.concatenate([own, got]), jnp.concatenate([got, own]))

    near = [block[:, :width], block[:, width:]]
    far = [None, None]
    paths = [bits[::-1], bits[:1] + bits[:0:-1]]
    for step in range(len(bits)):
        for i in range(2):
            if step:
                near[i] = jnp.concatenate([near[i], far[i]])
            far[i] = across(near[i], paths[i][step])
    prior = None
    for i in range(2):
        prior = project_out(order_of(paths[i][::-1]), rows, ids, near[i], far[i], out_weight, i * width, prior)
    send, keep = prior
    return (keep + swap(send)).astype(jnp.bfloat16)


def solution(mesh):
    return jax.shard_map(
        local,
        mesh=mesh,
        in_specs=(
            P(("grp", "gy"), "gx"),
            P("gx", "gy"),
            P("gx", None),
            P("gy", "gx"),
            P(("grp", "gx", "gy"), None, None),
            P(("grp", "gx", "gy"), None, None),
            P(("grp", "gx", "gy")),
        ),
        out_specs=P(("grp", "gy"), "gx"),
        check_vma=False,
    )
```

```python
import functools

import jax
import jax.numpy as jnp
from jax import lax
from jax.experimental import pallas as pl
from jax.experimental.pallas import tpu as pltpu
from jax.sharding import PartitionSpec as P

H = 24
DH = 256
MIB = 1024 * 1024
HBM = pl.BlockSpec(memory_space=pltpu.HBM)
ANY = pl.BlockSpec(memory_space=pl.ANY)
VMEM = pl.BlockSpec(memory_space=pltpu.VMEM)
SMEM = pl.BlockSpec(memory_space=pltpu.SMEM)


def slabs_of(depth):
    return depth // 256 if depth % 256 == 0 else 1


class InOrder:
    def __init__(self, copies, ahead):
        self.copies, self.ahead = copies, ahead
        for copy in copies[:ahead]:
            copy.start()

    def wait(self, at):
        self.copies[at].wait()
        if at + self.ahead < len(self.copies):
            self.copies[at + self.ahead].start()


def order_of(bits):
    order = [0]
    for bit in reversed(bits):
        order = order + [j + bit for j in order]
    return order


def project_kernel(order, rows, first, kv_width, after, ids_ref, own_ref, other_ref, w_ref, *refs):
    refs = list(refs)
    kv_ref = refs.pop(0) if kv_width else None
    send_ref, keep_ref, xs_ref, ws_ref, row_sem, w_sem = refs[after:]
    n = len(order)
    slabs, slab, columns = ws_ref.shape
    me, core = ids_ref[0], ids_ref[1]
    half = n // 2

    def row_copy(source_ref, p):
        block = jnp.bitwise_xor(me, order[p])
        source = pl.ds(pl.multiple_of((block % half) * rows, rows), rows)
        return pltpu.make_async_copy(
            source_ref.at[source, :], xs_ref.at[pl.ds(p * rows, rows), :], row_sem.at[p]
        )

    for p in range(n):
        mine = jnp.bitwise_xor(me, order[p]) // half == core

        @pl.when(mine)
        def _():
            row_copy(own_ref, p).start()

        @pl.when(jnp.logical_not(mine))
        def _():
            row_copy(other_ref, p).start()

    copies = []
    per_slab = 1
    for k in range(slabs):
        span = pl.ds(k * slab, slab)
        if kv_width:
            per_slab = 2
            own = pl.ds(pl.multiple_of(core * kv_width, kv_width), kv_width)
            target = ws_ref.at[k, :, pl.ds(0, kv_width)]
            copies.append(pltpu.make_async_copy(kv_ref.at[span, own], target, w_sem.at[1, k]))
        width = columns - kv_width
        target = ws_ref.at[k, :, pl.ds(kv_width, width)]
        copies.append(pltpu.make_async_copy(w_ref.at[span, pl.ds(first, width)], target, w_sem.at[0, k]))
    weights = InOrder(copies, 3 * per_slab)
    for p in range(n):
        row_copy(own_ref, p).wait()
    cut = n * rows // 2
    for k in range(slabs):
        for at in range(per_slab):
            weights.wait(k * per_slab + at)
        part = jnp.dot(
            xs_ref[:, k * slab : (k + 1) * slab], ws_ref[k], preferred_element_type=jnp.float32
        )
        if k == 0:
            keep_ref[...] = part[:cut]
            send_ref[...] = part[cut:]
        else:
            keep_ref[...] += part[:cut]
            send_ref[...] += part[cut:]


def project(bits, rows, ids, tokens, other, query_weight, kv_weight, first, width, after):
    features = tokens.shape[1]
    order = order_of(bits)
    n = len(order)
    slabs = slabs_of(features)
    kv_width = kv_weight.shape[1] // 2 if kv_weight is not None else 0
    columns = width + kv_width
    out = jax.ShapeDtypeStruct((n * rows // 2, columns), jnp.float32)
    weights = [query_weight] + ([kv_weight] if kv_width else [])
    return pl.pallas_call(
        functools.partial(project_kernel, order, rows, first, kv_width, len(after)),
        out_shape=(out, out),
        in_specs=[SMEM, ANY, ANY] + [HBM] * len(weights) + [ANY] * len(after),
        out_specs=(VMEM, VMEM),
        scratch_shapes=[
            pltpu.VMEM((n * rows, features), tokens.dtype),
            pltpu.VMEM((slabs, features // slabs, columns), tokens.dtype),
            pltpu.SemaphoreType.DMA((n,)),
            pltpu.SemaphoreType.DMA((2, slabs)),
        ],
        compiler_params=pltpu.CompilerParams(vmem_limit_bytes=46 * MIB),
        cost_estimate=pl.CostEstimate(
            flops=2 * n * rows * features * columns,
            bytes_accessed=2 * features * columns + 4 * n * rows * columns,
            transcendentals=0,
        ),
        name="project",
    )(ids, tokens, other, *weights, *after)


def attend_kernel(parts, scalars_ref, *refs):
    own_q, other_q = refs[: len(parts)], refs[len(parts) : 2 * len(parts)]
    k_hbm, v_hbm, own_out, other_out, k_ref, v_ref, q_scr, o_scr, sems = refs[2 * len(parts) :]
    core = scalars_ref[0]
    rows, positions, _ = k_ref.shape
    copies = []
    for row in range(rows):
        copies.append(pltpu.make_async_copy(k_hbm.at[row], k_ref.at[row], sems.at[0, row]))
        copies.append(pltpu.make_async_copy(v_hbm.at[row], v_ref.at[row], sems.at[1, row]))
    caches = InOrder(copies, 4)
    at = 0
    for side in (own_q, other_q):
        for ref, (heads, skip) in zip(side, parts):
            for head in range(heads):
                column = skip + head * DH
                q_scr[:, at, :] = ref[:, column : column + DH].astype(jnp.float32)
                at += 1
    total_heads = at
    first = own_q[0][:, :DH].astype(jnp.float32)
    second = other_q[0][:, :DH].astype(jnp.float32)
    new_keys = jnp.where(core == 0, first, second)
    new_values = jnp.where(core == 0, second, first)
    scale = DH**-0.5
    for row in range(rows):
        query = q_scr[row]
        caches.wait(2 * row)
        scores = scale * lax.dot_general(
            query.astype(jnp.bfloat16),
            k_ref[row],
            (((1,), (1,)), ((), ())),
            preferred_element_type=jnp.float32,
        )
        self_score = scale * jnp.sum(query * new_keys[row : row + 1], axis=1, keepdims=True)
        visible = lax.broadcasted_iota(jnp.int32, scores.shape, 1) < scalars_ref[1 + row]
        masked = jnp.where(visible, scores, jnp.float32(-1e30))
        peak = jnp.maximum(jnp.max(masked, axis=1, keepdims=True), self_score)
        raised = jnp.where(visible, jnp.exp(masked - peak), jnp.float32(0.0))
        self_raised = jnp.exp(self_score - peak)
        denominator = jnp.sum(raised, axis=1, keepdims=True) + self_raised
        weights = (raised / denominator).astype(jnp.bfloat16)
        self_weight = (self_raised / denominator).astype(jnp.bfloat16).astype(jnp.float32)
        caches.wait(2 * row + 1)
        total = jnp.dot(weights, v_ref[row], preferred_element_type=jnp.float32)
        o_scr[row] = total + self_weight * new_values[row : row + 1]
    half = total_heads // 2
    for head in range(total_heads):
        ref = own_out if head < half else other_out
        column = (head % half) * DH
        ref[:, column : column + DH] = o_scr[:, head, :].astype(jnp.bfloat16)


def attend(core, lengths, own_q, other_q, parts, keys, values):
    rows, positions, _ = keys.shape
    heads = 2 * sum(part[0] for part in parts)
    out = jax.ShapeDtypeStruct((rows, heads * DH // 2), jnp.bfloat16)
    scalars = jnp.concatenate([core[None], lengths])
    return pl.pallas_call(
        functools.partial(attend_kernel, parts),
        out_shape=(out, out),
        in_specs=[SMEM] + [VMEM] * (2 * len(parts)) + [HBM, HBM],
        out_specs=(VMEM, VMEM),
        scratch_shapes=[pltpu.VMEM(keys.shape, keys.dtype)] * 2
        + [pltpu.VMEM((rows, heads, DH), jnp.float32)] * 2
        + [pltpu.SemaphoreType.DMA((2, rows))],
        compiler_params=pltpu.CompilerParams(vmem_limit_bytes=52 * MIB),
        cost_estimate=pl.CostEstimate(
            flops=4 * rows * heads * positions * DH,
            bytes_accessed=4 * rows * positions * DH,
            transcendentals=rows * heads * positions,
        ),
        name="attend",
    )(scalars, *own_q, *other_q, keys, values)


def output_kernel(order, rows, first, with_prior, ids_ref, near_ref, far_ref, w_hbm, *refs):
    if with_prior:
        send_in, keep_in, send_ref, keep_ref, xs_ref, ws_ref, row_sem, w_sem = refs
    else:
        send_ref, keep_ref, xs_ref, ws_ref, row_sem, w_sem = refs
    me, core = ids_ref[0], ids_ref[1]
    n = len(order)
    half = n // 2
    slabs, slab, _ = ws_ref.shape
    row_copies = []
    for p, j in enumerate(order):
        block = jnp.bitwise_xor(me, j)
        place = block % half + jnp.where(block // half == core, half, 0)
        source = near_ref if p < half else far_ref
        row_copies.append(
            pltpu.make_async_copy(
                source.at[pl.ds((p % half) * rows, rows), :],
                xs_ref.at[pl.ds(pl.multiple_of(place * rows, rows), rows), :],
                row_sem.at[p],
            )
        )
    for copy in row_copies:
        copy.start()
    weights = InOrder(
        [
            pltpu.make_async_copy(w_hbm.at[pl.ds(first + k * slab, slab)], ws_ref.at[k], w_sem.at[k])
            for k in range(slabs)
        ],
        2,
    )
    for copy in row_copies:
        copy.wait()
    cut = half * rows
    for k in range(slabs):
        weights.wait(k)
        part = jnp.dot(
            xs_ref[:, k * slab : (k + 1) * slab], ws_ref[k], preferred_element_type=jnp.float32
        )
        if k:
            send_ref[...] += part[:cut]
            keep_ref[...] += part[cut:]
        elif with_prior:
            send_ref[...] = send_in[...] + part[:cut]
            keep_ref[...] = keep_in[...] + part[cut:]
        else:
            send_ref[...] = part[:cut]
            keep_ref[...] = part[cut:]


def project_out(order, rows, ids, near, far, out_weight, first, prior):
    depth = near.shape[1]
    columns = out_weight.shape[1]
    n = len(order)
    slabs = slabs_of(depth)
    out = jax.ShapeDtypeStruct((n * rows // 2, columns), jnp.float32)
    operands = [ids, near, far, out_weight] + ([] if prior is None else list(prior))
    return pl.pallas_call(
        functools.partial(output_kernel, order, rows, first, prior is not None),
        out_shape=(out, out),
        in_specs=[SMEM, ANY, ANY, HBM] + [VMEM] * (len(operands) - 4),
        out_specs=(VMEM, VMEM),
        scratch_shapes=[
            pltpu.VMEM((n * rows, depth), jnp.bfloat16),
            pltpu.VMEM((slabs, depth // slabs, columns), jnp.bfloat16),
            pltpu.SemaphoreType.DMA((n,)),
            pltpu.SemaphoreType.DMA((slabs,)),
        ],
        compiler_params=pltpu.CompilerParams(vmem_limit_bytes=46 * MIB),
        cost_estimate=pl.CostEstimate(
            flops=2 * n * rows * depth * columns,
            bytes_accessed=2 * depth * columns + 4 * n * rows * columns,
            transcendentals=0,
        ),
        name="project_out",
    )(*operands)


def local(tokens, query_weight, kv_weight, out_weight, key_cache, value_cache, lengths):
    n = lax.axis_size("gx")
    me = lax.axis_index("gx").astype(jnp.int32)
    core = lax.axis_index("gy").astype(jnp.int32)
    ids = jnp.stack([me, core])
    own_rows = key_cache.shape[0]
    rows = 2 * own_rows
    bits = [1 << i for i in range(n.bit_length() - 1)]

    def swap(array):
        return lax.ppermute(array, "gy", [(0, 1), (1, 0)])

    def across(array, mask):
        return lax.ppermute(array, "gx", [(g, g ^ mask) for g in range(n)])

    other_tokens = swap(tokens)
    own_tokens = jnp.where(me < n, tokens, jnp.bfloat16(0))
    width = query_weight.shape[1] // 2

    y, z = bits[:1], bits[1:]
    unit = query_weight.shape[1] // 12
    plan = [(3 * unit, y + z), (5 * unit, y + z), (4 * unit, z + y)]
    state, moving, first, after = [], [], 0, []
    for i, (columns, order) in enumerate(plan):
        send, keep = project(
            order, rows, ids, own_tokens, other_tokens, query_weight, None if i else kv_weight, first, columns, after
        )
        state.append((send, keep))
        moving.append(across(send, order[0]))
        first += columns
        after = []
    for step in range(len(bits)):
        for i, (columns, order) in enumerate(plan):
            total = state[i][1] + moving[i]
            if step + 1 < len(bits):
                cut = total.shape[0] // 2
                state[i] = (total[cut:], total[:cut])
                moving[i] = across(state[i][0], order[step + 1])
            else:
                state[i] = total
    mine, theirs = [], []
    for total in state:
        mine.append(lax.dynamic_slice_in_dim(total, core * own_rows, own_rows, 0).astype(jnp.bfloat16))
        give = lax.dynamic_slice_in_dim(total, (1 - core) * own_rows, own_rows, 0).astype(jnp.bfloat16)
        theirs.append(swap(give))

    kv_width = kv_weight.shape[1] // 2
    parts = tuple((columns // DH, 0 if i else kv_width) for i, (columns, _) in enumerate(plan))
    own, other = attend(core, lengths, mine, theirs, parts, key_cache, value_cache)
    got = swap(other)
    block = jnp.where(core == 0, jnp.concatenate([own, got]), jnp.concatenate([got, own]))

    near = [block[:, :width], block[:, width:]]
    far = [None, None]
    paths = [bits[::-1], bits[:1] + bits[:0:-1]]
    for step in range(len(bits)):
        for i in range(2):
            if step:
                near[i] = jnp.concatenate([near[i], far[i]])
            far[i] = across(near[i], paths[i][step])
    prior = None
    for i in range(2):
        prior = project_out(order_of(paths[i][::-1]), rows, ids, near[i], far[i], out_weight, i * width, prior)
    send, keep = prior
    return (keep + swap(send)).astype(jnp.bfloat16)


def solution(mesh):
    return jax.shard_map(
        local,
        mesh=mesh,
        in_specs=(
            P(("grp", "gy"), "gx"),
            P("gx", "gy"),
            P("gx", None),
            P("gy", "gx"),
            P(("grp", "gx", "gy"), None, None),
            P(("grp", "gx", "gy"), None, None),
            P(("grp", "gx", "gy")),
        ),
        out_specs=P(("grp", "gy"), "gx"),
        check_vma=False,
    )
```

```python
import functools

import jax
import jax.numpy as jnp
from jax import lax
from jax.experimental import pallas as pl
from jax.experimental.pallas import tpu as pltpu
from jax.sharding import PartitionSpec as P

H = 24
DH = 256
MIB = 1024 * 1024
HBM = pl.BlockSpec(memory_space=pltpu.HBM)
ANY = pl.BlockSpec(memory_space=pl.ANY)
VMEM = pl.BlockSpec(memory_space=pltpu.VMEM)
SMEM = pl.BlockSpec(memory_space=pltpu.SMEM)


class InOrder:
    def __init__(self, copies, ahead):
        self.copies, self.ahead = copies, ahead
        for copy in copies[:ahead]:
            copy.start()

    def wait(self, at):
        self.copies[at].wait()
        if at + self.ahead < len(self.copies):
            self.copies[at + self.ahead].start()


def order_of(bits):
    order = [0]
    for bit in reversed(bits):
        order = order + [j + bit for j in order]
    return order


def spans_of(width):
    return [(at, min(512, width - at)) for at in range(0, width, 512)]


def project_kernel(orders, rows, first, widths, kv_width, ids_ref, own_ref, other_ref, w_ref, *refs):
    refs = list(refs)
    kv_ref = refs.pop(0) if kv_width else None
    outs, (xs_ref, ws_ref, row_sem, w_sem) = refs[:-4], refs[-4:]
    n = len(orders[0])
    half = n // 2
    me, core = ids_ref[0], ids_ref[1]
    features = xs_ref.shape[2]

    def row_copy(source_ref, chunk, p):
        block = jnp.bitwise_xor(me, orders[chunk][p])
        source = pl.ds(pl.multiple_of((block % half) * rows, rows), rows)
        return pltpu.make_async_copy(
            source_ref.at[source, :],
            xs_ref.at[chunk, pl.ds(p * rows, rows), :],
            row_sem.at[chunk, p],
        )

    for chunk, order in enumerate(orders):
        for p in range(n):
            mine = jnp.bitwise_xor(me, order[p]) // half == core

            @pl.when(mine)
            def _():
                row_copy(own_ref, chunk, p).start()

            @pl.when(jnp.logical_not(mine))
            def _():
                row_copy(other_ref, chunk, p).start()

    tiles, copies, at, source = [], [], 0, first
    depth = features // 2 if features % 32 == 0 else features

    def fetch(from_ref, column, width):
        for part in range(features // depth):
            span = pl.ds(part * depth, depth)
            copies.append(
                pltpu.make_async_copy(
                    from_ref.at[span, pl.ds(column, width)],
                    ws_ref.at[span, pl.ds(at, width)],
                    w_sem.at[len(copies)],
                )
            )

    for chunk, width in enumerate(widths):
        column = 0
        if kv_width and chunk == 0:
            fetch(kv_ref, pl.multiple_of(core * kv_width, kv_width), kv_width)
            tiles.append((chunk, 0, at, kv_width))
            at += kv_width
            column = kv_width
        for offset, tile in spans_of(width):
            fetch(w_ref, source, tile)
            tiles.append((chunk, column + offset, at, tile))
            at += tile
            source += tile
    per_tile = features // depth
    weights = InOrder(copies, 3 * per_tile)
    cut = half * rows
    ready = set()
    for t, (chunk, column, at, width) in enumerate(tiles):
        if chunk not in ready:
            ready.add(chunk)
            for p in range(n):
                row_copy(own_ref, chunk, p).wait()
        for part in range(per_tile):
            weights.wait(t * per_tile + part)
        total = jnp.dot(
            xs_ref[chunk], ws_ref[:, at : at + width], preferred_element_type=jnp.float32
        )
        span = slice(column, column + width)
        outs[2 * chunk][:, span] = total[cut:]
        outs[2 * chunk + 1][:, span] = total[:cut]


def project(plan, rows, ids, tokens, other, query_weight, kv_weight, first):
    features = tokens.shape[1]
    orders = [order_of(bits) for _, bits in plan]
    widths = [width for width, _ in plan]
    n = len(orders[0])
    kv_width = kv_weight.shape[1] // 2 if kv_weight is not None else 0
    columns = sum(widths) + kv_width
    outs = []
    for chunk, width in enumerate(widths):
        shape = (n * rows // 2, width + (0 if chunk else kv_width))
        outs += [jax.ShapeDtypeStruct(shape, jnp.float32)] * 2
    weights = [query_weight] + ([kv_weight] if kv_width else [])
    copies = 2 * (len(weights) - 1 + sum(len(spans_of(width)) for width in widths))
    outs = pl.pallas_call(
        functools.partial(project_kernel, orders, rows, first, widths, kv_width),
        out_shape=outs,
        in_specs=[SMEM, ANY, ANY] + [HBM] * len(weights),
        out_specs=[VMEM] * len(outs),
        scratch_shapes=[
            pltpu.VMEM((len(orders), n * rows, features), tokens.dtype),
            pltpu.VMEM((features, columns), tokens.dtype),
            pltpu.SemaphoreType.DMA((len(orders), n)),
            pltpu.SemaphoreType.DMA((copies,)),
        ],
        compiler_params=pltpu.CompilerParams(vmem_limit_bytes=46 * MIB),
        cost_estimate=pl.CostEstimate(
            flops=2 * n * rows * features * columns,
            bytes_accessed=2 * features * columns + 4 * n * rows * columns,
            transcendentals=0,
        ),
        name="project",
    )(ids, tokens, other, *weights)
    return list(zip(outs[::2], outs[1::2]))


def attend_kernel(parts, scalars_ref, *refs):
    own_q, other_q = refs[: len(parts)], refs[len(parts) : 2 * len(parts)]
    k_hbm, v_hbm, own_out, other_out, k_ref, v_ref, q_scr, o_scr, sems = refs[2 * len(parts) :]
    core = scalars_ref[0]
    rows, positions, _ = k_ref.shape
    copies = []
    for row in range(rows):
        copies.append(pltpu.make_async_copy(k_hbm.at[row], k_ref.at[row], sems.at[0, row]))
        copies.append(pltpu.make_async_copy(v_hbm.at[row], v_ref.at[row], sems.at[1, row]))
    caches = InOrder(copies, 8)
    at = 0
    for side in (own_q, other_q):
        for ref, (heads, skip) in zip(side, parts):
            for head in range(heads):
                column = skip + head * DH
                q_scr[:, at, :] = ref[:, column : column + DH].astype(jnp.float32)
                at += 1
    total_heads = at
    first = own_q[0][:, :DH].astype(jnp.float32)
    second = other_q[0][:, :DH].astype(jnp.float32)
    new_keys = jnp.where(core == 0, first, second)
    new_values = jnp.where(core == 0, second, first)
    scale = DH**-0.5
    for row in range(rows):
        query = q_scr[row]
        caches.wait(2 * row)
        scores = scale * lax.dot_general(
            query.astype(jnp.bfloat16),
            k_ref[row],
            (((1,), (1,)), ((), ())),
            preferred_element_type=jnp.float32,
        )
        self_score = scale * jnp.sum(query * new_keys[row : row + 1], axis=1, keepdims=True)
        visible = lax.broadcasted_iota(jnp.int32, scores.shape, 1) < scalars_ref[1 + row]
        masked = jnp.where(visible, scores, jnp.float32(-1e30))
        peak = jnp.maximum(jnp.max(masked, axis=1, keepdims=True), self_score)
        raised = jnp.where(visible, jnp.exp(masked - peak), jnp.float32(0.0))
        self_raised = jnp.exp(self_score - peak)
        denominator = jnp.sum(raised, axis=1, keepdims=True) + self_raised
        weights = (raised / denominator).astype(jnp.bfloat16)
        self_weight = (self_raised / denominator).astype(jnp.bfloat16).astype(jnp.float32)
        caches.wait(2 * row + 1)
        total = jnp.dot(weights, v_ref[row], preferred_element_type=jnp.float32)
        o_scr[row] = total + self_weight * new_values[row : row + 1]
    half = total_heads // 2
    for head in range(total_heads):
        ref = own_out if head < half else other_out
        column = (head % half) * DH
        ref[:, column : column + DH] = o_scr[:, head, :].astype(jnp.bfloat16)


def attend(core, lengths, own_q, other_q, parts, keys, values):
    rows, positions, _ = keys.shape
    heads = 2 * sum(part[0] for part in parts)
    out = jax.ShapeDtypeStruct((rows, heads * DH // 2), jnp.bfloat16)
    scalars = jnp.concatenate([core[None], lengths])
    return pl.pallas_call(
        functools.partial(attend_kernel, parts),
        out_shape=(out, out),
        in_specs=[SMEM] + [VMEM] * (2 * len(parts)) + [HBM, HBM],
        out_specs=(VMEM, VMEM),
        scratch_shapes=[pltpu.VMEM(keys.shape, keys.dtype)] * 2
        + [pltpu.VMEM((rows, heads, DH), jnp.float32)] * 2
        + [pltpu.SemaphoreType.DMA((2, rows))],
        compiler_params=pltpu.CompilerParams(vmem_limit_bytes=52 * MIB),
        cost_estimate=pl.CostEstimate(
            flops=4 * rows * heads * positions * DH,
            bytes_accessed=4 * rows * positions * DH,
            transcendentals=rows * heads * positions,
        ),
        name="attend",
    )(scalars, *own_q, *other_q, keys, values)


def output_kernel(order, rows, first, spans, ids_ref, *refs):
    count = len(refs) - 7
    block_refs = refs[:count]
    w_hbm, send_ref, keep_ref, xs_ref, ws_ref, row_sem, w_sem = refs[count:]
    depth = block_refs[0].shape[1]
    copies = [
        pltpu.make_async_copy(
            w_hbm.at[:, pl.ds(first + at, width)], ws_ref.at[:, pl.ds(at, width)], w_sem.at[k]
        )
        for k, (at, width) in enumerate(spans)
    ]
    me, core = ids_ref[0], ids_ref[1]
    n = len(order[0])
    half = n // 2
    row_copies = []
    for group, (near_ref, far_ref) in enumerate(zip(block_refs[::2], block_refs[1::2])):
        for p, j in enumerate(order[group]):
            block = jnp.bitwise_xor(me, j)
            place = block % half + jnp.where(block // half == core, half, 0)
            source = near_ref if p < half else far_ref
            row_copies.append(
                pltpu.make_async_copy(
                    source.at[pl.ds((p % half) * rows, rows), :],
                    xs_ref.at[
                        pl.ds(pl.multiple_of(place * rows, rows), rows), pl.ds(group * depth, depth)
                    ],
                    row_sem.at[group, p],
                )
            )
    for copy in row_copies:
        copy.start()
    weights = InOrder(copies, 2)
    for copy in row_copies:
        copy.wait()
    cut = half * rows
    for k, (at, width) in enumerate(spans):
        weights.wait(k)
        span = slice(at, at + width)
        total = jnp.dot(xs_ref[...], ws_ref[:, span], preferred_element_type=jnp.float32)
        send_ref[:, span] = total[:cut]
        keep_ref[:, span] = total[cut:]


def project_out(orders, rows, ids, blocks, out_weight, first, columns):
    depth = out_weight.shape[0]
    n = len(orders[0])
    tile = 384 if columns % 384 == 0 else columns
    spans = [(at, tile) for at in range(0, columns, tile)]
    out = jax.ShapeDtypeStruct((n * rows // 2, columns), jnp.float32)
    return pl.pallas_call(
        functools.partial(output_kernel, orders, rows, first, spans),
        out_shape=(out, out),
        in_specs=[SMEM] + [ANY] * len(blocks) + [HBM],
        out_specs=(VMEM, VMEM),
        scratch_shapes=[
            pltpu.VMEM((n * rows, depth), jnp.bfloat16),
            pltpu.VMEM((depth, columns), jnp.bfloat16),
            pltpu.SemaphoreType.DMA((len(orders), n)),
            pltpu.SemaphoreType.DMA((len(spans),)),
        ],
        compiler_params=pltpu.CompilerParams(vmem_limit_bytes=46 * MIB),
        cost_estimate=pl.CostEstimate(
            flops=2 * n * rows * depth * columns,
            bytes_accessed=2 * depth * columns + 4 * n * rows * columns,
            transcendentals=0,
        ),
        name="project_out",
    )(ids, *blocks, out_weight)


def local(tokens, query_weight, kv_weight, out_weight, key_cache, value_cache, lengths):
    n = lax.axis_size("gx")
    me = lax.axis_index("gx").astype(jnp.int32)
    core = lax.axis_index("gy").astype(jnp.int32)
    ids = jnp.stack([me, core])
    own_rows = key_cache.shape[0]
    rows = 2 * own_rows
    bits = [1 << i for i in range(n.bit_length() - 1)]

    def swap(array):
        return lax.ppermute(array, "gy", [(0, 1), (1, 0)])

    def across(array, mask):
        return lax.ppermute(array, "gx", [(g, g ^ mask) for g in range(n)])

    other_tokens = swap(tokens)
    own_tokens = jnp.where(me < n, tokens, jnp.bfloat16(0))
    width = query_weight.shape[1] // 2

    y, z = bits[:1], bits[1:]
    unit = query_weight.shape[1] // 12
    plan = [(3 * unit, y + z[::-1]), (5 * unit, z[:1] + y + z[1:]), (4 * unit, z[:1] + y + z[1:])]
    state, first = [], 0
    for group in (slice(0, 3),):
        chunks = plan[group]
        weight = None if state else kv_weight
        state += project(chunks, rows, ids, own_tokens, other_tokens, query_weight, weight, first)
        first += sum(columns for columns, _ in chunks)
    moving = [across(send, order[0]) for (send, _), (_, order) in zip(state, plan)]
    for step in range(len(bits)):
        for i, (columns, order) in enumerate(plan):
            total = state[i][1] + moving[i]
            if step + 1 < len(bits):
                cut = total.shape[0] // 2
                state[i] = (total[cut:], total[:cut])
                moving[i] = across(state[i][0], order[step + 1])
            else:
                state[i] = total
    mine, theirs = [], []
    for total in state:
        mine.append(lax.dynamic_slice_in_dim(total, core * own_rows, own_rows, 0).astype(jnp.bfloat16))
        give = lax.dynamic_slice_in_dim(total, (1 - core) * own_rows, own_rows, 0).astype(jnp.bfloat16)
        theirs.append(swap(give))

    kv_width = kv_weight.shape[1] // 2
    parts = tuple((columns // DH, 0 if i else kv_width) for i, (columns, _) in enumerate(plan))
    own, other = attend(core, lengths, mine, theirs, parts, key_cache, value_cache)
    got = swap(other)
    block = jnp.where(core == 0, jnp.concatenate([own, got]), jnp.concatenate([got, own]))

    near = [block[:, :width], block[:, width:]]
    far = [None, None]
    paths = [bits[::-1], bits[:1] + bits[:0:-1]]
    for step in range(len(bits)):
        for i in range(2):
            if step:
                near[i] = jnp.concatenate([near[i], far[i]])
            far[i] = across(near[i], paths[i][step])
    orders = [order_of(path[::-1]) for path in paths]
    blocks = [b for pair in zip(near, far) for b in pair]
    total_columns = out_weight.shape[1]
    cuts = 2 if total_columns % 768 == 0 else 1
    columns = total_columns // cuts
    results = []
    for cut in range(cuts):
        send, keep = project_out(orders, rows, ids, blocks, out_weight, cut * columns, columns)
        results.append((keep + swap(send)).astype(jnp.bfloat16))
    return jnp.concatenate(results, axis=1)


def solution(mesh):
    return jax.shard_map(
        local,
        mesh=mesh,
        in_specs=(
            P(("grp", "gy"), "gx"),
            P("gx", "gy"),
            P("gx", None),
            P("gy", "gx"),
            P(("grp", "gx", "gy"), None, None),
            P(("grp", "gx", "gy"), None, None),
            P(("grp", "gx", "gy")),
        ),
        out_specs=P(("grp", "gy"), "gx"),
        check_vma=False,
    )
```

```python
import functools

import jax
import jax.numpy as jnp
from jax import lax
from jax.experimental import pallas as pl
from jax.experimental.pallas import tpu as pltpu
from jax.sharding import PartitionSpec as P

H = 24
DH = 256
MIB = 1024 * 1024
HBM = pl.BlockSpec(memory_space=pltpu.HBM)
ANY = pl.BlockSpec(memory_space=pl.ANY)
VMEM = pl.BlockSpec(memory_space=pltpu.VMEM)
SMEM = pl.BlockSpec(memory_space=pltpu.SMEM)


class InOrder:
    def __init__(self, copies, ahead):
        self.copies, self.ahead = copies, ahead
        for copy in copies[:ahead]:
            copy.start()

    def wait(self, at):
        self.copies[at].wait()
        if at + self.ahead < len(self.copies):
            self.copies[at + self.ahead].start()


def order_of(bits):
    order = [0]
    for bit in reversed(bits):
        order = order + [j + bit for j in order]
    return order


def cuts_of(array):
    if len(array.shape) == 3:
        return [(at, None) for at in range(array.shape[0])]
    depth, columns = array.shape
    tall, wide = 512, (768 if columns % 768 == 0 else columns)
    return [
        ((at, tall), (column, wide)) for at in range(0, depth, tall) for column in range(0, columns, wide)
    ]


def piece_of(array, cut):
    if cut[1] is None:
        shape = array.shape[1:]
    else:
        shape = (cut[0][1], cut[1][1])
    return jax.ShapeDtypeStruct(shape, array.dtype)


def fetches(refs, cuts, targets, sems):
    copies = []
    for ref, cut in cuts:
        source = refs[ref]
        view = source.at[cut[0]] if cut[1] is None else source.at[pl.ds(*cut[0]), pl.ds(*cut[1])]
        copies.append(pltpu.make_async_copy(view, targets[len(copies)], sems.at[len(copies)]))
    return copies


def load_kernel(after, cuts, count, *refs):
    refs = refs[after:]
    in_refs, out_refs, zero_ref, sems = refs[:count], refs[count:-2], refs[-2], refs[-1]
    copies = fetches(in_refs, cuts, out_refs, sems)
    for copy in copies:
        copy.start()
    zero_ref[...] = jnp.zeros_like(zero_ref)
    for copy in copies:
        copy.wait()


def load(arrays, cuts, after, grant):
    shapes = [piece_of(arrays[at], cut) for at, cut in cuts]
    *held, zero = pl.pallas_call(
        functools.partial(load_kernel, len(after), cuts, len(arrays)),
        out_shape=(*shapes, jax.ShapeDtypeStruct((8, 128), jnp.float32)),
        in_specs=[ANY] * len(after) + [HBM] * len(arrays),
        out_specs=[VMEM] * (len(cuts) + 1),
        scratch_shapes=[pltpu.SemaphoreType.DMA((len(cuts),))],
        compiler_params=pltpu.CompilerParams(vmem_limit_bytes=grant * MIB),
        cost_estimate=pl.CostEstimate(
            flops=0, bytes_accessed=sum(4 * s.shape[0] * s.shape[1] for s in shapes), transcendentals=0
        ),
        name="load",
    )(*after, *arrays)
    return held, zero[0, 0]


def spans_of(width):
    return [(at, min(512, width - at)) for at in range(0, width, 512)]


def project_kernel(orders, rows, first, widths, kv_width, after, ids_ref, own_ref, other_ref, w_ref, *refs):
    refs = list(refs)
    kv_ref = refs.pop(0) if kv_width else None
    outs, (xs_ref, ws_ref, row_sem, w_sem) = refs[after:-4], refs[-4:]
    n = len(orders[0])
    half = n // 2
    me, core = ids_ref[0], ids_ref[1]
    features = xs_ref.shape[2]

    def row_copy(source_ref, chunk, p):
        block = jnp.bitwise_xor(me, orders[chunk][p])
        source = pl.ds(pl.multiple_of((block % half) * rows, rows), rows)
        return pltpu.make_async_copy(
            source_ref.at[source, :],
            xs_ref.at[chunk, pl.ds(p * rows, rows), :],
            row_sem.at[chunk, p],
        )

    for chunk, order in enumerate(orders):
        for p in range(n):
            mine = jnp.bitwise_xor(me, order[p]) // half == core

            @pl.when(mine)
            def _():
                row_copy(own_ref, chunk, p).start()

            @pl.when(jnp.logical_not(mine))
            def _():
                row_copy(other_ref, chunk, p).start()

    tiles, copies, at, source = [], [], 0, first
    depth = features // 2 if features % 32 == 0 else features

    def fetch(from_ref, column, width):
        for part in range(features // depth):
            span = pl.ds(part * depth, depth)
            copies.append(
                pltpu.make_async_copy(
                    from_ref.at[span, pl.ds(column, width)],
                    ws_ref.at[span, pl.ds(at, width)],
                    w_sem.at[len(copies)],
                )
            )

    for chunk, width in enumerate(widths):
        column = 0
        if kv_width and chunk == 0:
            fetch(kv_ref, pl.multiple_of(core * kv_width, kv_width), kv_width)
            tiles.append((chunk, 0, at, kv_width))
            at += kv_width
            column = kv_width
        for offset, tile in spans_of(width):
            fetch(w_ref, source, tile)
            tiles.append((chunk, column + offset, at, tile))
            at += tile
            source += tile
    per_tile = features // depth
    weights = InOrder(copies, 3 * per_tile)
    cut = half * rows
    ready = set()
    for t, (chunk, column, at, width) in enumerate(tiles):
        if chunk not in ready:
            ready.add(chunk)
            for p in range(n):
                row_copy(own_ref, chunk, p).wait()
        for part in range(per_tile):
            weights.wait(t * per_tile + part)
        total = jnp.dot(
            xs_ref[chunk], ws_ref[:, at : at + width], preferred_element_type=jnp.float32
        )
        span = slice(column, column + width)
        outs[2 * chunk][:, span] = total[cut:]
        outs[2 * chunk + 1][:, span] = total[:cut]


def project(plan, rows, ids, tokens, other, query_weight, kv_weight, first, after):
    features = tokens.shape[1]
    orders = [order_of(bits) for _, bits in plan]
    widths = [width for width, _ in plan]
    n = len(orders[0])
    kv_width = kv_weight.shape[1] // 2 if kv_weight is not None else 0
    columns = sum(widths) + kv_width
    outs = []
    for chunk, width in enumerate(widths):
        shape = (n * rows // 2, width + (0 if chunk else kv_width))
        outs += [jax.ShapeDtypeStruct(shape, jnp.float32)] * 2
    weights = [query_weight] + ([kv_weight] if kv_width else [])
    copies = 2 * (len(weights) - 1 + sum(len(spans_of(width)) for width in widths))
    outs = pl.pallas_call(
        functools.partial(project_kernel, orders, rows, first, widths, kv_width, len(after)),
        out_shape=outs,
        in_specs=[SMEM, ANY, ANY] + [HBM] * len(weights) + [ANY] * len(after),
        out_specs=[VMEM] * len(outs),
        scratch_shapes=[
            pltpu.VMEM((len(orders), n * rows, features), tokens.dtype),
            pltpu.VMEM((features, columns), tokens.dtype),
            pltpu.SemaphoreType.DMA((len(orders), n)),
            pltpu.SemaphoreType.DMA((copies,)),
        ],
        compiler_params=pltpu.CompilerParams(vmem_limit_bytes=46 * MIB),
        cost_estimate=pl.CostEstimate(
            flops=2 * n * rows * features * columns,
            bytes_accessed=2 * features * columns + 4 * n * rows * columns,
            transcendentals=0,
        ),
        name="project",
    )(ids, tokens, other, *weights, *after)
    return list(zip(outs[::2], outs[1::2]))


def attend_kernel(parts, rows, cuts, scalars_ref, *refs):
    own_q, other_q = refs[: len(parts)], refs[len(parts) : 2 * len(parts)]
    refs = refs[2 * len(parts) :]
    k_refs, v_refs, w_hbm, refs = refs[:rows], refs[rows : 2 * rows], refs[2 * rows], refs[2 * rows + 1 :]
    own_out, other_out, held, (q_scr, o_scr, sems) = refs[0], refs[1], refs[2:-3], refs[-3:]
    copies = fetches([w_hbm], [(0, cut) for cut in cuts], held, sems)
    for copy in copies:
        copy.start()
    core = scalars_ref[0]
    at = 0
    for side in (own_q, other_q):
        for ref, (heads, skip) in zip(side, parts):
            for head in range(heads):
                column = skip + head * DH
                q_scr[:, at, :] = ref[:, column : column + DH].astype(jnp.float32)
                at += 1
    total_heads = at
    kv_at = [skip > 0 for _, skip in parts].index(True)
    first = own_q[kv_at][:, :DH].astype(jnp.float32)
    second = other_q[kv_at][:, :DH].astype(jnp.float32)
    new_keys = jnp.where(core == 0, first, second)
    new_values = jnp.where(core == 0, second, first)
    scale = DH**-0.5
    for row in range(rows):
        query = q_scr[row]
        scores = scale * lax.dot_general(
            query.astype(jnp.bfloat16),
            k_refs[row][...],
            (((1,), (1,)), ((), ())),
            preferred_element_type=jnp.float32,
        )
        self_score = scale * jnp.sum(query * new_keys[row : row + 1], axis=1, keepdims=True)
        visible = lax.broadcasted_iota(jnp.int32, scores.shape, 1) < scalars_ref[1 + row]
        masked = jnp.where(visible, scores, jnp.float32(-1e30))
        peak = jnp.maximum(jnp.max(masked, axis=1, keepdims=True), self_score)
        raised = jnp.where(visible, jnp.exp(masked - peak), jnp.float32(0.0))
        self_raised = jnp.exp(self_score - peak)
        denominator = jnp.sum(raised, axis=1, keepdims=True) + self_raised
        weights = (raised / denominator).astype(jnp.bfloat16)
        self_weight = (self_raised / denominator).astype(jnp.bfloat16).astype(jnp.float32)
        total = jnp.dot(weights, v_refs[row][...], preferred_element_type=jnp.float32)
        o_scr[row] = total + self_weight * new_values[row : row + 1]
    half = total_heads // 2
    for head in range(total_heads):
        ref = own_out if head < half else other_out
        column = (head % half) * DH
        ref[:, column : column + DH] = o_scr[:, head, :].astype(jnp.bfloat16)
    for copy in copies:
        copy.wait()


def attend(core, lengths, own_q, other_q, parts, keys, values, out_weight, cuts):
    rows, (positions, _) = len(keys), keys[0].shape
    heads = 2 * sum(part[0] for part in parts)
    out = jax.ShapeDtypeStruct((rows, heads * DH // 2), jnp.bfloat16)
    scalars = jnp.concatenate([core[None], lengths])
    return pl.pallas_call(
        functools.partial(attend_kernel, parts, rows, cuts),
        out_shape=[out, out] + [piece_of(out_weight, cut) for cut in cuts],
        in_specs=[SMEM] + [VMEM] * (2 * len(parts) + 2 * rows) + [HBM],
        out_specs=[VMEM] * (2 + len(cuts)),
        scratch_shapes=[pltpu.VMEM((rows, heads, DH), jnp.float32)] * 2
        + [pltpu.SemaphoreType.DMA((max(1, len(cuts)),))],
        compiler_params=pltpu.CompilerParams(vmem_limit_bytes=28 * MIB),
        cost_estimate=pl.CostEstimate(
            flops=4 * rows * heads * positions * DH,
            bytes_accessed=4 * rows * positions * DH,
            transcendentals=rows * heads * positions,
        ),
        name="attend",
    )(scalars, *own_q, *other_q, *keys, *values, out_weight)


def output_kernel(orders, rows, columns, pieces, ids_ref, *refs):
    count = 2 * len(orders)
    block_refs, w_refs = refs[:count], refs[count : count + len(pieces)]
    send_ref, keep_ref, xs_ref, row_sem = refs[count + len(pieces) :]
    depth = block_refs[0].shape[1]
    me, core = ids_ref[0], ids_ref[1]
    n = len(orders[0])
    half = n // 2
    row_copies = []
    for group, (near_ref, far_ref) in enumerate(zip(block_refs[::2], block_refs[1::2])):
        for p, j in enumerate(orders[group]):
            block = jnp.bitwise_xor(me, j)
            place = block % half + jnp.where(block // half == core, half, 0)
            source = near_ref if p < half else far_ref
            row_copies.append(
                pltpu.make_async_copy(
                    source.at[pl.ds((p % half) * rows, rows), :],
                    xs_ref.at[
                        pl.ds(pl.multiple_of(place * rows, rows), rows), pl.ds(group * depth, depth)
                    ],
                    row_sem.at[group, p],
                )
            )
    for copy in row_copies:
        copy.start()
    for copy in row_copies:
        copy.wait()
    cut = half * rows
    totals = {}
    for w_ref, ((first, tall), span) in zip(w_refs, pieces):
        part = jnp.dot(
            xs_ref[:, first : first + tall], w_ref[...], preferred_element_type=jnp.float32
        )
        totals[span] = totals[span] + part if span in totals else part
    for (column, width), total in totals.items():
        send_ref[:, column - columns[0] : column - columns[0] + width] = total[:cut]
        keep_ref[:, column - columns[0] : column - columns[0] + width] = total[cut:]


def project_out(orders, rows, ids, blocks, held, cuts, columns):
    chosen = [at for at, (_, (column, _)) in enumerate(cuts) if columns[0] <= column < sum(columns)]
    weights, pieces = [held[at] for at in chosen], [cuts[at] for at in chosen]
    pieces, weights = zip(*sorted(zip(pieces, weights), key=lambda pair: (pair[0][1], pair[0][0])))
    depth = len(orders) * blocks[0].shape[1]
    n = len(orders[0])
    out = jax.ShapeDtypeStruct((n * rows // 2, columns[1]), jnp.float32)
    return pl.pallas_call(
        functools.partial(output_kernel, orders, rows, columns, pieces),
        out_shape=(out, out),
        in_specs=[SMEM] + [ANY] * len(blocks) + [VMEM] * len(weights),
        out_specs=(VMEM, VMEM),
        scratch_shapes=[
            pltpu.VMEM((n * rows, depth), jnp.bfloat16),
            pltpu.SemaphoreType.DMA((len(orders), n)),
        ],
        compiler_params=pltpu.CompilerParams(vmem_limit_bytes=12 * MIB),
        cost_estimate=pl.CostEstimate(
            flops=2 * n * rows * depth * columns[1],
            bytes_accessed=2 * depth * columns[1] + 4 * n * rows * columns[1],
            transcendentals=0,
        ),
        name="project_out",
    )(ids, *blocks, *weights)


def local(tokens, query_weight, kv_weight, out_weight, key_cache, value_cache, lengths):
    n = lax.axis_size("gx")
    me = lax.axis_index("gx").astype(jnp.int32)
    core = lax.axis_index("gy").astype(jnp.int32)
    ids = jnp.stack([me, core])
    own_rows = key_cache.shape[0]
    rows = 2 * own_rows
    bits = [1 << i for i in range(n.bit_length() - 1)]

    def swap(array):
        return lax.ppermute(array, "gy", [(0, 1), (1, 0)])

    def across(array, mask):
        return lax.ppermute(array, "gx", [(g, g ^ mask) for g in range(n)])

    other_tokens = swap(tokens)
    own_tokens = jnp.where(me < n, tokens, jnp.bfloat16(0))
    width = query_weight.shape[1] // 2

    y, z = bits[:1], bits[1:]
    unit = query_weight.shape[1] // 12
    plan = [(3 * unit, y + z[::-1]), (5 * unit, z[:1] + y + z[1:]), (4 * unit, z[:1] + y + z[1:])]
    state, first, after = [None] * len(plan), 0, []
    for group in ((2,), (0, 1)):
        chunks = [plan[i] for i in group]
        weight = kv_weight if 0 in group else None
        made = project(chunks, rows, ids, own_tokens, other_tokens, query_weight, weight, first, after)
        for i, pair in zip(group, made):
            state[i] = pair
        after = [made[0][0]]
        first += sum(columns for columns, _ in chunks)
    moving = [across(send, order[0]) for (send, _), (_, order) in zip(state, plan)]
    cache_cuts = [(at, cut) for at in range(2) for cut in cuts_of(key_cache)]
    out_cuts = cuts_of(out_weight)
    early = len(out_cuts) * 9 // 18
    for step in range(len(bits)):
        for turn, i in enumerate((2, 0, 1)):
            columns, order = plan[i]
            total = state[i][1] + moving[i]
            if step == 0 and turn:
                ahead = [state[(2, 0, 1)[turn - 1]][0]]
                if turn == 1:
                    caches, zero = load([key_cache, value_cache], cache_cuts, ahead, 41)
                else:
                    first_cuts = [(0, cut) for cut in out_cuts[:early]]
                    out_first, zero = load([out_weight], first_cuts, ahead, 36)
                total = total + zero
            if step + 1 < len(bits):
                cut = total.shape[0] // 2
                state[i] = (total[cut:], total[:cut])
                moving[i] = across(state[i][0], order[step + 1])
            else:
                state[i] = total
    mine, theirs = [], []
    for total in state:
        mine.append(lax.dynamic_slice_in_dim(total, core * own_rows, own_rows, 0).astype(jnp.bfloat16))
        give = lax.dynamic_slice_in_dim(total, (1 - core) * own_rows, own_rows, 0).astype(jnp.bfloat16)
        theirs.append(swap(give))

    kv_width = kv_weight.shape[1] // 2
    by_column = [i for group in ((2,), (0, 1)) for i in group]
    parts = tuple((plan[i][0] // DH, 0 if i else kv_width) for i in by_column)
    mine, theirs = [mine[i] for i in by_column], [theirs[i] for i in by_column]
    keys, values = caches[:own_rows], caches[own_rows:]
    own, other, *out_rest = attend(
        core, lengths, mine, theirs, parts, keys, values, out_weight, out_cuts[early:]
    )
    out_held = [*out_first, *out_rest]
    got = swap(other)
    block = jnp.where(core == 0, jnp.concatenate([own, got]), jnp.concatenate([got, own]))

    near = [block[:, :width], block[:, width:]]
    far = [None, None]
    paths = [bits[::-1], bits[:1] + bits[:0:-1]]
    for step in range(len(bits)):
        for i in range(2):
            if step:
                near[i] = jnp.concatenate([near[i], far[i]])
            far[i] = across(near[i], paths[i][step])
    orders = [order_of(path[::-1]) for path in paths]
    blocks = [b for pair in zip(near, far) for b in pair]
    total_columns = out_weight.shape[1]
    last = 768 if total_columns % 768 == 0 and total_columns > 768 else 0
    results = []
    for columns in ((0, total_columns - last), (total_columns - last, last)):
        if columns[1]:
            send, keep = project_out(orders, rows, ids, blocks, out_held, out_cuts, columns)
            results.append((keep + swap(send)).astype(jnp.bfloat16))
    return jnp.concatenate(results, axis=1)


def solution(mesh):
    return jax.shard_map(
        local,
        mesh=mesh,
        in_specs=(
            P(("grp", "gy"), "gx"),
            P("gx", "gy"),
            P("gx", None),
            P("gy", "gx"),
            P(("grp", "gx", "gy"), None, None),
            P(("grp", "gx", "gy"), None, None),
            P(("grp", "gx", "gy")),
        ),
        out_specs=P(("grp", "gy"), "gx"),
        check_vma=False,
    )
```

```python
import functools

import jax
import jax.numpy as jnp
from jax import lax
from jax.experimental import pallas as pl
from jax.experimental.pallas import tpu as pltpu
from jax.sharding import PartitionSpec as P

H = 24
DH = 256
MIB = 1024 * 1024
HBM = pl.BlockSpec(memory_space=pltpu.HBM)
ANY = pl.BlockSpec(memory_space=pl.ANY)
VMEM = pl.BlockSpec(memory_space=pltpu.VMEM)
SMEM = pl.BlockSpec(memory_space=pltpu.SMEM)


class InOrder:
    def __init__(self, copies, ahead):
        self.copies, self.ahead = copies, ahead
        for copy in copies[:ahead]:
            copy.start()

    def wait(self, at):
        self.copies[at].wait()
        if at + self.ahead < len(self.copies):
            self.copies[at + self.ahead].start()


def order_of(bits):
    order = [0]
    for bit in reversed(bits):
        order = order + [j + bit for j in order]
    return order


def cuts_of(array):
    if len(array.shape) == 3:
        return [(at, None) for at in range(array.shape[0])]
    depth, columns = array.shape
    tall, wide = 512, (768 if columns % 768 == 0 else columns)
    return [
        ((at, tall), (column, wide)) for at in range(0, depth, tall) for column in range(0, columns, wide)
    ]


def piece_of(array, cut):
    if cut[1] is None:
        shape = array.shape[1:]
    else:
        shape = (cut[0][1], cut[1][1])
    return jax.ShapeDtypeStruct(shape, array.dtype)


def fetches(refs, cuts, targets, sems):
    copies = []
    for ref, cut in cuts:
        source = refs[ref]
        view = source.at[cut[0]] if cut[1] is None else source.at[pl.ds(*cut[0]), pl.ds(*cut[1])]
        copies.append(pltpu.make_async_copy(view, targets[len(copies)], sems.at[len(copies)]))
    return copies


def load_kernel(after, cuts, count, *refs):
    refs = refs[after:]
    in_refs, out_refs, zero_ref, sems = refs[:count], refs[count:-2], refs[-2], refs[-1]
    copies = fetches(in_refs, cuts, out_refs, sems)
    for copy in copies:
        copy.start()
    zero_ref[...] = jnp.zeros_like(zero_ref)
    for copy in copies:
        copy.wait()


def load(arrays, cuts, after, grant, zeros=128):
    shapes = [piece_of(arrays[at], cut) for at, cut in cuts]
    *held, zero = pl.pallas_call(
        functools.partial(load_kernel, len(after), cuts, len(arrays)),
        out_shape=(*shapes, jax.ShapeDtypeStruct((1, zeros), jnp.float32)),
        in_specs=[ANY] * len(after) + [HBM] * len(arrays),
        out_specs=[VMEM] * (len(cuts) + 1),
        scratch_shapes=[pltpu.SemaphoreType.DMA((len(cuts),))],
        compiler_params=pltpu.CompilerParams(vmem_limit_bytes=grant * MIB),
        cost_estimate=pl.CostEstimate(
            flops=0, bytes_accessed=sum(4 * s.shape[0] * s.shape[1] for s in shapes), transcendentals=0
        ),
        name="load",
    )(*after, *arrays)
    return held, zero


def spans_of(width):
    return [(at, min(512, width - at)) for at in range(0, width, 512)]


def project_kernel(orders, rows, first, widths, kv_width, after, ids_ref, own_ref, other_ref, w_ref, *refs):
    refs = list(refs)
    kv_ref = refs.pop(0) if kv_width else None
    outs, (xs_ref, ws_ref, row_sem, w_sem) = refs[after:-4], refs[-4:]
    n = len(orders[0])
    half = n // 2
    me, core = ids_ref[0], ids_ref[1]
    features = xs_ref.shape[2]

    def row_copy(source_ref, chunk, p):
        block = jnp.bitwise_xor(me, orders[chunk][p])
        source = pl.ds(pl.multiple_of((block % half) * rows, rows), rows)
        return pltpu.make_async_copy(
            source_ref.at[source, :],
            xs_ref.at[chunk, pl.ds(p * rows, rows), :],
            row_sem.at[chunk, p],
        )

    for chunk, order in enumerate(orders):
        for p in range(n):
            mine = jnp.bitwise_xor(me, order[p]) // half == core

            @pl.when(mine)
            def _():
                row_copy(own_ref, chunk, p).start()

            @pl.when(jnp.logical_not(mine))
            def _():
                row_copy(other_ref, chunk, p).start()

    tiles, copies, at, source = [], [], 0, first
    depth = features // 2 if features % 32 == 0 else features

    def fetch(from_ref, column, width):
        for part in range(features // depth):
            span = pl.ds(part * depth, depth)
            copies.append(
                pltpu.make_async_copy(
                    from_ref.at[span, pl.ds(column, width)],
                    ws_ref.at[span, pl.ds(at, width)],
                    w_sem.at[len(copies)],
                )
            )

    for chunk, width in enumerate(widths):
        column = 0
        if kv_width and chunk == 0:
            fetch(kv_ref, pl.multiple_of(core * kv_width, kv_width), kv_width)
            tiles.append((chunk, 0, at, kv_width))
            at += kv_width
            column = kv_width
        for offset, tile in spans_of(width):
            fetch(w_ref, source, tile)
            tiles.append((chunk, column + offset, at, tile))
            at += tile
            source += tile
    per_tile = features // depth
    weights = InOrder(copies, 3 * per_tile)
    cut = half * rows
    ready = set()
    for t, (chunk, column, at, width) in enumerate(tiles):
        if chunk not in ready:
            ready.add(chunk)
            for p in range(n):
                row_copy(own_ref, chunk, p).wait()
        for part in range(per_tile):
            weights.wait(t * per_tile + part)
        total = jnp.dot(
            xs_ref[chunk], ws_ref[:, at : at + width], preferred_element_type=jnp.float32
        )
        span = slice(column, column + width)
        outs[2 * chunk][:, span] = total[cut:]
        outs[2 * chunk + 1][:, span] = total[:cut]


def project(plan, rows, ids, tokens, other, query_weight, kv_weight, first, after):
    features = tokens.shape[1]
    orders = [order_of(bits) for _, bits in plan]
    widths = [width for width, _ in plan]
    n = len(orders[0])
    kv_width = kv_weight.shape[1] // 2 if kv_weight is not None else 0
    columns = sum(widths) + kv_width
    outs = []
    for chunk, width in enumerate(widths):
        shape = (n * rows // 2, width + (0 if chunk else kv_width))
        outs += [jax.ShapeDtypeStruct(shape, jnp.float32)] * 2
    weights = [query_weight] + ([kv_weight] if kv_width else [])
    copies = 2 * (len(weights) - 1 + sum(len(spans_of(width)) for width in widths))
    outs = pl.pallas_call(
        functools.partial(project_kernel, orders, rows, first, widths, kv_width, len(after)),
        out_shape=outs,
        in_specs=[SMEM, ANY, ANY] + [HBM] * len(weights) + [ANY] * len(after),
        out_specs=[VMEM] * len(outs),
        scratch_shapes=[
            pltpu.VMEM((len(orders), n * rows, features), tokens.dtype),
            pltpu.VMEM((features, columns), tokens.dtype),
            pltpu.SemaphoreType.DMA((len(orders), n)),
            pltpu.SemaphoreType.DMA((copies,)),
        ],
        compiler_params=pltpu.CompilerParams(vmem_limit_bytes=46 * MIB),
        cost_estimate=pl.CostEstimate(
            flops=2 * n * rows * features * columns,
            bytes_accessed=2 * features * columns + 4 * n * rows * columns,
            transcendentals=0,
        ),
        name="project",
    )(ids, tokens, other, *weights, *after)
    return list(zip(outs[::2], outs[1::2]))


def attend_kernel(parts, scalars_ref, *refs):
    own_q, other_q = refs[: len(parts)], refs[len(parts) : 2 * len(parts)]
    k_ref, v_hbm, own_out, other_out, v_ref, q_scr, o_scr, sems = refs[2 * len(parts) :]
    core = scalars_ref[0]
    rows, positions, _ = k_ref.shape
    copies = [pltpu.make_async_copy(v_hbm.at[row], v_ref.at[row], sems.at[row]) for row in range(rows)]
    for copy in copies:
        copy.start()
    at = 0
    for side in (own_q, other_q):
        for ref, (heads, skip) in zip(side, parts):
            for head in range(heads):
                column = skip + head * DH
                q_scr[:, at, :] = ref[:, column : column + DH].astype(jnp.float32)
                at += 1
    total_heads = at
    kv_at = [skip > 0 for _, skip in parts].index(True)
    first = own_q[kv_at][:, :DH].astype(jnp.float32)
    second = other_q[kv_at][:, :DH].astype(jnp.float32)
    new_keys = jnp.where(core == 0, first, second)
    new_values = jnp.where(core == 0, second, first)
    scale = DH**-0.5
    shares = []
    for row in range(rows):
        query = q_scr[row]
        scores = scale * lax.dot_general(
            query.astype(jnp.bfloat16),
            k_ref[row],
            (((1,), (1,)), ((), ())),
            preferred_element_type=jnp.float32,
        )
        self_score = scale * jnp.sum(query * new_keys[row : row + 1], axis=1, keepdims=True)
        visible = lax.broadcasted_iota(jnp.int32, scores.shape, 1) < scalars_ref[1 + row]
        masked = jnp.where(visible, scores, jnp.float32(-1e30))
        peak = jnp.maximum(jnp.max(masked, axis=1, keepdims=True), self_score)
        raised = jnp.where(visible, jnp.exp(masked - peak), jnp.float32(0.0))
        self_raised = jnp.exp(self_score - peak)
        denominator = jnp.sum(raised, axis=1, keepdims=True) + self_raised
        weights = (raised / denominator).astype(jnp.bfloat16)
        self_weight = (self_raised / denominator).astype(jnp.bfloat16).astype(jnp.float32)
        shares.append((weights, self_weight))
    for copy in copies:
        copy.wait()
    for row, (weights, self_weight) in enumerate(shares):
        total = jnp.dot(weights, v_ref[row], preferred_element_type=jnp.float32)
        o_scr[row] = total + self_weight * new_values[row : row + 1]
    half = total_heads // 2
    for head in range(total_heads):
        ref = own_out if head < half else other_out
        column = (head % half) * DH
        ref[:, column : column + DH] = o_scr[:, head, :].astype(jnp.bfloat16)


def attend(core, lengths, own_q, other_q, parts, keys, values):
    rows, positions, _ = keys.shape
    heads = 2 * sum(part[0] for part in parts)
    out = jax.ShapeDtypeStruct((rows, heads * DH // 2), jnp.bfloat16)
    scalars = jnp.concatenate([core[None], lengths])
    return pl.pallas_call(
        functools.partial(attend_kernel, parts),
        out_shape=(out, out),
        in_specs=[SMEM] + [VMEM] * (2 * len(parts) + 1) + [HBM],
        out_specs=(VMEM, VMEM),
        scratch_shapes=[pltpu.VMEM(values.shape, values.dtype)]
        + [pltpu.VMEM((rows, heads, DH), jnp.float32)] * 2
        + [pltpu.SemaphoreType.DMA((rows,))],
        compiler_params=pltpu.CompilerParams(vmem_limit_bytes=49 * MIB),
        cost_estimate=pl.CostEstimate(
            flops=4 * rows * heads * positions * DH,
            bytes_accessed=4 * rows * positions * DH,
            transcendentals=rows * heads * positions,
        ),
        name="attend",
    )(scalars, *own_q, *other_q, keys, values)


def output_kernel(orders, rows, columns, pieces, ids_ref, *refs):
    count = 2 * len(orders)
    block_refs, w_refs = refs[:count], refs[count : count + len(pieces)]
    send_ref, keep_ref, xs_ref, row_sem = refs[count + len(pieces) :]
    depth = block_refs[0].shape[1]
    me, core = ids_ref[0], ids_ref[1]
    n = len(orders[0])
    half = n // 2
    row_copies = []
    for group, (near_ref, far_ref) in enumerate(zip(block_refs[::2], block_refs[1::2])):
        for p, j in enumerate(orders[group]):
            block = jnp.bitwise_xor(me, j)
            place = block % half + jnp.where(block // half == core, half, 0)
            source = near_ref if p < half else far_ref
            row_copies.append(
                pltpu.make_async_copy(
                    source.at[pl.ds((p % half) * rows, rows), :],
                    xs_ref.at[
                        pl.ds(pl.multiple_of(place * rows, rows), rows), pl.ds(group * depth, depth)
                    ],
                    row_sem.at[group, p],
                )
            )
    for copy in row_copies:
        copy.start()
    for copy in row_copies:
        copy.wait()
    cut = half * rows
    totals = {}
    for w_ref, ((first, tall), span) in zip(w_refs, pieces):
        part = jnp.dot(
            xs_ref[:, first : first + tall], w_ref[...], preferred_element_type=jnp.float32
        )
        totals[span] = totals[span] + part if span in totals else part
    for (column, width), total in totals.items():
        send_ref[:, column - columns[0] : column - columns[0] + width] = total[:cut]
        keep_ref[:, column - columns[0] : column - columns[0] + width] = total[cut:]


def project_out(orders, rows, ids, blocks, held, cuts, columns):
    chosen = [at for at, (_, (column, _)) in enumerate(cuts) if columns[0] <= column < sum(columns)]
    weights, pieces = [held[at] for at in chosen], [cuts[at] for at in chosen]
    pieces, weights = zip(*sorted(zip(pieces, weights), key=lambda pair: (pair[0][1], pair[0][0])))
    depth = len(orders) * blocks[0].shape[1]
    n = len(orders[0])
    out = jax.ShapeDtypeStruct((n * rows // 2, columns[1]), jnp.float32)
    return pl.pallas_call(
        functools.partial(output_kernel, orders, rows, columns, pieces),
        out_shape=(out, out),
        in_specs=[SMEM] + [ANY] * len(blocks) + [VMEM] * len(weights),
        out_specs=(VMEM, VMEM),
        scratch_shapes=[
            pltpu.VMEM((n * rows, depth), jnp.bfloat16),
            pltpu.SemaphoreType.DMA((len(orders), n)),
        ],
        compiler_params=pltpu.CompilerParams(vmem_limit_bytes=12 * MIB),
        cost_estimate=pl.CostEstimate(
            flops=2 * n * rows * depth * columns[1],
            bytes_accessed=2 * depth * columns[1] + 4 * n * rows * columns[1],
            transcendentals=0,
        ),
        name="project_out",
    )(ids, *blocks, *weights)


def local(tokens, query_weight, kv_weight, out_weight, key_cache, value_cache, lengths):
    n = lax.axis_size("gx")
    me = lax.axis_index("gx").astype(jnp.int32)
    core = lax.axis_index("gy").astype(jnp.int32)
    ids = jnp.stack([me, core])
    own_rows = key_cache.shape[0]
    rows = 2 * own_rows
    bits = [1 << i for i in range(n.bit_length() - 1)]

    def swap(array):
        return lax.ppermute(array, "gy", [(0, 1), (1, 0)])

    def across(array, mask):
        return lax.ppermute(array, "gx", [(g, g ^ mask) for g in range(n)])

    other_tokens = swap(tokens)
    own_tokens = jnp.where(me < n, tokens, jnp.bfloat16(0))
    width = query_weight.shape[1] // 2

    y, z = bits[:1], bits[1:]
    unit = query_weight.shape[1] // 12
    plan = [(3 * unit, y + z[::-1]), (5 * unit, z[:1] + y + z[1:]), (4 * unit, z[:1] + y + z[1:])]
    state, first, after = [None] * len(plan), 0, []
    for group in ((2,), (0, 1)):
        chunks = [plan[i] for i in group]
        weight = kv_weight if 0 in group else None
        made = project(chunks, rows, ids, own_tokens, other_tokens, query_weight, weight, first, after)
        for i, pair in zip(group, made):
            state[i] = pair
        after = [made[0][0]]
        first += sum(columns for columns, _ in chunks)
    moving = [across(send, order[0]) for (send, _), (_, order) in zip(state, plan)]
    for step in range(len(bits)):
        for i in (2, 0, 1):
            columns, order = plan[i]
            total = state[i][1] + moving[i]
            if step + 1 < len(bits):
                cut = total.shape[0] // 2
                state[i] = (total[cut:], total[:cut])
                moving[i] = across(state[i][0], order[step + 1])
            else:
                state[i] = total
    mine, theirs = [], []
    for total in state:
        mine.append(lax.dynamic_slice_in_dim(total, core * own_rows, own_rows, 0).astype(jnp.bfloat16))
        give = lax.dynamic_slice_in_dim(total, (1 - core) * own_rows, own_rows, 0).astype(jnp.bfloat16)
        theirs.append(swap(give))

    kv_width = kv_weight.shape[1] // 2
    by_column = [i for group in ((2,), (0, 1)) for i in group]
    parts = tuple((plan[i][0] // DH, 0 if i else kv_width) for i in by_column)
    mine, theirs = [mine[i] for i in by_column], [theirs[i] for i in by_column]
    own, other = attend(core, lengths, mine, theirs, parts, key_cache, value_cache)
    got = swap(other)
    block = jnp.where(core == 0, jnp.concatenate([own, got]), jnp.concatenate([got, own]))

    near = [block[:, :width], block[:, width:]]
    far = [None, None]
    paths = [bits[::-1], bits[:1] + bits[:0:-1]]
    out_cuts, out_held = cuts_of(out_weight), []
    early = len(out_cuts) * 9 // 18
    for step in range(len(bits)):
        for i in range(2):
            if step:
                near[i] = jnp.concatenate([near[i], far[i]])
                if i == 0 and out_held:
                    near[i] = near[i] + zero.astype(jnp.bfloat16)
                if i == 1 and step + 2 >= len(bits):
                    part = out_cuts[early:] if out_held else out_cuts[:early]
                    held, zero = load([out_weight], [(0, cut) for cut in part], near, 36, width)
                    out_held += held
            far[i] = across(near[i], paths[i][step])
    orders = [order_of(path[::-1]) for path in paths]
    blocks = [b for pair in zip(near, far) for b in pair]
    total_columns = out_weight.shape[1]
    last = 768 if total_columns % 768 == 0 and total_columns > 768 else 0
    results = []
    for columns in ((0, total_columns - last), (total_columns - last, last)):
        if columns[1]:
            send, keep = project_out(orders, rows, ids, blocks, out_held, out_cuts, columns)
            results.append((keep + swap(send)).astype(jnp.bfloat16))
    return jnp.concatenate(results, axis=1)


def solution(mesh):
    return jax.shard_map(
        local,
        mesh=mesh,
        in_specs=(
            P(("grp", "gy"), "gx"),
            P("gx", "gy"),
            P("gx", None),
            P("gy", "gx"),
            P(("grp", "gx", "gy"), None, None),
            P(("grp", "gx", "gy"), None, None),
            P(("grp", "gx", "gy")),
        ),
        out_specs=P(("grp", "gy"), "gx"),
        check_vma=False,
    )
```

```python
import functools

import jax
import jax.numpy as jnp
from jax import lax
from jax.experimental import pallas as pl
from jax.experimental.pallas import tpu as pltpu
from jax.sharding import PartitionSpec as P

H = 24
DH = 256
MIB = 1024 * 1024
HBM = pl.BlockSpec(memory_space=pltpu.HBM)
ANY = pl.BlockSpec(memory_space=pl.ANY)
VMEM = pl.BlockSpec(memory_space=pltpu.VMEM)
SMEM = pl.BlockSpec(memory_space=pltpu.SMEM)


class InOrder:
    def __init__(self, copies, ahead):
        self.copies, self.ahead = copies, ahead
        for copy in copies[:ahead]:
            copy.start()

    def wait(self, at):
        self.copies[at].wait()
        if at + self.ahead < len(self.copies):
            self.copies[at + self.ahead].start()


def order_of(bits):
    order = [0]
    for bit in reversed(bits):
        order = order + [j + bit for j in order]
    return order


def cuts_of(array):
    if len(array.shape) == 3:
        return [(at, None) for at in range(array.shape[0])]
    depth, columns = array.shape
    tall, wide = 512, (768 if columns % 768 == 0 else columns)
    return [
        ((at, tall), (column, wide)) for at in range(0, depth, tall) for column in range(0, columns, wide)
    ]


def piece_of(array, cut):
    if cut[1] is None:
        shape = array.shape[1:]
    else:
        shape = (cut[0][1], cut[1][1])
    return jax.ShapeDtypeStruct(shape, array.dtype)


def fetches(refs, cuts, targets, sems):
    copies = []
    for ref, cut in cuts:
        source = refs[ref]
        view = source.at[cut[0]] if cut[1] is None else source.at[pl.ds(*cut[0]), pl.ds(*cut[1])]
        copies.append(pltpu.make_async_copy(view, targets[len(copies)], sems.at[len(copies)]))
    return copies


def load_kernel(after, cuts, count, *refs):
    refs = refs[after:]
    in_refs, out_refs, zero_ref, sems = refs[:count], refs[count:-2], refs[-2], refs[-1]
    copies = fetches(in_refs, cuts, out_refs, sems)
    for copy in copies:
        copy.start()
    zero_ref[...] = jnp.zeros_like(zero_ref)
    for copy in copies:
        copy.wait()


def load(arrays, cuts, after, grant, zeros=128):
    shapes = [piece_of(arrays[at], cut) for at, cut in cuts]
    *held, zero = pl.pallas_call(
        functools.partial(load_kernel, len(after), cuts, len(arrays)),
        out_shape=(*shapes, jax.ShapeDtypeStruct((1, zeros), jnp.float32)),
        in_specs=[ANY] * len(after) + [HBM] * len(arrays),
        out_specs=[VMEM] * (len(cuts) + 1),
        scratch_shapes=[pltpu.SemaphoreType.DMA((len(cuts),))],
        compiler_params=pltpu.CompilerParams(vmem_limit_bytes=grant * MIB),
        cost_estimate=pl.CostEstimate(
            flops=0, bytes_accessed=sum(4 * s.shape[0] * s.shape[1] for s in shapes), transcendentals=0
        ),
        name="load",
    )(*after, *arrays)
    return held, zero


def spans_of(width):
    return [(at, min(512, width - at)) for at in range(0, width, 512)]


def project_kernel(orders, rows, first, widths, kv_width, after, ids_ref, own_ref, other_ref, w_ref, *refs):
    refs = list(refs)
    kv_ref = refs.pop(0) if kv_width else None
    outs, (xs_ref, ws_ref, row_sem, w_sem) = refs[after:-4], refs[-4:]
    n = len(orders[0])
    half = n // 2
    me, core = ids_ref[0], ids_ref[1]
    features = xs_ref.shape[2]

    def row_copy(source_ref, chunk, p):
        block = jnp.bitwise_xor(me, orders[chunk][p])
        source = pl.ds(pl.multiple_of((block % half) * rows, rows), rows)
        return pltpu.make_async_copy(
            source_ref.at[source, :],
            xs_ref.at[chunk, pl.ds(p * rows, rows), :],
            row_sem.at[chunk, p],
        )

    for chunk, order in enumerate(orders):
        for p in range(n):
            mine = jnp.bitwise_xor(me, order[p]) // half == core

            @pl.when(mine)
            def _():
                row_copy(own_ref, chunk, p).start()

            @pl.when(jnp.logical_not(mine))
            def _():
                row_copy(other_ref, chunk, p).start()

    tiles, copies, at, source = [], [], 0, first
    depth = features // 2 if features % 32 == 0 else features

    def fetch(from_ref, column, width):
        for part in range(features // depth):
            span = pl.ds(part * depth, depth)
            copies.append(
                pltpu.make_async_copy(
                    from_ref.at[span, pl.ds(column, width)],
                    ws_ref.at[span, pl.ds(at, width)],
                    w_sem.at[len(copies)],
                )
            )

    for chunk, width in enumerate(widths):
        column = 0
        if kv_width and chunk == 0:
            fetch(kv_ref, pl.multiple_of(core * kv_width, kv_width), kv_width)
            tiles.append((chunk, 0, at, kv_width))
            at += kv_width
            column = kv_width
        for offset, tile in spans_of(width):
            fetch(w_ref, source, tile)
            tiles.append((chunk, column + offset, at, tile))
            at += tile
            source += tile
    per_tile = features // depth
    weights = InOrder(copies, 3)
    cut = half * rows
    ready = set()
    for t, (chunk, column, at, width) in enumerate(tiles):
        if chunk not in ready:
            ready.add(chunk)
            for p in range(n):
                row_copy(own_ref, chunk, p).wait()
        for part in range(per_tile):
            weights.wait(t * per_tile + part)
        total = jnp.dot(
            xs_ref[chunk], ws_ref[:, at : at + width], preferred_element_type=jnp.float32
        )
        span = slice(column, column + width)
        outs[2 * chunk][:, span] = total[cut:]
        outs[2 * chunk + 1][:, span] = total[:cut]


def project(plan, rows, ids, tokens, other, query_weight, kv_weight, first, after):
    features = tokens.shape[1]
    orders = [order_of(bits) for _, bits in plan]
    widths = [width for width, _ in plan]
    n = len(orders[0])
    kv_width = kv_weight.shape[1] // 2 if kv_weight is not None else 0
    columns = sum(widths) + kv_width
    outs = []
    for chunk, width in enumerate(widths):
        shape = (n * rows // 2, width + (0 if chunk else kv_width))
        outs += [jax.ShapeDtypeStruct(shape, jnp.float32)] * 2
    weights = [query_weight] + ([kv_weight] if kv_width else [])
    copies = 2 * (len(weights) - 1 + sum(len(spans_of(width)) for width in widths))
    outs = pl.pallas_call(
        functools.partial(project_kernel, orders, rows, first, widths, kv_width, len(after)),
        out_shape=outs,
        in_specs=[SMEM, ANY, ANY] + [HBM] * len(weights) + [ANY] * len(after),
        out_specs=[VMEM] * len(outs),
        scratch_shapes=[
            pltpu.VMEM((len(orders), n * rows, features), tokens.dtype),
            pltpu.VMEM((features, columns), tokens.dtype),
            pltpu.SemaphoreType.DMA((len(orders), n)),
            pltpu.SemaphoreType.DMA((copies,)),
        ],
        compiler_params=pltpu.CompilerParams(vmem_limit_bytes=46 * MIB),
        cost_estimate=pl.CostEstimate(
            flops=2 * n * rows * features * columns,
            bytes_accessed=2 * features * columns + 4 * n * rows * columns,
            transcendentals=0,
        ),
        name="project",
    )(ids, tokens, other, *weights, *after)
    return list(zip(outs[::2], outs[1::2]))


def attend_kernel(parts, scalars_ref, *refs):
    own_q, other_q = refs[: len(parts)], refs[len(parts) : 2 * len(parts)]
    k_ref, v_hbm, own_out, other_out, v_ref, q_scr, o_scr, sems = refs[2 * len(parts) :]
    core = scalars_ref[0]
    rows, positions, _ = k_ref.shape
    copies = [pltpu.make_async_copy(v_hbm.at[row], v_ref.at[row], sems.at[row]) for row in range(rows)]
    for copy in copies:
        copy.start()
    at = 0
    for side in (own_q, other_q):
        for ref, (heads, skip) in zip(side, parts):
            for head in range(heads):
                column = skip + head * DH
                q_scr[:, at, :] = ref[:, column : column + DH].astype(jnp.float32)
                at += 1
    total_heads = at
    kv_at = [skip > 0 for _, skip in parts].index(True)
    first = own_q[kv_at][:, :DH].astype(jnp.float32)
    second = other_q[kv_at][:, :DH].astype(jnp.float32)
    new_keys = jnp.where(core == 0, first, second)
    new_values = jnp.where(core == 0, second, first)
    scale = DH**-0.5
    shares = []
    for row in range(rows):
        query = q_scr[row]
        scores = scale * lax.dot_general(
            query.astype(jnp.bfloat16),
            k_ref[row],
            (((1,), (1,)), ((), ())),
            preferred_element_type=jnp.float32,
        )
        self_score = scale * jnp.sum(query * new_keys[row : row + 1], axis=1, keepdims=True)
        visible = lax.broadcasted_iota(jnp.int32, scores.shape, 1) < scalars_ref[1 + row]
        masked = jnp.where(visible, scores, jnp.float32(-1e30))
        peak = jnp.maximum(jnp.max(masked, axis=1, keepdims=True), self_score)
        raised = jnp.where(visible, jnp.exp(masked - peak), jnp.float32(0.0))
        self_raised = jnp.exp(self_score - peak)
        denominator = jnp.sum(raised, axis=1, keepdims=True) + self_raised
        weights = (raised / denominator).astype(jnp.bfloat16)
        self_weight = (self_raised / denominator).astype(jnp.bfloat16).astype(jnp.float32)
        shares.append((weights, self_weight))
    for copy in copies:
        copy.wait()
    for row, (weights, self_weight) in enumerate(shares):
        total = jnp.dot(weights, v_ref[row], preferred_element_type=jnp.float32)
        o_scr[row] = total + self_weight * new_values[row : row + 1]
    half = total_heads // 2
    for head in range(total_heads):
        ref = own_out if head < half else other_out
        column = (head % half) * DH
        ref[:, column : column + DH] = o_scr[:, head, :].astype(jnp.bfloat16)


def attend(core, lengths, own_q, other_q, parts, keys, values):
    rows, positions, _ = keys.shape
    heads = 2 * sum(part[0] for part in parts)
    out = jax.ShapeDtypeStruct((rows, heads * DH // 2), jnp.bfloat16)
    scalars = jnp.concatenate([core[None], lengths])
    return pl.pallas_call(
        functools.partial(attend_kernel, parts),
        out_shape=(out, out),
        in_specs=[SMEM] + [VMEM] * (2 * len(parts) + 1) + [HBM],
        out_specs=(VMEM, VMEM),
        scratch_shapes=[pltpu.VMEM(values.shape, values.dtype)]
        + [pltpu.VMEM((rows, heads, DH), jnp.float32)] * 2
        + [pltpu.SemaphoreType.DMA((rows,))],
        compiler_params=pltpu.CompilerParams(vmem_limit_bytes=49 * MIB),
        cost_estimate=pl.CostEstimate(
            flops=4 * rows * heads * positions * DH,
            bytes_accessed=4 * rows * positions * DH,
            transcendentals=rows * heads * positions,
        ),
        name="attend",
    )(scalars, *own_q, *other_q, keys, values)


def output_kernel(orders, rows, columns, pieces, after, ids_ref, *refs):
    count = 2 * len(orders)
    block_refs, w_refs = refs[:count], refs[count : count + len(pieces)]
    send_ref, keep_ref, xs_ref = refs[count + len(pieces) + after :]
    depth = block_refs[0].shape[1]
    me, core = ids_ref[0], ids_ref[1]
    n = len(orders[0])
    half = n // 2
    for group, (near_ref, far_ref) in enumerate(zip(block_refs[::2], block_refs[1::2])):
        for p, j in enumerate(orders[group]):
            block = jnp.bitwise_xor(me, j)
            place = block % half + jnp.where(block // half == core, half, 0)
            source = near_ref if p < half else far_ref
            at = (p % half) * rows
            xs_ref[
                pl.ds(pl.multiple_of(place * rows, rows), rows), group * depth : (group + 1) * depth
            ] = source[at : at + rows, :]
    cut = half * rows
    totals = {}
    for w_ref, ((first, tall), span) in zip(w_refs, pieces):
        part = jnp.dot(
            xs_ref[:, first : first + tall], w_ref[...], preferred_element_type=jnp.float32
        )
        totals[span] = totals[span] + part if span in totals else part
    for (column, width), total in totals.items():
        send_ref[:, column - columns[0] : column - columns[0] + width] = total[:cut]
        keep_ref[:, column - columns[0] : column - columns[0] + width] = total[cut:]


def project_out(orders, rows, ids, blocks, held, cuts, columns, after):
    chosen = [at for at, (_, (column, _)) in enumerate(cuts) if columns[0] <= column < sum(columns)]
    weights, pieces = [held[at] for at in chosen], [cuts[at] for at in chosen]
    pieces, weights = zip(*sorted(zip(pieces, weights), key=lambda pair: (pair[0][1], pair[0][0])))
    depth = len(orders) * blocks[0].shape[1]
    n = len(orders[0])
    out = jax.ShapeDtypeStruct((n * rows // 2, columns[1]), jnp.float32)
    return pl.pallas_call(
        functools.partial(output_kernel, orders, rows, columns, pieces, len(after)),
        out_shape=(out, out),
        in_specs=[SMEM] + [VMEM] * (len(blocks) + len(weights)) + [ANY] * len(after),
        out_specs=(VMEM, VMEM),
        scratch_shapes=[pltpu.VMEM((n * rows, depth), jnp.bfloat16)],
        compiler_params=pltpu.CompilerParams(vmem_limit_bytes=12 * MIB),
        cost_estimate=pl.CostEstimate(
            flops=2 * n * rows * depth * columns[1],
            bytes_accessed=2 * depth * columns[1] + 4 * n * rows * columns[1],
            transcendentals=0,
        ),
        name="project_out",
    )(ids, *blocks, *weights, *after)


def local(tokens, query_weight, kv_weight, out_weight, key_cache, value_cache, lengths):
    n = lax.axis_size("gx")
    me = lax.axis_index("gx").astype(jnp.int32)
    core = lax.axis_index("gy").astype(jnp.int32)
    ids = jnp.stack([me, core])
    own_rows = key_cache.shape[0]
    rows = 2 * own_rows
    bits = [1 << i for i in range(n.bit_length() - 1)]

    def swap(array):
        return lax.ppermute(array, "gy", [(0, 1), (1, 0)])

    def across(array, mask):
        return lax.ppermute(array, "gx", [(g, g ^ mask) for g in range(n)])

    other_tokens = swap(tokens)
    own_tokens = jnp.where(me < n, tokens, jnp.bfloat16(0))
    width = query_weight.shape[1] // 2

    y, z = bits[:1], bits[1:]
    unit = query_weight.shape[1] // 12
    plan = [(3 * unit, z[:1] + y + z[1:]), (5 * unit, y + z), (4 * unit, z + y)]
    state, first, after = [None] * len(plan), 0, []
    for group in ((2,), (0, 1)):
        chunks = [plan[i] for i in group]
        weight = kv_weight if 0 in group else None
        made = project(chunks, rows, ids, own_tokens, other_tokens, query_weight, weight, first, after)
        for i, pair in zip(group, made):
            state[i] = pair
        after = [made[0][0]]
        first += sum(columns for columns, _ in chunks)
    moving = [across(send, order[0]) for (send, _), (_, order) in zip(state, plan)]
    for step in range(len(bits)):
        for i in (2, 0, 1):
            columns, order = plan[i]
            total = state[i][1] + moving[i]
            if step + 1 < len(bits):
                cut = total.shape[0] // 2
                state[i] = (total[cut:], total[:cut])
                moving[i] = across(state[i][0], order[step + 1])
            else:
                state[i] = total
    mine, theirs = [], []
    for total in state:
        mine.append(lax.dynamic_slice_in_dim(total, core * own_rows, own_rows, 0).astype(jnp.bfloat16))
        give = lax.dynamic_slice_in_dim(total, (1 - core) * own_rows, own_rows, 0).astype(jnp.bfloat16)
        theirs.append(swap(give))

    kv_width = kv_weight.shape[1] // 2
    by_column = [i for group in ((2,), (0, 1)) for i in group]
    parts = tuple((plan[i][0] // DH, 0 if i else kv_width) for i in by_column)
    mine, theirs = [mine[i] for i in by_column], [theirs[i] for i in by_column]
    own, other = attend(core, lengths, mine, theirs, parts, key_cache, value_cache)
    got = swap(other)
    block = jnp.where(core == 0, jnp.concatenate([own, got]), jnp.concatenate([got, own]))

    near = [block[:, :width], block[:, width:]]
    far = [None, None]
    paths = [bits[::-1], bits[:1] + bits[:0:-1]]
    out_cuts, out_held = cuts_of(out_weight), []
    early = len(out_cuts) * 9 // 18
    for step in range(len(bits)):
        for i in range(2):
            if step:
                near[i] = jnp.concatenate([near[i], far[i]])
                if i == 0 and out_held:
                    near[i] = near[i] + zero.astype(jnp.bfloat16)
                if i == 1 and step + 2 >= len(bits):
                    part = out_cuts[early:] if out_held else out_cuts[:early]
                    held, zero = load([out_weight], [(0, cut) for cut in part], near, 36, width)
                    out_held += held
            far[i] = across(near[i], paths[i][step])
    orders = [order_of(path[::-1]) for path in paths]
    blocks = [b for pair in zip(near, far) for b in pair]
    total_columns = out_weight.shape[1]
    last = 768 if total_columns % 768 == 0 and total_columns > 768 else 0
    results, after = [], []
    for columns in ((0, total_columns - last), (total_columns - last, last)):
        if columns[1]:
            send, keep = project_out(orders, rows, ids, blocks, out_held, out_cuts, columns, after)
            after = [send]
            results.append((keep + swap(send)).astype(jnp.bfloat16))
    return jnp.concatenate(results, axis=1)


def solution(mesh):
    return jax.shard_map(
        local,
        mesh=mesh,
        in_specs=(
            P(("grp", "gy"), "gx"),
            P("gx", "gy"),
            P("gx", None),
            P("gy", "gx"),
            P(("grp", "gx", "gy"), None, None),
            P(("grp", "gx", "gy"), None, None),
            P(("grp", "gx", "gy")),
        ),
        out_specs=P(("grp", "gy"), "gx"),
        check_vma=False,
    )
```

```python
import functools

import jax
import jax.numpy as jnp
from jax import lax
from jax.experimental import pallas as pl
from jax.experimental.pallas import tpu as pltpu
from jax.sharding import PartitionSpec as P

H = 24
DH = 256
MIB = 1024 * 1024
HBM = pl.BlockSpec(memory_space=pltpu.HBM)
ANY = pl.BlockSpec(memory_space=pl.ANY)
VMEM = pl.BlockSpec(memory_space=pltpu.VMEM)
SMEM = pl.BlockSpec(memory_space=pltpu.SMEM)


class InOrder:
    def __init__(self, copies, ahead):
        self.copies, self.ahead = copies, ahead
        for copy in copies[:ahead]:
            copy.start()

    def wait(self, at):
        self.copies[at].wait()
        if at + self.ahead < len(self.copies):
            self.copies[at + self.ahead].start()


def order_of(bits):
    order = [0]
    for bit in reversed(bits):
        order = order + [j + bit for j in order]
    return order


def cuts_of(array):
    if len(array.shape) == 3:
        return [(at, None) for at in range(array.shape[0])]
    depth, columns = array.shape
    tall, wide = 512, (768 if columns % 768 == 0 else columns)
    return [
        ((at, tall), (column, wide)) for at in range(0, depth, tall) for column in range(0, columns, wide)
    ]


def piece_of(array, cut):
    if cut[1] is None:
        shape = array.shape[1:]
    else:
        shape = (cut[0][1], cut[1][1])
    return jax.ShapeDtypeStruct(shape, array.dtype)


def fetches(refs, cuts, targets, sems):
    copies = []
    for ref, cut in cuts:
        source = refs[ref]
        view = source.at[cut[0]] if cut[1] is None else source.at[pl.ds(*cut[0]), pl.ds(*cut[1])]
        copies.append(pltpu.make_async_copy(view, targets[len(copies)], sems.at[len(copies)]))
    return copies


def load_kernel(after, cuts, count, *refs):
    refs = refs[after:]
    in_refs, out_refs, zero_ref, sems = refs[:count], refs[count:-2], refs[-2], refs[-1]
    copies = fetches(in_refs, cuts, out_refs, sems)
    for copy in copies:
        copy.start()
    zero_ref[...] = jnp.zeros_like(zero_ref)
    for copy in copies:
        copy.wait()


def load(arrays, cuts, after, grant, zeros=128):
    shapes = [piece_of(arrays[at], cut) for at, cut in cuts]
    *held, zero = pl.pallas_call(
        functools.partial(load_kernel, len(after), cuts, len(arrays)),
        out_shape=(*shapes, jax.ShapeDtypeStruct((1, zeros), jnp.float32)),
        in_specs=[ANY] * len(after) + [HBM] * len(arrays),
        out_specs=[VMEM] * (len(cuts) + 1),
        scratch_shapes=[pltpu.SemaphoreType.DMA((len(cuts),))],
        compiler_params=pltpu.CompilerParams(vmem_limit_bytes=grant * MIB),
        cost_estimate=pl.CostEstimate(
            flops=0, bytes_accessed=sum(4 * s.shape[0] * s.shape[1] for s in shapes), transcendentals=0
        ),
        name="load",
    )(*after, *arrays)
    return held, zero


def spans_of(width):
    return [(at, min(512, width - at)) for at in range(0, width, 512)]


def project_kernel(orders, rows, first, widths, kv_width, after, ids_ref, own_ref, other_ref, w_ref, *refs):
    refs = list(refs)
    kv_ref = refs.pop(0) if kv_width else None
    outs, (xs_ref, ws_ref, row_sem, w_sem) = refs[after:-4], refs[-4:]
    n = len(orders[0])
    half = n // 2
    me, core = ids_ref[0], ids_ref[1]
    features = xs_ref.shape[2]

    def row_copy(source_ref, chunk, p):
        block = jnp.bitwise_xor(me, orders[chunk][p])
        source = pl.ds(pl.multiple_of((block % half) * rows, rows), rows)
        return pltpu.make_async_copy(
            source_ref.at[source, :],
            xs_ref.at[chunk, pl.ds(p * rows, rows), :],
            row_sem.at[chunk, p],
        )

    for chunk, order in enumerate(orders):
        for p in range(n):
            mine = jnp.bitwise_xor(me, order[p]) // half == core

            @pl.when(mine)
            def _():
                row_copy(own_ref, chunk, p).start()

            @pl.when(jnp.logical_not(mine))
            def _():
                row_copy(other_ref, chunk, p).start()

    tiles, copies, at, source = [], [], 0, first
    depth = 768 if features % 768 == 0 else features

    def fetch(from_ref, column, width):
        for part in range(features // depth):
            span = pl.ds(part * depth, depth)
            copies.append(
                pltpu.make_async_copy(
                    from_ref.at[span, pl.ds(column, width)],
                    ws_ref.at[span, pl.ds(at, width)],
                    w_sem.at[len(copies)],
                )
            )

    for chunk, width in enumerate(widths):
        column = 0
        if kv_width and chunk == 0:
            fetch(kv_ref, pl.multiple_of(core * kv_width, kv_width), kv_width)
            tiles.append((chunk, 0, at, kv_width))
            at += kv_width
            column = kv_width
        for offset, tile in spans_of(width):
            fetch(w_ref, source, tile)
            tiles.append((chunk, column + offset, at, tile))
            at += tile
            source += tile
    per_tile = features // depth
    weights = InOrder(copies, 9)
    cut = half * rows
    ready = set()
    for t, (chunk, column, at, width) in enumerate(tiles):
        if chunk not in ready:
            ready.add(chunk)
            for p in range(n):
                row_copy(own_ref, chunk, p).wait()
        for part in range(per_tile):
            weights.wait(t * per_tile + part)
        total = jnp.dot(
            xs_ref[chunk], ws_ref[:, at : at + width], preferred_element_type=jnp.float32
        )
        span = slice(column, column + width)
        outs[2 * chunk][:, span] = total[cut:]
        outs[2 * chunk + 1][:, span] = total[:cut]


def project(plan, rows, ids, tokens, other, query_weight, kv_weight, first, after):
    features = tokens.shape[1]
    orders = [order_of(bits) for _, bits in plan]
    widths = [width for width, _ in plan]
    n = len(orders[0])
    kv_width = kv_weight.shape[1] // 2 if kv_weight is not None else 0
    columns = sum(widths) + kv_width
    outs = []
    for chunk, width in enumerate(widths):
        shape = (n * rows // 2, width + (0 if chunk else kv_width))
        outs += [jax.ShapeDtypeStruct(shape, jnp.float32)] * 2
    weights = [query_weight] + ([kv_weight] if kv_width else [])
    parts = features // 768 if features % 768 == 0 else 1
    copies = parts * (len(weights) - 1 + sum(len(spans_of(width)) for width in widths))
    outs = pl.pallas_call(
        functools.partial(project_kernel, orders, rows, first, widths, kv_width, len(after)),
        out_shape=outs,
        in_specs=[SMEM, ANY, ANY] + [HBM] * len(weights) + [ANY] * len(after),
        out_specs=[VMEM] * len(outs),
        scratch_shapes=[
            pltpu.VMEM((len(orders), n * rows, features), tokens.dtype),
            pltpu.VMEM((features, columns), tokens.dtype),
            pltpu.SemaphoreType.DMA((len(orders), n)),
            pltpu.SemaphoreType.DMA((copies,)),
        ],
        compiler_params=pltpu.CompilerParams(vmem_limit_bytes=46 * MIB),
        cost_estimate=pl.CostEstimate(
            flops=2 * n * rows * features * columns,
            bytes_accessed=2 * features * columns + 4 * n * rows * columns,
            transcendentals=0,
        ),
        name="project",
    )(ids, tokens, other, *weights, *after)
    return list(zip(outs[::2], outs[1::2]))


def attend_kernel(parts, scalars_ref, *refs):
    own_q, other_q = refs[: len(parts)], refs[len(parts) : 2 * len(parts)]
    k_ref, v_hbm, own_out, other_out, v_ref, q_scr, o_scr, sems = refs[2 * len(parts) :]
    core = scalars_ref[0]
    rows, positions, _ = k_ref.shape
    copies = [pltpu.make_async_copy(v_hbm.at[row], v_ref.at[row], sems.at[row]) for row in range(rows)]
    for copy in copies:
        copy.start()
    at = 0
    for side in (own_q, other_q):
        for ref, (heads, skip) in zip(side, parts):
            for head in range(heads):
                column = skip + head * DH
                q_scr[:, at, :] = ref[:, column : column + DH].astype(jnp.float32)
                at += 1
    total_heads = at
    kv_at = [skip > 0 for _, skip in parts].index(True)
    first = own_q[kv_at][:, :DH].astype(jnp.float32)
    second = other_q[kv_at][:, :DH].astype(jnp.float32)
    new_keys = jnp.where(core == 0, first, second)
    new_values = jnp.where(core == 0, second, first)
    scale = DH**-0.5
    shares = []
    for row in range(rows):
        query = q_scr[row]
        scores = scale * lax.dot_general(
            query.astype(jnp.bfloat16),
            k_ref[row],
            (((1,), (1,)), ((), ())),
            preferred_element_type=jnp.float32,
        )
        self_score = scale * jnp.sum(query * new_keys[row : row + 1], axis=1, keepdims=True)
        visible = lax.broadcasted_iota(jnp.int32, scores.shape, 1) < scalars_ref[1 + row]
        masked = jnp.where(visible, scores, jnp.float32(-1e30))
        peak = jnp.maximum(jnp.max(masked, axis=1, keepdims=True), self_score)
        raised = jnp.where(visible, jnp.exp(masked - peak), jnp.float32(0.0))
        self_raised = jnp.exp(self_score - peak)
        denominator = jnp.sum(raised, axis=1, keepdims=True) + self_raised
        weights = (raised / denominator).astype(jnp.bfloat16)
        self_weight = (self_raised / denominator).astype(jnp.bfloat16).astype(jnp.float32)
        shares.append((weights, self_weight))
    for copy in copies:
        copy.wait()
    for row, (weights, self_weight) in enumerate(shares):
        total = jnp.dot(weights, v_ref[row], preferred_element_type=jnp.float32)
        o_scr[row] = total + self_weight * new_values[row : row + 1]
    half = total_heads // 2
    for head in range(total_heads):
        ref = own_out if head < half else other_out
        column = (head % half) * DH
        ref[:, column : column + DH] = o_scr[:, head, :].astype(jnp.bfloat16)


def attend(core, lengths, own_q, other_q, parts, keys, values):
    rows, positions, _ = keys.shape
    heads = 2 * sum(part[0] for part in parts)
    out = jax.ShapeDtypeStruct((rows, heads * DH // 2), jnp.bfloat16)
    scalars = jnp.concatenate([core[None], lengths])
    return pl.pallas_call(
        functools.partial(attend_kernel, parts),
        out_shape=(out, out),
        in_specs=[SMEM] + [VMEM] * (2 * len(parts) + 1) + [HBM],
        out_specs=(VMEM, VMEM),
        scratch_shapes=[pltpu.VMEM(values.shape, values.dtype)]
        + [pltpu.VMEM((rows, heads, DH), jnp.float32)] * 2
        + [pltpu.SemaphoreType.DMA((rows,))],
        compiler_params=pltpu.CompilerParams(vmem_limit_bytes=49 * MIB),
        cost_estimate=pl.CostEstimate(
            flops=4 * rows * heads * positions * DH,
            bytes_accessed=4 * rows * positions * DH,
            transcendentals=rows * heads * positions,
        ),
        name="attend",
    )(scalars, *own_q, *other_q, keys, values)


def output_kernel(orders, rows, columns, pieces, after, ids_ref, *refs):
    count = 2 * len(orders)
    block_refs, w_refs = refs[:count], refs[count : count + len(pieces)]
    send_ref, keep_ref, xs_ref = refs[count + len(pieces) + after :]
    depth = block_refs[0].shape[1]
    me, core = ids_ref[0], ids_ref[1]
    n = len(orders[0])
    half = n // 2
    for group, (near_ref, far_ref) in enumerate(zip(block_refs[::2], block_refs[1::2])):
        for p, j in enumerate(orders[group]):
            block = jnp.bitwise_xor(me, j)
            place = block % half + jnp.where(block // half == core, half, 0)
            source = near_ref if p < half else far_ref
            at = (p % half) * rows
            xs_ref[
                pl.ds(pl.multiple_of(place * rows, rows), rows), group * depth : (group + 1) * depth
            ] = source[at : at + rows, :]
    cut = half * rows
    totals = {}
    for w_ref, ((first, tall), span) in zip(w_refs, pieces):
        part = jnp.dot(
            xs_ref[:, first : first + tall], w_ref[...], preferred_element_type=jnp.float32
        )
        totals[span] = totals[span] + part if span in totals else part
    for (column, width), total in totals.items():
        send_ref[:, column - columns[0] : column - columns[0] + width] = total[:cut]
        keep_ref[:, column - columns[0] : column - columns[0] + width] = total[cut:]


def project_out(orders, rows, ids, blocks, held, cuts, columns, after):
    chosen = [at for at, (_, (column, _)) in enumerate(cuts) if columns[0] <= column < sum(columns)]
    weights, pieces = [held[at] for at in chosen], [cuts[at] for at in chosen]
    pieces, weights = zip(*sorted(zip(pieces, weights), key=lambda pair: (pair[0][1], pair[0][0])))
    depth = len(orders) * blocks[0].shape[1]
    n = len(orders[0])
    out = jax.ShapeDtypeStruct((n * rows // 2, columns[1]), jnp.float32)
    return pl.pallas_call(
        functools.partial(output_kernel, orders, rows, columns, pieces, len(after)),
        out_shape=(out, out),
        in_specs=[SMEM] + [VMEM] * (len(blocks) + len(weights)) + [ANY] * len(after),
        out_specs=(VMEM, VMEM),
        scratch_shapes=[pltpu.VMEM((n * rows, depth), jnp.bfloat16)],
        compiler_params=pltpu.CompilerParams(vmem_limit_bytes=12 * MIB),
        cost_estimate=pl.CostEstimate(
            flops=2 * n * rows * depth * columns[1],
            bytes_accessed=2 * depth * columns[1] + 4 * n * rows * columns[1],
            transcendentals=0,
        ),
        name="project_out",
    )(ids, *blocks, *weights, *after)


def local(tokens, query_weight, kv_weight, out_weight, key_cache, value_cache, lengths):
    n = lax.axis_size("gx")
    me = lax.axis_index("gx").astype(jnp.int32)
    core = lax.axis_index("gy").astype(jnp.int32)
    ids = jnp.stack([me, core])
    own_rows = key_cache.shape[0]
    rows = 2 * own_rows
    bits = [1 << i for i in range(n.bit_length() - 1)]

    def swap(array):
        return lax.ppermute(array, "gy", [(0, 1), (1, 0)])

    def across(array, mask):
        return lax.ppermute(array, "gx", [(g, g ^ mask) for g in range(n)])

    other_tokens = swap(tokens)
    own_tokens = jnp.where(me < n, tokens, jnp.bfloat16(0))
    width = query_weight.shape[1] // 2

    y, z = bits[:1], bits[1:]
    unit = query_weight.shape[1] // 12
    plan = [(3 * unit, z[:1] + y + z[1:]), (5 * unit, y + z), (4 * unit, z + y)]
    state, first, after = [None] * len(plan), 0, []
    for group in ((2,), (0, 1)):
        chunks = [plan[i] for i in group]
        weight = kv_weight if 0 in group else None
        made = project(chunks, rows, ids, own_tokens, other_tokens, query_weight, weight, first, after)
        for i, pair in zip(group, made):
            state[i] = pair
        after = [made[0][0]]
        first += sum(columns for columns, _ in chunks)
    moving = [across(send, order[0]) for (send, _), (_, order) in zip(state, plan)]
    for step in range(len(bits)):
        for i in (2, 0, 1):
            columns, order = plan[i]
            total = state[i][1] + moving[i]
            if step + 1 < len(bits):
                cut = total.shape[0] // 2
                state[i] = (total[cut:], total[:cut])
                moving[i] = across(state[i][0], order[step + 1])
            else:
                state[i] = total
    mine, theirs = [], []
    for total in state:
        mine.append(lax.dynamic_slice_in_dim(total, core * own_rows, own_rows, 0).astype(jnp.bfloat16))
        give = lax.dynamic_slice_in_dim(total, (1 - core) * own_rows, own_rows, 0).astype(jnp.bfloat16)
        theirs.append(swap(give))

    kv_width = kv_weight.shape[1] // 2
    by_column = [i for group in ((2,), (0, 1)) for i in group]
    parts = tuple((plan[i][0] // DH, 0 if i else kv_width) for i in by_column)
    mine, theirs = [mine[i] for i in by_column], [theirs[i] for i in by_column]
    own, other = attend(core, lengths, mine, theirs, parts, key_cache, value_cache)
    got = swap(other)
    block = jnp.where(core == 0, jnp.concatenate([own, got]), jnp.concatenate([got, own]))

    near = [block[:, :width], block[:, width:]]
    far = [None, None]
    paths = [bits[::-1], bits[:1] + bits[:0:-1]]
    out_cuts, out_held = cuts_of(out_weight), []
    early = len(out_cuts) * 9 // 18
    for step in range(len(bits)):
        for i in range(2):
            if step:
                near[i] = jnp.concatenate([near[i], far[i]])
                if i == 0 and out_held:
                    near[i] = near[i] + zero.astype(jnp.bfloat16)
                if i == 1 and step + 2 >= len(bits):
                    part = out_cuts[early:] if out_held else out_cuts[:early]
                    held, zero = load([out_weight], [(0, cut) for cut in part], near, 36, width)
                    out_held += held
            far[i] = across(near[i], paths[i][step])
    orders = [order_of(path[::-1]) for path in paths]
    blocks = [b for pair in zip(near, far) for b in pair]
    total_columns = out_weight.shape[1]
    last = 768 if total_columns % 768 == 0 and total_columns > 768 else 0
    results, after = [], []
    for columns in ((0, total_columns - last), (total_columns - last, last)):
        if columns[1]:
            send, keep = project_out(orders, rows, ids, blocks, out_held, out_cuts, columns, after)
            after = [send]
            results.append((keep + swap(send)).astype(jnp.bfloat16))
    return jnp.concatenate(results, axis=1)


def solution(mesh):
    return jax.shard_map(
        local,
        mesh=mesh,
        in_specs=(
            P(("grp", "gy"), "gx"),
            P("gx", "gy"),
            P("gx", None),
            P("gy", "gx"),
            P(("grp", "gx", "gy"), None, None),
            P(("grp", "gx", "gy"), None, None),
            P(("grp", "gx", "gy")),
        ),
        out_specs=P(("grp", "gy"), "gx"),
        check_vma=False,
    )
```

```python
import functools

import jax
import jax.numpy as jnp
from jax import lax
from jax.experimental import pallas as pl
from jax.experimental.pallas import tpu as pltpu
from jax.sharding import PartitionSpec as P

H = 24
DH = 256
MIB = 1024 * 1024
HBM = pl.BlockSpec(memory_space=pltpu.HBM)
ANY = pl.BlockSpec(memory_space=pl.ANY)
VMEM = pl.BlockSpec(memory_space=pltpu.VMEM)
SMEM = pl.BlockSpec(memory_space=pltpu.SMEM)


class InOrder:
    def __init__(self, copies, ahead):
        self.copies, self.ahead = copies, ahead
        for copy in copies[:ahead]:
            copy.start()

    def wait(self, at):
        self.copies[at].wait()
        if at + self.ahead < len(self.copies):
            self.copies[at + self.ahead].start()


def order_of(bits):
    order = [0]
    for bit in reversed(bits):
        order = order + [j + bit for j in order]
    return order


def cuts_of(array):
    if len(array.shape) == 3:
        return [(at, None) for at in range(array.shape[0])]
    depth, columns = array.shape
    tall, wide = 512, (768 if columns % 768 == 0 else columns)
    return [
        ((at, tall), (column, wide)) for at in range(0, depth, tall) for column in range(0, columns, wide)
    ]


def piece_of(array, cut):
    if cut[1] is None:
        shape = array.shape[1:]
    else:
        shape = (cut[0][1], cut[1][1])
    return jax.ShapeDtypeStruct(shape, array.dtype)


def fetches(refs, cuts, targets, sems):
    copies = []
    for ref, cut in cuts:
        source = refs[ref]
        view = source.at[cut[0]] if cut[1] is None else source.at[pl.ds(*cut[0]), pl.ds(*cut[1])]
        copies.append(pltpu.make_async_copy(view, targets[len(copies)], sems.at[len(copies)]))
    return copies


def load_kernel(after, cuts, count, *refs):
    refs = refs[after:]
    in_refs, out_refs, zero_ref, sems = refs[:count], refs[count:-2], refs[-2], refs[-1]
    copies = fetches(in_refs, cuts, out_refs, sems)
    for copy in copies:
        copy.start()
    zero_ref[...] = jnp.zeros_like(zero_ref)
    for copy in copies:
        copy.wait()


def load(arrays, cuts, after, grant, zeros=128):
    shapes = [piece_of(arrays[at], cut) for at, cut in cuts]
    *held, zero = pl.pallas_call(
        functools.partial(load_kernel, len(after), cuts, len(arrays)),
        out_shape=(*shapes, jax.ShapeDtypeStruct((1, zeros), jnp.float32)),
        in_specs=[ANY] * len(after) + [HBM] * len(arrays),
        out_specs=[VMEM] * (len(cuts) + 1),
        scratch_shapes=[pltpu.SemaphoreType.DMA((len(cuts),))],
        compiler_params=pltpu.CompilerParams(vmem_limit_bytes=grant * MIB),
        cost_estimate=pl.CostEstimate(
            flops=0, bytes_accessed=sum(4 * s.shape[0] * s.shape[1] for s in shapes), transcendentals=0
        ),
        name="load",
    )(*after, *arrays)
    return held, zero


def spans_of(width):
    return [(at, min(512, width - at)) for at in range(0, width, 512)]


def project_kernel(orders, rows, first, widths, kv_width, after, ids_ref, own_ref, other_ref, w_ref, *refs):
    refs = list(refs)
    kv_ref = refs.pop(0) if kv_width else None
    outs, (xs_ref, ws_ref, w_sem) = refs[after:-3], refs[-3:]
    n = len(orders[0])
    half = n // 2
    me, core = ids_ref[0], ids_ref[1]
    features = xs_ref.shape[1]

    tiles, copies, at, source = [], [], 0, first
    depth = 768 if features % 768 == 0 else features

    def fetch(from_ref, column, width):
        for part in range(features // depth):
            span = pl.ds(part * depth, depth)
            copies.append(
                pltpu.make_async_copy(
                    from_ref.at[span, pl.ds(column, width)],
                    ws_ref.at[span, pl.ds(at, width)],
                    w_sem.at[len(copies)],
                )
            )

    for chunk, width in enumerate(widths):
        column = 0
        if kv_width and chunk == 0:
            fetch(kv_ref, pl.multiple_of(core * kv_width, kv_width), kv_width)
            tiles.append((chunk, 0, at, kv_width))
            at += kv_width
            column = kv_width
        for offset, tile in spans_of(width):
            fetch(w_ref, source, tile)
            tiles.append((chunk, column + offset, at, tile))
            at += tile
            source += tile
    per_tile = features // depth
    weights = InOrder(copies, 9)
    def place_rows(low_ref, high_ref):
        for j in range(n):
            block = jnp.bitwise_xor(me, j) % half
            source = low_ref if j < half else high_ref
            xs_ref[j * rows : (j + 1) * rows, :] = source[
                pl.ds(pl.multiple_of(block * rows, rows), rows), :
            ]

    low_mine = me // half == core

    @pl.when(low_mine)
    def _():
        place_rows(own_ref, other_ref)

    @pl.when(jnp.logical_not(low_mine))
    def _():
        place_rows(other_ref, own_ref)

    for t, (chunk, column, at, width) in enumerate(tiles):
        for part in range(per_tile):
            weights.wait(t * per_tile + part)
        total = jnp.dot(xs_ref[...], ws_ref[:, at : at + width], preferred_element_type=jnp.float32)
        span = slice(column, column + width)
        for p, j in enumerate(orders[chunk]):
            out = outs[2 * chunk + 1] if p < half else outs[2 * chunk]
            out[(p % half) * rows : (p % half + 1) * rows, span] = total[j * rows : (j + 1) * rows]


def project(plan, rows, ids, tokens, other, query_weight, kv_weight, first, after):
    features = tokens.shape[1]
    orders = [order_of(bits) for _, bits in plan]
    widths = [width for width, _ in plan]
    n = len(orders[0])
    kv_width = kv_weight.shape[1] // 2 if kv_weight is not None else 0
    columns = sum(widths) + kv_width
    outs = []
    for chunk, width in enumerate(widths):
        shape = (n * rows // 2, width + (0 if chunk else kv_width))
        outs += [jax.ShapeDtypeStruct(shape, jnp.float32)] * 2
    weights = [query_weight] + ([kv_weight] if kv_width else [])
    parts = features // 768 if features % 768 == 0 else 1
    copies = parts * (len(weights) - 1 + sum(len(spans_of(width)) for width in widths))
    outs = pl.pallas_call(
        functools.partial(project_kernel, orders, rows, first, widths, kv_width, len(after)),
        out_shape=outs,
        in_specs=[SMEM, VMEM, VMEM] + [HBM] * len(weights) + [ANY] * len(after),
        out_specs=[VMEM] * len(outs),
        scratch_shapes=[
            pltpu.VMEM((n * rows, features), tokens.dtype),
            pltpu.VMEM((features, columns), tokens.dtype),
            pltpu.SemaphoreType.DMA((copies,)),
        ],
        compiler_params=pltpu.CompilerParams(vmem_limit_bytes=46 * MIB),
        cost_estimate=pl.CostEstimate(
            flops=2 * n * rows * features * columns,
            bytes_accessed=2 * features * columns + 4 * n * rows * columns,
            transcendentals=0,
        ),
        name="project",
    )(ids, tokens, other, *weights, *after)
    return list(zip(outs[::2], outs[1::2]))


def attend_kernel(parts, scalars_ref, *refs):
    own_q, other_q = refs[: len(parts)], refs[len(parts) : 2 * len(parts)]
    k_ref, v_hbm, own_out, other_out, v_ref, q_scr, o_scr, sems = refs[2 * len(parts) :]
    core = scalars_ref[0]
    rows, positions, _ = k_ref.shape
    copies = [pltpu.make_async_copy(v_hbm.at[row], v_ref.at[row], sems.at[row]) for row in range(rows)]
    for copy in copies:
        copy.start()
    at = 0
    for side in (own_q, other_q):
        for ref, (heads, skip) in zip(side, parts):
            for head in range(heads):
                column = skip + head * DH
                q_scr[:, at, :] = ref[:, column : column + DH].astype(jnp.float32)
                at += 1
    total_heads = at
    kv_at = [skip > 0 for _, skip in parts].index(True)
    first = own_q[kv_at][:, :DH].astype(jnp.float32)
    second = other_q[kv_at][:, :DH].astype(jnp.float32)
    new_keys = jnp.where(core == 0, first, second)
    new_values = jnp.where(core == 0, second, first)
    scale = DH**-0.5
    shares = []
    for row in range(rows):
        query = q_scr[row]
        scores = scale * lax.dot_general(
            query.astype(jnp.bfloat16),
            k_ref[row],
            (((1,), (1,)), ((), ())),
            preferred_element_type=jnp.float32,
        )
        self_score = scale * jnp.sum(query * new_keys[row : row + 1], axis=1, keepdims=True)
        visible = lax.broadcasted_iota(jnp.int32, scores.shape, 1) < scalars_ref[1 + row]
        masked = jnp.where(visible, scores, jnp.float32(-1e30))
        peak = jnp.maximum(jnp.max(masked, axis=1, keepdims=True), self_score)
        raised = jnp.where(visible, jnp.exp(masked - peak), jnp.float32(0.0))
        self_raised = jnp.exp(self_score - peak)
        denominator = jnp.sum(raised, axis=1, keepdims=True) + self_raised
        weights = (raised / denominator).astype(jnp.bfloat16)
        self_weight = (self_raised / denominator).astype(jnp.bfloat16).astype(jnp.float32)
        shares.append((weights, self_weight))
    for copy in copies:
        copy.wait()
    for row, (weights, self_weight) in enumerate(shares):
        total = jnp.dot(weights, v_ref[row], preferred_element_type=jnp.float32)
        o_scr[row] = total + self_weight * new_values[row : row + 1]
    half = total_heads // 2
    for head in range(total_heads):
        ref = own_out if head < half else other_out
        column = (head % half) * DH
        ref[:, column : column + DH] = o_scr[:, head, :].astype(jnp.bfloat16)


def attend(core, lengths, own_q, other_q, parts, keys, values):
    rows, positions, _ = keys.shape
    heads = 2 * sum(part[0] for part in parts)
    out = jax.ShapeDtypeStruct((rows, heads * DH // 2), jnp.bfloat16)
    scalars = jnp.concatenate([core[None], lengths])
    return pl.pallas_call(
        functools.partial(attend_kernel, parts),
        out_shape=(out, out),
        in_specs=[SMEM] + [VMEM] * (2 * len(parts) + 1) + [HBM],
        out_specs=(VMEM, VMEM),
        scratch_shapes=[pltpu.VMEM(values.shape, values.dtype)]
        + [pltpu.VMEM((rows, heads, DH), jnp.float32)] * 2
        + [pltpu.SemaphoreType.DMA((rows,))],
        compiler_params=pltpu.CompilerParams(vmem_limit_bytes=49 * MIB),
        cost_estimate=pl.CostEstimate(
            flops=4 * rows * heads * positions * DH,
            bytes_accessed=4 * rows * positions * DH,
            transcendentals=rows * heads * positions,
        ),
        name="attend",
    )(scalars, *own_q, *other_q, keys, values)


def output_kernel(orders, rows, columns, pieces, after, ids_ref, *refs):
    count = 2 * len(orders)
    block_refs, w_refs = refs[:count], refs[count : count + len(pieces)]
    send_ref, keep_ref, xs_ref = refs[count + len(pieces) + after :]
    depth = block_refs[0].shape[1]
    me, core = ids_ref[0], ids_ref[1]
    n = len(orders[0])
    half = n // 2
    for group, (near_ref, far_ref) in enumerate(zip(block_refs[::2], block_refs[1::2])):
        for p, j in enumerate(orders[group]):
            block = jnp.bitwise_xor(me, j)
            place = block % half + jnp.where(block // half == core, half, 0)
            source = near_ref if p < half else far_ref
            at = (p % half) * rows
            xs_ref[
                pl.ds(pl.multiple_of(place * rows, rows), rows), group * depth : (group + 1) * depth
            ] = source[at : at + rows, :]
    cut = half * rows
    totals = {}
    for w_ref, ((first, tall), span) in zip(w_refs, pieces):
        part = jnp.dot(
            xs_ref[:, first : first + tall], w_ref[...], preferred_element_type=jnp.float32
        )
        totals[span] = totals[span] + part if span in totals else part
    for (column, width), total in totals.items():
        send_ref[:, column - columns[0] : column - columns[0] + width] = total[:cut]
        keep_ref[:, column - columns[0] : column - columns[0] + width] = total[cut:]


def project_out(orders, rows, ids, blocks, held, cuts, columns, after):
    chosen = [at for at, (_, (column, _)) in enumerate(cuts) if columns[0] <= column < sum(columns)]
    weights, pieces = [held[at] for at in chosen], [cuts[at] for at in chosen]
    pieces, weights = zip(*sorted(zip(pieces, weights), key=lambda pair: (pair[0][1], pair[0][0])))
    depth = len(orders) * blocks[0].shape[1]
    n = len(orders[0])
    out = jax.ShapeDtypeStruct((n * rows // 2, columns[1]), jnp.float32)
    return pl.pallas_call(
        functools.partial(output_kernel, orders, rows, columns, pieces, len(after)),
        out_shape=(out, out),
        in_specs=[SMEM] + [VMEM] * (len(blocks) + len(weights)) + [ANY] * len(after),
        out_specs=(VMEM, VMEM),
        scratch_shapes=[pltpu.VMEM((n * rows, depth), jnp.bfloat16)],
        compiler_params=pltpu.CompilerParams(vmem_limit_bytes=12 * MIB),
        cost_estimate=pl.CostEstimate(
            flops=2 * n * rows * depth * columns[1],
            bytes_accessed=2 * depth * columns[1] + 4 * n * rows * columns[1],
            transcendentals=0,
        ),
        name="project_out",
    )(ids, *blocks, *weights, *after)


def local(tokens, query_weight, kv_weight, out_weight, key_cache, value_cache, lengths):
    n = lax.axis_size("gx")
    me = lax.axis_index("gx").astype(jnp.int32)
    core = lax.axis_index("gy").astype(jnp.int32)
    ids = jnp.stack([me, core])
    own_rows = key_cache.shape[0]
    rows = 2 * own_rows
    bits = [1 << i for i in range(n.bit_length() - 1)]

    def swap(array):
        return lax.ppermute(array, "gy", [(0, 1), (1, 0)])

    def across(array, mask):
        return lax.ppermute(array, "gx", [(g, g ^ mask) for g in range(n)])

    other_tokens = swap(tokens)
    own_tokens = jnp.where(me < n, tokens, jnp.bfloat16(0))
    width = query_weight.shape[1] // 2

    y, z = bits[:1], bits[1:]
    unit = query_weight.shape[1] // 12
    plan = [(3 * unit, z[:1] + y + z[1:]), (5 * unit, y + z), (4 * unit, z + y)]
    state, first, after = [None] * len(plan), 0, []
    for group in ((2,), (0, 1)):
        chunks = [plan[i] for i in group]
        weight = kv_weight if 0 in group else None
        made = project(chunks, rows, ids, own_tokens, other_tokens, query_weight, weight, first, after)
        for i, pair in zip(group, made):
            state[i] = pair
        after = [made[0][0]]
        first += sum(columns for columns, _ in chunks)
    moving = [across(send, order[0]) for (send, _), (_, order) in zip(state, plan)]
    for step in range(len(bits)):
        for i in (2, 0, 1):
            columns, order = plan[i]
            total = state[i][1] + moving[i]
            if step + 1 < len(bits):
                cut = total.shape[0] // 2
                state[i] = (total[cut:], total[:cut])
                moving[i] = across(state[i][0], order[step + 1])
            else:
                state[i] = total
    mine, theirs = [], []
    for total in state:
        mine.append(lax.dynamic_slice_in_dim(total, core * own_rows, own_rows, 0).astype(jnp.bfloat16))
        give = lax.dynamic_slice_in_dim(total, (1 - core) * own_rows, own_rows, 0).astype(jnp.bfloat16)
        theirs.append(swap(give))

    kv_width = kv_weight.shape[1] // 2
    by_column = [i for group in ((2,), (0, 1)) for i in group]
    parts = tuple((plan[i][0] // DH, 0 if i else kv_width) for i in by_column)
    mine, theirs = [mine[i] for i in by_column], [theirs[i] for i in by_column]
    own, other = attend(core, lengths, mine, theirs, parts, key_cache, value_cache)
    got = swap(other)
    block = jnp.where(core == 0, jnp.concatenate([own, got]), jnp.concatenate([got, own]))

    near = [block[:, :width], block[:, width:]]
    far = [None, None]
    paths = [bits[::-1], bits[:1] + bits[:0:-1]]
    out_cuts, out_held = cuts_of(out_weight), []
    early = len(out_cuts) * 9 // 18
    for step in range(len(bits)):
        for i in range(2):
            if step:
                near[i] = jnp.concatenate([near[i], far[i]])
                if i == 0 and out_held:
                    near[i] = near[i] + zero.astype(jnp.bfloat16)
                if i == 1 and step + 2 >= len(bits):
                    part = out_cuts[early:] if out_held else out_cuts[:early]
                    held, zero = load([out_weight], [(0, cut) for cut in part], near, 36, width)
                    out_held += held
            far[i] = across(near[i], paths[i][step])
    orders = [order_of(path[::-1]) for path in paths]
    blocks = [b for pair in zip(near, far) for b in pair]
    total_columns = out_weight.shape[1]
    last = 768 if total_columns % 768 == 0 and total_columns > 768 else 0
    results, after = [], []
    for columns in ((0, total_columns - last), (total_columns - last, last)):
        if columns[1]:
            send, keep = project_out(orders, rows, ids, blocks, out_held, out_cuts, columns, after)
            after = [send]
            results.append((keep + swap(send)).astype(jnp.bfloat16))
    return jnp.concatenate(results, axis=1)


def solution(mesh):
    return jax.shard_map(
        local,
        mesh=mesh,
        in_specs=(
            P(("grp", "gy"), "gx"),
            P("gx", "gy"),
            P("gx", None),
            P("gy", "gx"),
            P(("grp", "gx", "gy"), None, None),
            P(("grp", "gx", "gy"), None, None),
            P(("grp", "gx", "gy")),
        ),
        out_specs=P(("grp", "gy"), "gx"),
        check_vma=False,
    )
```

```python
import functools

import jax
import jax.numpy as jnp
from jax import lax
from jax.experimental import pallas as pl
from jax.experimental.pallas import tpu as pltpu
from jax.sharding import PartitionSpec as P

H = 24
DH = 256
MIB = 1024 * 1024
HBM = pl.BlockSpec(memory_space=pltpu.HBM)
ANY = pl.BlockSpec(memory_space=pl.ANY)
VMEM = pl.BlockSpec(memory_space=pltpu.VMEM)
SMEM = pl.BlockSpec(memory_space=pltpu.SMEM)


class InOrder:
    def __init__(self, copies, ahead):
        self.copies, self.ahead = copies, ahead
        for copy in copies[:ahead]:
            copy.start()

    def wait(self, at):
        self.copies[at].wait()
        if at + self.ahead < len(self.copies):
            self.copies[at + self.ahead].start()


def order_of(bits):
    order = [0]
    for bit in reversed(bits):
        order = order + [j + bit for j in order]
    return order


def cuts_of(array):
    if len(array.shape) == 3:
        return [(at, None) for at in range(array.shape[0])]
    depth, columns = array.shape
    tall, wide = 512, (768 if columns % 768 == 0 else columns)
    return [
        ((at, tall), (column, wide)) for at in range(0, depth, tall) for column in range(0, columns, wide)
    ]


def piece_of(array, cut):
    if cut[1] is None:
        shape = array.shape[1:]
    else:
        shape = (cut[0][1], cut[1][1])
    return jax.ShapeDtypeStruct(shape, array.dtype)


def fetches(refs, cuts, targets, sems):
    copies = []
    for ref, cut in cuts:
        source = refs[ref]
        view = source.at[cut[0]] if cut[1] is None else source.at[pl.ds(*cut[0]), pl.ds(*cut[1])]
        copies.append(pltpu.make_async_copy(view, targets[len(copies)], sems.at[len(copies)]))
    return copies


def load_kernel(after, cuts, count, *refs):
    refs = refs[after:]
    in_refs, out_refs, zero_ref, sems = refs[:count], refs[count:-2], refs[-2], refs[-1]
    copies = fetches(in_refs, cuts, out_refs, sems)
    for copy in copies:
        copy.start()
    zero_ref[...] = jnp.zeros_like(zero_ref)
    for copy in copies:
        copy.wait()


def load(arrays, cuts, after, grant, zeros=128):
    shapes = [piece_of(arrays[at], cut) for at, cut in cuts]
    *held, zero = pl.pallas_call(
        functools.partial(load_kernel, len(after), cuts, len(arrays)),
        out_shape=(*shapes, jax.ShapeDtypeStruct((1, zeros), jnp.float32)),
        in_specs=[ANY] * len(after) + [HBM] * len(arrays),
        out_specs=[VMEM] * (len(cuts) + 1),
        scratch_shapes=[pltpu.SemaphoreType.DMA((len(cuts),))],
        compiler_params=pltpu.CompilerParams(vmem_limit_bytes=grant * MIB),
        cost_estimate=pl.CostEstimate(
            flops=0, bytes_accessed=sum(4 * s.shape[0] * s.shape[1] for s in shapes), transcendentals=0
        ),
        name="load",
    )(*after, *arrays)
    return held, zero


def spans_of(width):
    return [(at, min(512, width - at)) for at in range(0, width, 512)]


def project_kernel(orders, rows, first, widths, kv_width, after, ids_ref, own_ref, other_ref, w_ref, *refs):
    refs = list(refs)
    kv_ref = refs.pop(0) if kv_width else None
    outs, (xs_ref, ws_ref, w_sem) = refs[after:-3], refs[-3:]
    n = len(orders[0])
    half = n // 2
    me, core = ids_ref[0], ids_ref[1]
    features = xs_ref.shape[1]

    tiles, copies, at, source = [], [], 0, first
    depth = 768 if features % 768 == 0 else features

    def fetch(from_ref, column, width):
        for part in range(features // depth):
            span = pl.ds(part * depth, depth)
            copies.append(
                pltpu.make_async_copy(
                    from_ref.at[span, pl.ds(column, width)],
                    ws_ref.at[span, pl.ds(at, width)],
                    w_sem.at[len(copies)],
                )
            )

    for chunk, width in enumerate(widths):
        column = 0
        if kv_width and chunk == 0:
            fetch(kv_ref, pl.multiple_of(core * kv_width, kv_width), kv_width)
            tiles.append((chunk, 0, at, kv_width))
            at += kv_width
            column = kv_width
        for offset, tile in spans_of(width):
            fetch(w_ref, source, tile)
            tiles.append((chunk, column + offset, at, tile))
            at += tile
            source += tile
    per_tile = features // depth
    weights = InOrder(copies, 9)
    def place_rows(low_ref, high_ref):
        for j in range(n):
            block = jnp.bitwise_xor(me, j) % half
            source = low_ref if j < half else high_ref
            xs_ref[j * rows : (j + 1) * rows, :] = source[
                pl.ds(pl.multiple_of(block * rows, rows), rows), :
            ]

    low_mine = me // half == core

    @pl.when(low_mine)
    def _():
        place_rows(own_ref, other_ref)

    @pl.when(jnp.logical_not(low_mine))
    def _():
        place_rows(other_ref, own_ref)

    for t, (chunk, column, at, width) in enumerate(tiles):
        for part in range(per_tile):
            weights.wait(t * per_tile + part)
        total = jnp.dot(xs_ref[...], ws_ref[:, at : at + width], preferred_element_type=jnp.float32)
        span = slice(column, column + width)
        for p, j in enumerate(orders[chunk]):
            out = outs[2 * chunk + 1] if p < half else outs[2 * chunk]
            out[(p % half) * rows : (p % half + 1) * rows, span] = total[j * rows : (j + 1) * rows]


def project(plan, rows, ids, tokens, other, query_weight, kv_weight, first, after):
    features = tokens.shape[1]
    orders = [order_of(bits) for _, bits in plan]
    widths = [width for width, _ in plan]
    n = len(orders[0])
    kv_width = kv_weight.shape[1] // 2 if kv_weight is not None else 0
    columns = sum(widths) + kv_width
    outs = []
    for chunk, width in enumerate(widths):
        shape = (n * rows // 2, width + (0 if chunk else kv_width))
        outs += [jax.ShapeDtypeStruct(shape, jnp.float32)] * 2
    weights = [query_weight] + ([kv_weight] if kv_width else [])
    parts = features // 768 if features % 768 == 0 else 1
    copies = parts * (len(weights) - 1 + sum(len(spans_of(width)) for width in widths))
    outs = pl.pallas_call(
        functools.partial(project_kernel, orders, rows, first, widths, kv_width, len(after)),
        out_shape=outs,
        in_specs=[SMEM, VMEM, VMEM] + [HBM] * len(weights) + [ANY] * len(after),
        out_specs=[VMEM] * len(outs),
        scratch_shapes=[
            pltpu.VMEM((n * rows, features), tokens.dtype),
            pltpu.VMEM((features, columns), tokens.dtype),
            pltpu.SemaphoreType.DMA((copies,)),
        ],
        compiler_params=pltpu.CompilerParams(vmem_limit_bytes=46 * MIB),
        cost_estimate=pl.CostEstimate(
            flops=2 * n * rows * features * columns,
            bytes_accessed=2 * features * columns + 4 * n * rows * columns,
            transcendentals=0,
        ),
        name="project",
    )(ids, tokens, other, *weights, *after)
    return list(zip(outs[::2], outs[1::2]))


def attend_kernel(parts, scalars_ref, *refs):
    own_q, other_q = refs[: len(parts)], refs[len(parts) : 2 * len(parts)]
    k_ref, v_hbm, own_out, other_out, v_ref, q_scr, o_scr, sems = refs[2 * len(parts) :]
    core = scalars_ref[0]
    rows, positions, _ = k_ref.shape
    copies = [pltpu.make_async_copy(v_hbm.at[row], v_ref.at[row], sems.at[row]) for row in range(rows)]
    for copy in copies:
        copy.start()
    at = 0
    for side in (own_q, other_q):
        for ref, (heads, skip) in zip(side, parts):
            for head in range(heads):
                column = skip + head * DH
                q_scr[:, at, :] = ref[:, column : column + DH].astype(jnp.float32)
                at += 1
    total_heads = at
    kv_at = [skip > 0 for _, skip in parts].index(True)
    first = own_q[kv_at][:, :DH].astype(jnp.float32)
    second = other_q[kv_at][:, :DH].astype(jnp.float32)
    new_keys = jnp.where(core == 0, first, second)
    new_values = jnp.where(core == 0, second, first)
    scale = DH**-0.5
    shares = []
    for row in range(rows):
        query = q_scr[row]
        scores = scale * lax.dot_general(
            query.astype(jnp.bfloat16),
            k_ref[row],
            (((1,), (1,)), ((), ())),
            preferred_element_type=jnp.float32,
        )
        self_score = scale * jnp.sum(query * new_keys[row : row + 1], axis=1, keepdims=True)
        visible = lax.broadcasted_iota(jnp.int32, scores.shape, 1) < scalars_ref[1 + row]
        masked = jnp.where(visible, scores, jnp.float32(-1e30))
        peak = jnp.maximum(jnp.max(masked, axis=1, keepdims=True), self_score)
        raised = jnp.where(visible, jnp.exp(masked - peak), jnp.float32(0.0))
        self_raised = jnp.exp(self_score - peak)
        denominator = jnp.sum(raised, axis=1, keepdims=True) + self_raised
        weights = (raised / denominator).astype(jnp.bfloat16)
        self_weight = (self_raised / denominator).astype(jnp.bfloat16).astype(jnp.float32)
        shares.append((weights, self_weight))
    for copy in copies:
        copy.wait()
    for row, (weights, self_weight) in enumerate(shares):
        total = jnp.dot(weights, v_ref[row], preferred_element_type=jnp.float32)
        o_scr[row] = total + self_weight * new_values[row : row + 1]
    half = total_heads // 2
    for head in range(total_heads):
        ref = own_out if head < half else other_out
        column = (head % half) * DH
        ref[:, column : column + DH] = o_scr[:, head, :].astype(jnp.bfloat16)


def attend(core, lengths, own_q, other_q, parts, keys, values):
    rows, positions, _ = keys.shape
    heads = 2 * sum(part[0] for part in parts)
    out = jax.ShapeDtypeStruct((rows, heads * DH // 2), jnp.bfloat16)
    scalars = jnp.concatenate([core[None], lengths])
    return pl.pallas_call(
        functools.partial(attend_kernel, parts),
        out_shape=(out, out),
        in_specs=[SMEM] + [VMEM] * (2 * len(parts) + 1) + [HBM],
        out_specs=(VMEM, VMEM),
        scratch_shapes=[pltpu.VMEM(values.shape, values.dtype)]
        + [pltpu.VMEM((rows, heads, DH), jnp.float32)] * 2
        + [pltpu.SemaphoreType.DMA((rows,))],
        compiler_params=pltpu.CompilerParams(vmem_limit_bytes=49 * MIB),
        cost_estimate=pl.CostEstimate(
            flops=4 * rows * heads * positions * DH,
            bytes_accessed=4 * rows * positions * DH,
            transcendentals=rows * heads * positions,
        ),
        name="attend",
    )(scalars, *own_q, *other_q, keys, values)


def output_kernel(layout, rows, pieces, ahead, ids_ref, *refs):
    block_refs, refs = refs[: len(layout)], refs[len(layout) :]
    w_refs, refs = refs[: len(pieces)], refs[len(pieces) :]
    w_hbm, refs = refs[: bool(ahead)], refs[bool(ahead) :]
    send_ref, keep_ref, next_refs, (xs_ref, sems) = refs[0], refs[1], refs[2:-2], refs[-2:]
    copies = fetches(w_hbm, [(0, cut) for cut in ahead], next_refs, sems)
    for copy in copies:
        copy.start()
    me, core = ids_ref[0], ids_ref[1]
    depth = block_refs[0].shape[1]
    half = xs_ref.shape[0] // rows // 2
    for ref, (group, places) in zip(block_refs, layout):
        for at, j in enumerate(places):
            block = jnp.bitwise_xor(me, j)
            place = block % half + jnp.where(block // half == core, half, 0)
            xs_ref[
                pl.ds(pl.multiple_of(place * rows, rows), rows), group * depth : (group + 1) * depth
            ] = ref[at * rows : (at + 1) * rows, :]
    cut = half * rows
    totals = {}
    for w_ref, ((first, tall), span) in zip(w_refs, pieces):
        part = jnp.dot(
            xs_ref[:, first : first + tall], w_ref[...], preferred_element_type=jnp.float32
        )
        totals[span] = totals[span] + part if span in totals else part
    base = min(column for column, _ in totals)
    for (column, width), total in totals.items():
        send_ref[:, column - base : column - base + width] = total[:cut]
        keep_ref[:, column - base : column - base + width] = total[cut:]
    for copy in copies:
        copy.wait()


def project_out(rows, ids, blocks, held, cuts, out_weight, ahead):
    chosen = sorted(range(len(cuts)), key=lambda at: (cuts[at][1], cuts[at][0]))
    pieces, weights = [cuts[at] for at in chosen], [held[at] for at in chosen]
    layout = [(group, tuple(places)) for group, arrays in enumerate(blocks) for _, places in arrays]
    arrays = [array for group in blocks for array, _ in group]
    depth = out_weight.shape[0]
    columns = sum(dict.fromkeys(span for _, span in pieces), ())[1::2]
    total_rows = rows * sum(len(places) for _, places in layout) // len(blocks)
    out = jax.ShapeDtypeStruct((total_rows // 2, sum(columns)), jnp.float32)
    return pl.pallas_call(
        functools.partial(output_kernel, layout, rows, pieces, ahead),
        out_shape=[out, out] + [piece_of(out_weight, cut) for cut in ahead],
        in_specs=[SMEM] + [VMEM] * (len(arrays) + len(weights)) + [HBM] * bool(ahead),
        out_specs=[VMEM] * (2 + len(ahead)),
        scratch_shapes=[
            pltpu.VMEM((total_rows, depth), jnp.bfloat16),
            pltpu.SemaphoreType.DMA((max(1, len(ahead)),)),
        ],
        compiler_params=pltpu.CompilerParams(vmem_limit_bytes=34 * MIB),
        cost_estimate=pl.CostEstimate(
            flops=2 * total_rows * depth * sum(columns),
            bytes_accessed=2 * depth * sum(columns) + 4 * total_rows * sum(columns),
            transcendentals=0,
        ),
        name="project_out",
    )(ids, *arrays, *weights, *([out_weight] if ahead else []))


def local(tokens, query_weight, kv_weight, out_weight, key_cache, value_cache, lengths):
    n = lax.axis_size("gx")
    me = lax.axis_index("gx").astype(jnp.int32)
    core = lax.axis_index("gy").astype(jnp.int32)
    ids = jnp.stack([me, core])
    own_rows = key_cache.shape[0]
    rows = 2 * own_rows
    bits = [1 << i for i in range(n.bit_length() - 1)]

    def swap(array):
        return lax.ppermute(array, "gy", [(0, 1), (1, 0)])

    def across(array, mask):
        return lax.ppermute(array, "gx", [(g, g ^ mask) for g in range(n)])

    other_tokens = swap(tokens)
    own_tokens = jnp.where(me < n, tokens, jnp.bfloat16(0))
    width = query_weight.shape[1] // 2

    y, z = bits[:1], bits[1:]
    unit = query_weight.shape[1] // 12
    plan = [(3 * unit, z[:1] + y + z[1:]), (5 * unit, y + z), (4 * unit, z + y)]
    state, first, after = [None] * len(plan), 0, []
    for group in ((2,), (0, 1)):
        chunks = [plan[i] for i in group]
        weight = kv_weight if 0 in group else None
        made = project(chunks, rows, ids, own_tokens, other_tokens, query_weight, weight, first, after)
        for i, pair in zip(group, made):
            state[i] = pair
        after = [made[0][0]]
        first += sum(columns for columns, _ in chunks)
    moving = [across(send, order[0]) for (send, _), (_, order) in zip(state, plan)]
    second = None
    for step in range(len(bits)):
        for i in (2, 0, 1):
            columns, order = plan[i]
            total = state[i][1] + moving[i]
            if i == 0 and step == 2 and len(bits) == 3:
                total = total + 0.0 * second[:1, : total.shape[1]]
            if i == 1 and step == 1:
                second = total
            if step + 1 < len(bits):
                cut = total.shape[0] // 2
                state[i] = (total[cut:], total[:cut])
                moving[i] = across(state[i][0], order[step + 1])
            else:
                state[i] = total
    mine, theirs = [], []
    for total in state:
        mine.append(lax.dynamic_slice_in_dim(total, core * own_rows, own_rows, 0).astype(jnp.bfloat16))
        give = lax.dynamic_slice_in_dim(total, (1 - core) * own_rows, own_rows, 0).astype(jnp.bfloat16)
        theirs.append(swap(give))

    kv_width = kv_weight.shape[1] // 2
    by_column = [i for group in ((2,), (0, 1)) for i in group]
    parts = tuple((plan[i][0] // DH, 0 if i else kv_width) for i in by_column)
    mine, theirs = [mine[i] for i in by_column], [theirs[i] for i in by_column]
    own, other = attend(core, lengths, mine, theirs, parts, key_cache, value_cache)
    got = swap(other)
    block = jnp.where(core == 0, jnp.concatenate([own, got]), jnp.concatenate([got, own]))

    def along_z(array):
        return [array] + [across(array, 2 * m) for m in range(1, n // 2)]

    first, second = block[:, :width], block[:, width:]
    pair = jnp.concatenate([second, across(second, 1)])
    near = jnp.concatenate(along_z(first)) + jnp.bfloat16(0) * pair[-1:]
    blocks = [[(near, range(0, n, 2)), (across(near, 1), range(1, n, 2))]]
    blocks.append([(array, (2 * m, 2 * m + 1)) for m, array in enumerate(along_z(pair))])

    total_columns = out_weight.shape[1]
    last = 768 if total_columns % 768 == 0 and total_columns > 768 else 0
    out_cuts = cuts_of(out_weight)
    early = [cut for cut in out_cuts if cut[1][0] < total_columns - last]
    late = [cut for cut in out_cuts if cut[1][0] >= total_columns - last]
    held, _ = load([out_weight], [(0, cut) for cut in early], [near], 40)
    send, keep, *held = project_out(rows, ids, blocks, held, early, out_weight, late)
    results = [(keep, swap(send))]
    if late:
        send, keep = project_out(rows, ids, blocks, held, late, out_weight, [])
        results.append((keep, swap(send)))
    return jnp.concatenate([(keep + got).astype(jnp.bfloat16) for keep, got in results], axis=1)


def solution(mesh):
    return jax.shard_map(
        local,
        mesh=mesh,
        in_specs=(
            P(("grp", "gy"), "gx"),
            P("gx", "gy"),
            P("gx", None),
            P("gy", "gx"),
            P(("grp", "gx", "gy"), None, None),
            P(("grp", "gx", "gy"), None, None),
            P(("grp", "gx", "gy")),
        ),
        out_specs=P(("grp", "gy"), "gx"),
        check_vma=False,
    )
```

```python
import functools

import jax
import jax.numpy as jnp
from jax import lax
from jax.experimental import pallas as pl
from jax.experimental.pallas import tpu as pltpu
from jax.sharding import PartitionSpec as P

H = 24
DH = 256
MIB = 1024 * 1024
HBM = pl.BlockSpec(memory_space=pltpu.HBM)
ANY = pl.BlockSpec(memory_space=pl.ANY)
VMEM = pl.BlockSpec(memory_space=pltpu.VMEM)
SMEM = pl.BlockSpec(memory_space=pltpu.SMEM)


class InOrder:
    def __init__(self, copies, ahead):
        self.copies, self.ahead = copies, ahead
        for copy in copies[:ahead]:
            copy.start()

    def wait(self, at):
        self.copies[at].wait()
        if at + self.ahead < len(self.copies):
            self.copies[at + self.ahead].start()


def order_of(bits):
    order = [0]
    for bit in reversed(bits):
        order = order + [j + bit for j in order]
    return order


def cuts_of(array):
    if len(array.shape) == 3:
        return [(at, None) for at in range(array.shape[0])]
    depth, columns = array.shape
    tall, wide = 512, (768 if columns % 768 == 0 else columns)
    return [
        ((at, tall), (column, wide)) for at in range(0, depth, tall) for column in range(0, columns, wide)
    ]


def piece_of(array, cut):
    if cut[1] is None:
        shape = array.shape[1:]
    else:
        shape = (cut[0][1], cut[1][1])
    return jax.ShapeDtypeStruct(shape, array.dtype)


def fetches(refs, cuts, targets, sems):
    copies = []
    for ref, cut in cuts:
        source = refs[ref]
        view = source.at[cut[0]] if cut[1] is None else source.at[pl.ds(*cut[0]), pl.ds(*cut[1])]
        copies.append(pltpu.make_async_copy(view, targets[len(copies)], sems.at[len(copies)]))
    return copies


def load_kernel(after, cuts, count, *refs):
    refs = refs[after:]
    in_refs, out_refs, zero_ref, sems = refs[:count], refs[count:-2], refs[-2], refs[-1]
    copies = fetches(in_refs, cuts, out_refs, sems)
    for copy in copies:
        copy.start()
    zero_ref[...] = jnp.zeros_like(zero_ref)
    for copy in copies:
        copy.wait()


def load(arrays, cuts, after, grant, zeros=128):
    shapes = [piece_of(arrays[at], cut) for at, cut in cuts]
    *held, zero = pl.pallas_call(
        functools.partial(load_kernel, len(after), cuts, len(arrays)),
        out_shape=(*shapes, jax.ShapeDtypeStruct((1, zeros), jnp.float32)),
        in_specs=[ANY] * len(after) + [HBM] * len(arrays),
        out_specs=[VMEM] * (len(cuts) + 1),
        scratch_shapes=[pltpu.SemaphoreType.DMA((len(cuts),))],
        compiler_params=pltpu.CompilerParams(vmem_limit_bytes=grant * MIB),
        cost_estimate=pl.CostEstimate(
            flops=0, bytes_accessed=sum(4 * s.shape[0] * s.shape[1] for s in shapes), transcendentals=0
        ),
        name="load",
    )(*after, *arrays)
    return held, zero


def spans_of(width):
    return [(at, min(512, width - at)) for at in range(0, width, 512)]


def project_kernel(orders, rows, first, widths, kv_width, after, ids_ref, own_ref, other_ref, w_ref, *refs):
    refs = list(refs)
    kv_ref = refs.pop(0) if kv_width else None
    outs, (xs_ref, ws_ref, w_sem) = refs[after:-3], refs[-3:]
    n = len(orders[0])
    half = n // 2
    me, core = ids_ref[0], ids_ref[1]
    features = xs_ref.shape[1]

    tiles, copies, at, source = [], [], 0, first
    depth = 768 if features % 768 == 0 else features

    def fetch(from_ref, column, width):
        for part in range(features // depth):
            span = pl.ds(part * depth, depth)
            copies.append(
                pltpu.make_async_copy(
                    from_ref.at[span, pl.ds(column, width)],
                    ws_ref.at[span, pl.ds(at, width)],
                    w_sem.at[len(copies)],
                )
            )

    for chunk, width in enumerate(widths):
        column = 0
        if kv_width and chunk == 0:
            fetch(kv_ref, pl.multiple_of(core * kv_width, kv_width), kv_width)
            tiles.append((chunk, 0, at, kv_width))
            at += kv_width
            column = kv_width
        for offset, tile in spans_of(width):
            fetch(w_ref, source, tile)
            tiles.append((chunk, column + offset, at, tile))
            at += tile
            source += tile
    per_tile = features // depth
    weights = InOrder(copies, 9)
    def place_rows(low_ref, high_ref):
        for j in range(n):
            block = jnp.bitwise_xor(me, j) % half
            source = low_ref if j < half else high_ref
            xs_ref[j * rows : (j + 1) * rows, :] = source[
                pl.ds(pl.multiple_of(block * rows, rows), rows), :
            ]

    low_mine = me // half == core

    @pl.when(low_mine)
    def _():
        place_rows(own_ref, other_ref)

    @pl.when(jnp.logical_not(low_mine))
    def _():
        place_rows(other_ref, own_ref)

    for t, (chunk, column, at, width) in enumerate(tiles):
        for part in range(per_tile):
            weights.wait(t * per_tile + part)
        total = jnp.dot(xs_ref[...], ws_ref[:, at : at + width], preferred_element_type=jnp.float32)
        span = slice(column, column + width)
        for p, j in enumerate(orders[chunk]):
            out = outs[2 * chunk + 1] if p < half else outs[2 * chunk]
            out[(p % half) * rows : (p % half + 1) * rows, span] = total[j * rows : (j + 1) * rows]


def project(plan, rows, ids, tokens, other, query_weight, kv_weight, first, after):
    features = tokens.shape[1]
    orders = [order_of(bits) for _, bits in plan]
    widths = [width for width, _ in plan]
    n = len(orders[0])
    kv_width = kv_weight.shape[1] // 2 if kv_weight is not None else 0
    columns = sum(widths) + kv_width
    outs = []
    for chunk, width in enumerate(widths):
        shape = (n * rows // 2, width + (0 if chunk else kv_width))
        outs += [jax.ShapeDtypeStruct(shape, jnp.float32)] * 2
    weights = [query_weight] + ([kv_weight] if kv_width else [])
    parts = features // 768 if features % 768 == 0 else 1
    copies = parts * (len(weights) - 1 + sum(len(spans_of(width)) for width in widths))
    outs = pl.pallas_call(
        functools.partial(project_kernel, orders, rows, first, widths, kv_width, len(after)),
        out_shape=outs,
        in_specs=[SMEM, VMEM, VMEM] + [HBM] * len(weights) + [ANY] * len(after),
        out_specs=[VMEM] * len(outs),
        scratch_shapes=[
            pltpu.VMEM((n * rows, features), tokens.dtype),
            pltpu.VMEM((features, columns), tokens.dtype),
            pltpu.SemaphoreType.DMA((copies,)),
        ],
        compiler_params=pltpu.CompilerParams(vmem_limit_bytes=46 * MIB),
        cost_estimate=pl.CostEstimate(
            flops=2 * n * rows * features * columns,
            bytes_accessed=2 * features * columns + 4 * n * rows * columns,
            transcendentals=0,
        ),
        name="project",
    )(ids, tokens, other, *weights, *after)
    return list(zip(outs[::2], outs[1::2]))


def attend_kernel(parts, scalars_ref, *refs):
    own_q, other_q = refs[: len(parts)], refs[len(parts) : 2 * len(parts)]
    k_ref, v_hbm, own_out, other_out, v_ref, q_scr, o_scr, sems = refs[2 * len(parts) :]
    core = scalars_ref[0]
    rows, positions, _ = k_ref.shape
    copies = [pltpu.make_async_copy(v_hbm.at[row], v_ref.at[row], sems.at[row]) for row in range(rows)]
    for copy in copies:
        copy.start()
    at = 0
    for side in (own_q, other_q):
        for ref, (heads, skip) in zip(side, parts):
            for head in range(heads):
                column = skip + head * DH
                q_scr[:, at, :] = ref[:, column : column + DH].astype(jnp.float32)
                at += 1
    total_heads = at
    kv_at = [skip > 0 for _, skip in parts].index(True)
    first = own_q[kv_at][:, :DH].astype(jnp.float32)
    second = other_q[kv_at][:, :DH].astype(jnp.float32)
    new_keys = jnp.where(core == 0, first, second)
    new_values = jnp.where(core == 0, second, first)
    scale = DH**-0.5
    shares = []
    for row in range(rows):
        query = q_scr[row]
        scores = scale * lax.dot_general(
            query.astype(jnp.bfloat16),
            k_ref[row],
            (((1,), (1,)), ((), ())),
            preferred_element_type=jnp.float32,
        )
        self_score = scale * jnp.sum(query * new_keys[row : row + 1], axis=1, keepdims=True)
        visible = lax.broadcasted_iota(jnp.int32, scores.shape, 1) < scalars_ref[1 + row]
        masked = jnp.where(visible, scores, jnp.float32(-1e30))
        peak = jnp.maximum(jnp.max(masked, axis=1, keepdims=True), self_score)
        raised = jnp.where(visible, jnp.exp(masked - peak), jnp.float32(0.0))
        self_raised = jnp.exp(self_score - peak)
        denominator = jnp.sum(raised, axis=1, keepdims=True) + self_raised
        weights = (raised / denominator).astype(jnp.bfloat16)
        self_weight = (self_raised / denominator).astype(jnp.bfloat16).astype(jnp.float32)
        shares.append((weights, self_weight))
    for copy in copies:
        copy.wait()
    for row, (weights, self_weight) in enumerate(shares):
        total = jnp.dot(weights, v_ref[row], preferred_element_type=jnp.float32)
        o_scr[row] = total + self_weight * new_values[row : row + 1]
    half = total_heads // 2
    for head in range(total_heads):
        ref = own_out if head < half else other_out
        column = (head % half) * DH
        ref[:, column : column + DH] = o_scr[:, head, :].astype(jnp.bfloat16)


def attend(core, lengths, own_q, other_q, parts, keys, values):
    rows, positions, _ = keys.shape
    heads = 2 * sum(part[0] for part in parts)
    out = jax.ShapeDtypeStruct((rows, heads * DH // 2), jnp.bfloat16)
    scalars = jnp.concatenate([core[None], lengths])
    return pl.pallas_call(
        functools.partial(attend_kernel, parts),
        out_shape=(out, out),
        in_specs=[SMEM] + [VMEM] * (2 * len(parts) + 1) + [HBM],
        out_specs=(VMEM, VMEM),
        scratch_shapes=[pltpu.VMEM(values.shape, values.dtype)]
        + [pltpu.VMEM((rows, heads, DH), jnp.float32)] * 2
        + [pltpu.SemaphoreType.DMA((rows,))],
        compiler_params=pltpu.CompilerParams(vmem_limit_bytes=49 * MIB),
        cost_estimate=pl.CostEstimate(
            flops=4 * rows * heads * positions * DH,
            bytes_accessed=4 * rows * positions * DH,
            transcendentals=rows * heads * positions,
        ),
        name="attend",
    )(scalars, *own_q, *other_q, keys, values)


def output_kernel(orders, rows, columns, pieces, after, ids_ref, *refs):
    count = 2 * len(orders)
    block_refs, w_refs = refs[:count], refs[count : count + len(pieces)]
    send_ref, keep_ref, xs_ref = refs[count + len(pieces) + after :]
    depth = block_refs[0].shape[1]
    me, core = ids_ref[0], ids_ref[1]
    n = len(orders[0])
    half = n // 2
    for group, (near_ref, far_ref) in enumerate(zip(block_refs[::2], block_refs[1::2])):
        for p, j in enumerate(orders[group]):
            block = jnp.bitwise_xor(me, j)
            place = block % half + jnp.where(block // half == core, half, 0)
            source = near_ref if p < half else far_ref
            at = (p % half) * rows
            xs_ref[
                pl.ds(pl.multiple_of(place * rows, rows), rows), group * depth : (group + 1) * depth
            ] = source[at : at + rows, :]
    cut = half * rows
    totals = {}
    for w_ref, ((first, tall), span) in zip(w_refs, pieces):
        part = jnp.dot(
            xs_ref[:, first : first + tall], w_ref[...], preferred_element_type=jnp.float32
        )
        totals[span] = totals[span] + part if span in totals else part
    for (column, width), total in totals.items():
        send_ref[:, column - columns[0] : column - columns[0] + width] = total[:cut]
        keep_ref[:, column - columns[0] : column - columns[0] + width] = total[cut:]


def project_out(orders, rows, ids, blocks, held, cuts, columns, after):
    chosen = [at for at, (_, (column, _)) in enumerate(cuts) if columns[0] <= column < sum(columns)]
    weights, pieces = [held[at] for at in chosen], [cuts[at] for at in chosen]
    pieces, weights = zip(*sorted(zip(pieces, weights), key=lambda pair: (pair[0][1], pair[0][0])))
    depth = len(orders) * blocks[0].shape[1]
    n = len(orders[0])
    out = jax.ShapeDtypeStruct((n * rows // 2, columns[1]), jnp.float32)
    return pl.pallas_call(
        functools.partial(output_kernel, orders, rows, columns, pieces, len(after)),
        out_shape=(out, out),
        in_specs=[SMEM] + [VMEM] * (len(blocks) + len(weights)) + [ANY] * len(after),
        out_specs=(VMEM, VMEM),
        scratch_shapes=[pltpu.VMEM((n * rows, depth), jnp.bfloat16)],
        compiler_params=pltpu.CompilerParams(vmem_limit_bytes=12 * MIB),
        cost_estimate=pl.CostEstimate(
            flops=2 * n * rows * depth * columns[1],
            bytes_accessed=2 * depth * columns[1] + 4 * n * rows * columns[1],
            transcendentals=0,
        ),
        name="project_out",
    )(ids, *blocks, *weights, *after)


def local(tokens, query_weight, kv_weight, out_weight, key_cache, value_cache, lengths):
    n = lax.axis_size("gx")
    me = lax.axis_index("gx").astype(jnp.int32)
    core = lax.axis_index("gy").astype(jnp.int32)
    ids = jnp.stack([me, core])
    own_rows = key_cache.shape[0]
    rows = 2 * own_rows
    bits = [1 << i for i in range(n.bit_length() - 1)]

    def swap(array):
        return lax.ppermute(array, "gy", [(0, 1), (1, 0)])

    def across(array, mask):
        return lax.ppermute(array, "gx", [(g, g ^ mask) for g in range(n)])

    other_tokens = swap(tokens)
    own_tokens = jnp.where(me < n, tokens, jnp.bfloat16(0))
    width = query_weight.shape[1] // 2

    y, z = bits[:1], bits[1:]
    unit = query_weight.shape[1] // 12
    plan = [(3 * unit, z[:1] + y + z[1:]), (5 * unit, y + z), (4 * unit, z + y)]
    state, first, after = [None] * len(plan), 0, []
    for group in ((2,), (0, 1)):
        chunks = [plan[i] for i in group]
        weight = kv_weight if 0 in group else None
        made = project(chunks, rows, ids, own_tokens, other_tokens, query_weight, weight, first, after)
        for i, pair in zip(group, made):
            state[i] = pair
        after = [made[0][0]]
        first += sum(columns for columns, _ in chunks)
    moving = [across(send, order[0]) for (send, _), (_, order) in zip(state, plan)]
    second = None
    for step in range(len(bits)):
        for i in (2, 0, 1):
            columns, order = plan[i]
            total = state[i][1] + moving[i]
            if i == 0 and step == 2 and len(bits) == 3:
                total = total + 0.0 * second[:1, : total.shape[1]]
            if i == 1 and step == 1:
                second = total
            if step + 1 < len(bits):
                cut = total.shape[0] // 2
                state[i] = (total[cut:], total[:cut])
                moving[i] = across(state[i][0], order[step + 1])
            else:
                state[i] = total
    mine, theirs = [], []
    for total in state:
        mine.append(lax.dynamic_slice_in_dim(total, core * own_rows, own_rows, 0).astype(jnp.bfloat16))
        give = lax.dynamic_slice_in_dim(total, (1 - core) * own_rows, own_rows, 0).astype(jnp.bfloat16)
        theirs.append(swap(give))

    kv_width = kv_weight.shape[1] // 2
    by_column = [i for group in ((2,), (0, 1)) for i in group]
    parts = tuple((plan[i][0] // DH, 0 if i else kv_width) for i in by_column)
    mine, theirs = [mine[i] for i in by_column], [theirs[i] for i in by_column]
    own, other = attend(core, lengths, mine, theirs, parts, key_cache, value_cache)
    got = swap(other)
    block = jnp.where(core == 0, jnp.concatenate([own, got]), jnp.concatenate([got, own]))

    near = [block[:, :width], block[:, width:]]
    far = [None, None]
    paths = [bits[::-1], bits[:1] + bits[:0:-1]]
    out_cuts, out_held = cuts_of(out_weight), []
    early = len(out_cuts) * 9 // 18
    for step in range(len(bits)):
        for i in range(2):
            if step:
                near[i] = jnp.concatenate([near[i], far[i]])
                if i == 0 and out_held:
                    near[i] = near[i] + zero.astype(jnp.bfloat16)
                if i == 1 and step + 2 >= len(bits):
                    part = out_cuts[early:] if out_held else out_cuts[:early]
                    held, zero = load([out_weight], [(0, cut) for cut in part], near, 36, width)
                    out_held += held
            far[i] = across(near[i], paths[i][step])
    orders = [order_of(path[::-1]) for path in paths]
    blocks = [b for pair in zip(near, far) for b in pair]
    total_columns = out_weight.shape[1]
    last = 768 if total_columns % 768 == 0 and total_columns > 768 else 0
    results, after = [], []
    for columns in ((0, total_columns - last), (total_columns - last, last)):
        if columns[1]:
            send, keep = project_out(orders, rows, ids, blocks, out_held, out_cuts, columns, after)
            after = [send]
            results.append((keep + swap(send)).astype(jnp.bfloat16))
    return jnp.concatenate(results, axis=1)


def solution(mesh):
    return jax.shard_map(
        local,
        mesh=mesh,
        in_specs=(
            P(("grp", "gy"), "gx"),
            P("gx", "gy"),
            P("gx", None),
            P("gy", "gx"),
            P(("grp", "gx", "gy"), None, None),
            P(("grp", "gx", "gy"), None, None),
            P(("grp", "gx", "gy")),
        ),
        out_specs=P(("grp", "gy"), "gx"),
        check_vma=False,
    )
```

```python
import functools

import jax
import jax.numpy as jnp
from jax import lax
from jax.experimental import pallas as pl
from jax.experimental.pallas import tpu as pltpu
from jax.sharding import PartitionSpec as P

H = 24
DH = 256
MIB = 1024 * 1024
HBM = pl.BlockSpec(memory_space=pltpu.HBM)
ANY = pl.BlockSpec(memory_space=pl.ANY)
VMEM = pl.BlockSpec(memory_space=pltpu.VMEM)
SMEM = pl.BlockSpec(memory_space=pltpu.SMEM)


class InOrder:
    def __init__(self, copies, ahead):
        self.copies, self.ahead = copies, ahead
        for copy in copies[:ahead]:
            copy.start()

    def wait(self, at):
        self.copies[at].wait()
        if at + self.ahead < len(self.copies):
            self.copies[at + self.ahead].start()


def order_of(bits):
    order = [0]
    for bit in reversed(bits):
        order = order + [j + bit for j in order]
    return order


def cuts_of(array):
    if len(array.shape) == 3:
        return [(at, None) for at in range(array.shape[0])]
    depth, columns = array.shape
    tall, wide = 512, (768 if columns % 768 == 0 else columns)
    return [
        ((at, tall), (column, wide)) for at in range(0, depth, tall) for column in range(0, columns, wide)
    ]


def piece_of(array, cut):
    if cut[1] is None:
        shape = array.shape[1:]
    else:
        shape = (cut[0][1], cut[1][1])
    return jax.ShapeDtypeStruct(shape, array.dtype)


def fetches(refs, cuts, targets, sems):
    copies = []
    for ref, cut in cuts:
        source = refs[ref]
        view = source.at[cut[0]] if cut[1] is None else source.at[pl.ds(*cut[0]), pl.ds(*cut[1])]
        copies.append(pltpu.make_async_copy(view, targets[len(copies)], sems.at[len(copies)]))
    return copies


def load_kernel(after, cuts, count, *refs):
    refs = refs[after:]
    in_refs, out_refs, zero_ref, sems = refs[:count], refs[count:-2], refs[-2], refs[-1]
    copies = fetches(in_refs, cuts, out_refs, sems)
    for copy in copies:
        copy.start()
    zero_ref[...] = jnp.zeros_like(zero_ref)
    for copy in copies:
        copy.wait()


def load(arrays, cuts, after, grant, zeros=128):
    shapes = [piece_of(arrays[at], cut) for at, cut in cuts]
    *held, zero = pl.pallas_call(
        functools.partial(load_kernel, len(after), cuts, len(arrays)),
        out_shape=(*shapes, jax.ShapeDtypeStruct((1, zeros), jnp.float32)),
        in_specs=[ANY] * len(after) + [HBM] * len(arrays),
        out_specs=[VMEM] * (len(cuts) + 1),
        scratch_shapes=[pltpu.SemaphoreType.DMA((len(cuts),))],
        compiler_params=pltpu.CompilerParams(vmem_limit_bytes=grant * MIB),
        cost_estimate=pl.CostEstimate(
            flops=0, bytes_accessed=sum(4 * s.shape[0] * s.shape[1] for s in shapes), transcendentals=0
        ),
        name="load",
    )(*after, *arrays)
    return held, zero


def spans_of(width):
    return [(at, min(512, width - at)) for at in range(0, width, 512)]


def project_kernel(orders, rows, first, widths, kv_width, after, ids_ref, own_ref, other_ref, w_ref, *refs):
    refs = list(refs)
    kv_ref = refs.pop(0) if kv_width else None
    outs, (xs_ref, ws_ref, w_sem) = refs[after:-3], refs[-3:]
    n = len(orders[0])
    half = n // 2
    me, core = ids_ref[0], ids_ref[1]
    features = xs_ref.shape[1]

    tiles, copies, at, source = [], [], 0, first
    depth = 768 if features % 768 == 0 else features

    def fetch(from_ref, column, width):
        for part in range(features // depth):
            span = pl.ds(part * depth, depth)
            copies.append(
                pltpu.make_async_copy(
                    from_ref.at[span, pl.ds(column, width)],
                    ws_ref.at[span, pl.ds(at, width)],
                    w_sem.at[len(copies)],
                )
            )

    for chunk, width in enumerate(widths):
        column = 0
        if kv_width and chunk == 0:
            fetch(kv_ref, pl.multiple_of(core * kv_width, kv_width), kv_width)
            tiles.append((chunk, 0, at, kv_width))
            at += kv_width
            column = kv_width
        for offset, tile in spans_of(width):
            fetch(w_ref, source, tile)
            tiles.append((chunk, column + offset, at, tile))
            at += tile
            source += tile
    per_tile = features // depth
    weights = InOrder(copies, 9)
    def place_rows(low_ref, high_ref):
        for j in range(n):
            block = jnp.bitwise_xor(me, j) % half
            source = low_ref if j < half else high_ref
            xs_ref[j * rows : (j + 1) * rows, :] = source[
                pl.ds(pl.multiple_of(block * rows, rows), rows), :
            ]

    low_mine = me // half == core

    @pl.when(low_mine)
    def _():
        place_rows(own_ref, other_ref)

    @pl.when(jnp.logical_not(low_mine))
    def _():
        place_rows(other_ref, own_ref)

    for t, (chunk, column, at, width) in enumerate(tiles):
        for part in range(per_tile):
            weights.wait(t * per_tile + part)
        total = jnp.dot(xs_ref[...], ws_ref[:, at : at + width], preferred_element_type=jnp.float32)
        span = slice(column, column + width)
        for p, j in enumerate(orders[chunk]):
            out = outs[2 * chunk + 1] if p < half else outs[2 * chunk]
            out[(p % half) * rows : (p % half + 1) * rows, span] = total[j * rows : (j + 1) * rows]


def project(plan, rows, ids, tokens, other, query_weight, kv_weight, first, after):
    features = tokens.shape[1]
    orders = [order_of(bits) for _, bits in plan]
    widths = [width for width, _ in plan]
    n = len(orders[0])
    kv_width = kv_weight.shape[1] // 2 if kv_weight is not None else 0
    columns = sum(widths) + kv_width
    outs = []
    for chunk, width in enumerate(widths):
        shape = (n * rows // 2, width + (0 if chunk else kv_width))
        outs += [jax.ShapeDtypeStruct(shape, jnp.float32)] * 2
    weights = [query_weight] + ([kv_weight] if kv_width else [])
    parts = features // 768 if features % 768 == 0 else 1
    copies = parts * (len(weights) - 1 + sum(len(spans_of(width)) for width in widths))
    outs = pl.pallas_call(
        functools.partial(project_kernel, orders, rows, first, widths, kv_width, len(after)),
        out_shape=outs,
        in_specs=[SMEM, VMEM, VMEM] + [HBM] * len(weights) + [ANY] * len(after),
        out_specs=[VMEM] * len(outs),
        scratch_shapes=[
            pltpu.VMEM((n * rows, features), tokens.dtype),
            pltpu.VMEM((features, columns), tokens.dtype),
            pltpu.SemaphoreType.DMA((copies,)),
        ],
        compiler_params=pltpu.CompilerParams(vmem_limit_bytes=46 * MIB),
        cost_estimate=pl.CostEstimate(
            flops=2 * n * rows * features * columns,
            bytes_accessed=2 * features * columns + 4 * n * rows * columns,
            transcendentals=0,
        ),
        name="project",
    )(ids, tokens, other, *weights, *after)
    return list(zip(outs[::2], outs[1::2]))


def attend_kernel(kv_column, scalars_ref, own_q, other_q, *refs):
    k_ref, v_hbm, own_out, other_out, v_ref, q_scr, o_scr, sems = refs
    core = scalars_ref[0]
    rows, positions, _ = k_ref.shape
    copies = [pltpu.make_async_copy(v_hbm.at[row], v_ref.at[row], sems.at[row]) for row in range(rows)]
    for copy in copies:
        copy.start()
    at = 0
    for ref in (own_q, other_q):
        for column in range(0, ref.shape[1], DH):
            if column != kv_column:
                q_scr[:, at, :] = ref[:, column : column + DH].astype(jnp.float32)
                at += 1
    total_heads = at
    first = own_q[:, kv_column : kv_column + DH].astype(jnp.float32)
    second = other_q[:, kv_column : kv_column + DH].astype(jnp.float32)
    new_keys = jnp.where(core == 0, first, second)
    new_values = jnp.where(core == 0, second, first)
    scale = DH**-0.5
    shares = []
    for row in range(rows):
        query = q_scr[row]
        scores = scale * lax.dot_general(
            query.astype(jnp.bfloat16),
            k_ref[row],
            (((1,), (1,)), ((), ())),
            preferred_element_type=jnp.float32,
        )
        self_score = scale * jnp.sum(query * new_keys[row : row + 1], axis=1, keepdims=True)
        visible = lax.broadcasted_iota(jnp.int32, scores.shape, 1) < scalars_ref[1 + row]
        masked = jnp.where(visible, scores, jnp.float32(-1e30))
        peak = jnp.maximum(jnp.max(masked, axis=1, keepdims=True), self_score)
        raised = jnp.where(visible, jnp.exp(masked - peak), jnp.float32(0.0))
        self_raised = jnp.exp(self_score - peak)
        denominator = jnp.sum(raised, axis=1, keepdims=True) + self_raised
        weights = (raised / denominator).astype(jnp.bfloat16)
        self_weight = (self_raised / denominator).astype(jnp.bfloat16).astype(jnp.float32)
        shares.append((weights, self_weight))
    for copy in copies:
        copy.wait()
    for row, (weights, self_weight) in enumerate(shares):
        total = jnp.dot(weights, v_ref[row], preferred_element_type=jnp.float32)
        o_scr[row] = total + self_weight * new_values[row : row + 1]
    half = total_heads // 2
    for head in range(total_heads):
        ref = own_out if head < half else other_out
        column = (head % half) * DH
        ref[:, column : column + DH] = o_scr[:, head, :].astype(jnp.bfloat16)


def attend(core, lengths, own_q, other_q, kv_column, keys, values):
    rows, positions, _ = keys.shape
    heads = 2 * (own_q.shape[1] // DH - 1)
    out = jax.ShapeDtypeStruct((rows, heads * DH // 2), jnp.bfloat16)
    scalars = jnp.concatenate([core[None], lengths])
    return pl.pallas_call(
        functools.partial(attend_kernel, kv_column),
        out_shape=(out, out),
        in_specs=[SMEM] + [VMEM] * 3 + [HBM],
        out_specs=(VMEM, VMEM),
        scratch_shapes=[pltpu.VMEM(values.shape, values.dtype)]
        + [pltpu.VMEM((rows, heads, DH), jnp.float32)] * 2
        + [pltpu.SemaphoreType.DMA((rows,))],
        compiler_params=pltpu.CompilerParams(vmem_limit_bytes=49 * MIB),
        cost_estimate=pl.CostEstimate(
            flops=4 * rows * heads * positions * DH,
            bytes_accessed=4 * rows * positions * DH,
            transcendentals=rows * heads * positions,
        ),
        name="attend",
    )(scalars, own_q, other_q, keys, values)


def output_kernel(orders, rows, columns, pieces, after, ids_ref, *refs):
    count = 2 * len(orders)
    block_refs, w_refs = refs[:count], refs[count : count + len(pieces)]
    send_ref, keep_ref, xs_ref = refs[count + len(pieces) + after :]
    depth = block_refs[0].shape[1]
    me, core = ids_ref[0], ids_ref[1]
    n = len(orders[0])
    half = n // 2
    for group, (near_ref, far_ref) in enumerate(zip(block_refs[::2], block_refs[1::2])):
        for p, j in enumerate(orders[group]):
            block = jnp.bitwise_xor(me, j)
            place = block % half + jnp.where(block // half == core, half, 0)
            source = near_ref if p < half else far_ref
            at = (p % half) * rows
            xs_ref[
                pl.ds(pl.multiple_of(place * rows, rows), rows), group * depth : (group + 1) * depth
            ] = source[at : at + rows, :]
    cut = half * rows
    totals = {}
    for w_ref, ((first, tall), span) in zip(w_refs, pieces):
        part = jnp.dot(
            xs_ref[:, first : first + tall], w_ref[...], preferred_element_type=jnp.float32
        )
        totals[span] = totals[span] + part if span in totals else part
    for (column, width), total in totals.items():
        send_ref[:, column - columns[0] : column - columns[0] + width] = total[:cut]
        keep_ref[:, column - columns[0] : column - columns[0] + width] = total[cut:]


def project_out(orders, rows, ids, blocks, held, cuts, columns, after):
    chosen = [at for at, (_, (column, _)) in enumerate(cuts) if columns[0] <= column < sum(columns)]
    weights, pieces = [held[at] for at in chosen], [cuts[at] for at in chosen]
    pieces, weights = zip(*sorted(zip(pieces, weights), key=lambda pair: (pair[0][1], pair[0][0])))
    depth = len(orders) * blocks[0].shape[1]
    n = len(orders[0])
    out = jax.ShapeDtypeStruct((n * rows // 2, columns[1]), jnp.float32)
    return pl.pallas_call(
        functools.partial(output_kernel, orders, rows, columns, pieces, len(after)),
        out_shape=(out, out),
        in_specs=[SMEM] + [VMEM] * (len(blocks) + len(weights)) + [ANY] * len(after),
        out_specs=(VMEM, VMEM),
        scratch_shapes=[pltpu.VMEM((n * rows, depth), jnp.bfloat16)],
        compiler_params=pltpu.CompilerParams(vmem_limit_bytes=12 * MIB),
        cost_estimate=pl.CostEstimate(
            flops=2 * n * rows * depth * columns[1],
            bytes_accessed=2 * depth * columns[1] + 4 * n * rows * columns[1],
            transcendentals=0,
        ),
        name="project_out",
    )(ids, *blocks, *weights, *after)


def local(tokens, query_weight, kv_weight, out_weight, key_cache, value_cache, lengths):
    n = lax.axis_size("gx")
    me = lax.axis_index("gx").astype(jnp.int32)
    core = lax.axis_index("gy").astype(jnp.int32)
    ids = jnp.stack([me, core])
    own_rows = key_cache.shape[0]
    rows = 2 * own_rows
    bits = [1 << i for i in range(n.bit_length() - 1)]

    def swap(array):
        return lax.ppermute(array, "gy", [(0, 1), (1, 0)])

    def across(array, mask):
        return lax.ppermute(array, "gx", [(g, g ^ mask) for g in range(n)])

    other_tokens = swap(tokens)
    own_tokens = jnp.where(me < n, tokens, jnp.bfloat16(0))
    width = query_weight.shape[1] // 2

    y, z = bits[:1], bits[1:]
    unit = query_weight.shape[1] // 12
    plan = [(3 * unit, z[:1] + y + z[1:]), (5 * unit, y + z), (4 * unit, z + y)]
    state, first, after = [None] * len(plan), 0, []
    for group in ((2,), (0, 1)):
        chunks = [plan[i] for i in group]
        weight = kv_weight if 0 in group else None
        made = project(chunks, rows, ids, own_tokens, other_tokens, query_weight, weight, first, after)
        for i, pair in zip(group, made):
            state[i] = pair
        after = [made[0][0]]
        first += sum(columns for columns, _ in chunks)
    moving = [across(send, order[0]) for (send, _), (_, order) in zip(state, plan)]
    for step in range(len(bits)):
        for i in (2, 0, 1):
            columns, order = plan[i]
            total = state[i][1] + moving[i]
            if step + 1 < len(bits):
                cut = total.shape[0] // 2
                state[i] = (total[cut:], total[:cut])
                moving[i] = across(state[i][0], order[step + 1])
            else:
                state[i] = total
    kv_width = kv_weight.shape[1] // 2
    by_column = [i for group in ((2,), (0, 1)) for i in group]
    total = jnp.concatenate([state[i] for i in by_column], axis=1)
    mine = lax.dynamic_slice_in_dim(total, core * own_rows, own_rows, 0).astype(jnp.bfloat16)
    give = lax.dynamic_slice_in_dim(total, (1 - core) * own_rows, own_rows, 0).astype(jnp.bfloat16)
    kv_column = sum(plan[i][0] for i in by_column[: by_column.index(0)])
    own, other = attend(core, lengths, mine, swap(give), kv_column, key_cache, value_cache)
    got = swap(other)
    block = jnp.where(core == 0, jnp.concatenate([own, got]), jnp.concatenate([got, own]))

    near = [block[:, :width], block[:, width:]]
    far = [None, None]
    paths = [bits[::-1], bits[:1] + bits[:0:-1]]
    out_cuts, out_held = cuts_of(out_weight), []
    early = len(out_cuts) * 9 // 18
    for step in range(len(bits)):
        for i in range(2):
            if step:
                near[i] = jnp.concatenate([near[i], far[i]])
                if i == 0 and out_held:
                    near[i] = near[i] + zero.astype(jnp.bfloat16)
                if i == 1 and step + 2 >= len(bits):
                    part = out_cuts[early:] if out_held else out_cuts[:early]
                    held, zero = load([out_weight], [(0, cut) for cut in part], near, 36, width)
                    out_held += held
            far[i] = across(near[i], paths[i][step])
    orders = [order_of(path[::-1]) for path in paths]
    blocks = [b for pair in zip(near, far) for b in pair]
    total_columns = out_weight.shape[1]
    last = 768 if total_columns % 768 == 0 and total_columns > 768 else 0
    results, after = [], []
    for columns in ((0, total_columns - last), (total_columns - last, last)):
        if columns[1]:
            send, keep = project_out(orders, rows, ids, blocks, out_held, out_cuts, columns, after)
            after = [send]
            results.append((keep + swap(send)).astype(jnp.bfloat16))
    return jnp.concatenate(results, axis=1)


def solution(mesh):
    return jax.shard_map(
        local,
        mesh=mesh,
        in_specs=(
            P(("grp", "gy"), "gx"),
            P("gx", "gy"),
            P("gx", None),
            P("gy", "gx"),
            P(("grp", "gx", "gy"), None, None),
            P(("grp", "gx", "gy"), None, None),
            P(("grp", "gx", "gy")),
        ),
        out_specs=P(("grp", "gy"), "gx"),
        check_vma=False,
    )
```

```python
import functools

import jax
import jax.numpy as jnp
from jax import lax
from jax.experimental import pallas as pl
from jax.experimental.pallas import tpu as pltpu
from jax.sharding import PartitionSpec as P

H = 24
DH = 256
MIB = 1024 * 1024
HBM = pl.BlockSpec(memory_space=pltpu.HBM)
ANY = pl.BlockSpec(memory_space=pl.ANY)
VMEM = pl.BlockSpec(memory_space=pltpu.VMEM)
SMEM = pl.BlockSpec(memory_space=pltpu.SMEM)


class InOrder:
    def __init__(self, copies, ahead):
        self.copies, self.ahead = copies, ahead
        for copy in copies[:ahead]:
            copy.start()

    def wait(self, at):
        self.copies[at].wait()
        if at + self.ahead < len(self.copies):
            self.copies[at + self.ahead].start()


def order_of(bits):
    order = [0]
    for bit in reversed(bits):
        order = order + [j + bit for j in order]
    return order


def cuts_of(array):
    if len(array.shape) == 3:
        return [(at, None) for at in range(array.shape[0])]
    depth, columns = array.shape
    tall, wide = 512, (768 if columns % 768 == 0 else columns)
    return [
        ((at, tall), (column, wide)) for at in range(0, depth, tall) for column in range(0, columns, wide)
    ]


def piece_of(array, cut):
    if cut[1] is None:
        shape = array.shape[1:]
    else:
        shape = (cut[0][1], cut[1][1])
    return jax.ShapeDtypeStruct(shape, array.dtype)


def fetches(refs, cuts, targets, sems):
    copies = []
    for ref, cut in cuts:
        source = refs[ref]
        view = source.at[cut[0]] if cut[1] is None else source.at[pl.ds(*cut[0]), pl.ds(*cut[1])]
        copies.append(pltpu.make_async_copy(view, targets[len(copies)], sems.at[len(copies)]))
    return copies


def load_kernel(after, cuts, count, *refs):
    refs = refs[after:]
    in_refs, out_refs, zero_ref, sems = refs[:count], refs[count:-2], refs[-2], refs[-1]
    copies = fetches(in_refs, cuts, out_refs, sems)
    for copy in copies:
        copy.start()
    zero_ref[...] = jnp.zeros_like(zero_ref)
    for copy in copies:
        copy.wait()


def load(arrays, cuts, after, grant, zeros=128):
    shapes = [piece_of(arrays[at], cut) for at, cut in cuts]
    *held, zero = pl.pallas_call(
        functools.partial(load_kernel, len(after), cuts, len(arrays)),
        out_shape=(*shapes, jax.ShapeDtypeStruct((1, zeros), jnp.float32)),
        in_specs=[ANY] * len(after) + [HBM] * len(arrays),
        out_specs=[VMEM] * (len(cuts) + 1),
        scratch_shapes=[pltpu.SemaphoreType.DMA((len(cuts),))],
        compiler_params=pltpu.CompilerParams(vmem_limit_bytes=grant * MIB),
        cost_estimate=pl.CostEstimate(
            flops=0, bytes_accessed=sum(4 * s.shape[0] * s.shape[1] for s in shapes), transcendentals=0
        ),
        name="load",
    )(*after, *arrays)
    return held, zero


def spans_of(width):
    return [(at, min(512, width - at)) for at in range(0, width, 512)]


def project_kernel(orders, rows, first, widths, kv_width, after, ids_ref, own_ref, other_ref, w_ref, *refs):
    refs = list(refs)
    kv_ref = refs.pop(0) if kv_width else None
    outs, (xs_ref, ws_ref, w_sem) = refs[after:-3], refs[-3:]
    n = len(orders[0])
    half = n // 2
    me, core = ids_ref[0], ids_ref[1]
    features = xs_ref.shape[1]

    tiles, copies, at, source = [], [], 0, first
    depth = 768 if features % 768 == 0 else features

    def fetch(from_ref, column, width):
        for part in range(features // depth):
            span = pl.ds(part * depth, depth)
            copies.append(
                pltpu.make_async_copy(
                    from_ref.at[span, pl.ds(column, width)],
                    ws_ref.at[span, pl.ds(at, width)],
                    w_sem.at[len(copies)],
                )
            )

    for chunk, width in enumerate(widths):
        column = 0
        if kv_width and chunk == 0:
            fetch(kv_ref, pl.multiple_of(core * kv_width, kv_width), kv_width)
            tiles.append((chunk, 0, at, kv_width))
            at += kv_width
            column = kv_width
        for offset, tile in spans_of(width):
            fetch(w_ref, source, tile)
            tiles.append((chunk, column + offset, at, tile))
            at += tile
            source += tile
    per_tile = features // depth
    weights = InOrder(copies, 9)
    def place_rows(low_ref, high_ref):
        for j in range(n):
            block = jnp.bitwise_xor(me, j) % half
            source = low_ref if j < half else high_ref
            xs_ref[j * rows : (j + 1) * rows, :] = source[
                pl.ds(pl.multiple_of(block * rows, rows), rows), :
            ]

    low_mine = me // half == core

    @pl.when(low_mine)
    def _():
        place_rows(own_ref, other_ref)

    @pl.when(jnp.logical_not(low_mine))
    def _():
        place_rows(other_ref, own_ref)

    for t, (chunk, column, at, width) in enumerate(tiles):
        for part in range(per_tile):
            weights.wait(t * per_tile + part)
        total = jnp.dot(xs_ref[...], ws_ref[:, at : at + width], preferred_element_type=jnp.float32)
        span = slice(column, column + width)
        for p, j in enumerate(orders[chunk]):
            out = outs[2 * chunk + 1] if p < half else outs[2 * chunk]
            out[(p % half) * rows : (p % half + 1) * rows, span] = total[j * rows : (j + 1) * rows]


def project(plan, rows, ids, tokens, other, query_weight, kv_weight, first, after):
    features = tokens.shape[1]
    orders = [order_of(bits) for _, bits in plan]
    widths = [width for width, _ in plan]
    n = len(orders[0])
    kv_width = kv_weight.shape[1] // 2 if kv_weight is not None else 0
    columns = sum(widths) + kv_width
    outs = []
    for chunk, width in enumerate(widths):
        shape = (n * rows // 2, width + (0 if chunk else kv_width))
        outs += [jax.ShapeDtypeStruct(shape, jnp.float32)] * 2
    weights = [query_weight] + ([kv_weight] if kv_width else [])
    parts = features // 768 if features % 768 == 0 else 1
    copies = parts * (len(weights) - 1 + sum(len(spans_of(width)) for width in widths))
    outs = pl.pallas_call(
        functools.partial(project_kernel, orders, rows, first, widths, kv_width, len(after)),
        out_shape=outs,
        in_specs=[SMEM, VMEM, VMEM] + [HBM] * len(weights) + [ANY] * len(after),
        out_specs=[VMEM] * len(outs),
        scratch_shapes=[
            pltpu.VMEM((n * rows, features), tokens.dtype),
            pltpu.VMEM((features, columns), tokens.dtype),
            pltpu.SemaphoreType.DMA((copies,)),
        ],
        compiler_params=pltpu.CompilerParams(vmem_limit_bytes=46 * MIB),
        cost_estimate=pl.CostEstimate(
            flops=2 * n * rows * features * columns,
            bytes_accessed=2 * features * columns + 4 * n * rows * columns,
            transcendentals=0,
        ),
        name="project",
    )(ids, tokens, other, *weights, *after)
    return list(zip(outs[::2], outs[1::2]))


def attend_kernel(kv_column, scalars_ref, own_q, other_q, *refs):
    k_ref, v_hbm, own_out, other_out, v_ref, q_scr, o_scr, sems = refs
    core = scalars_ref[0]
    rows, positions, _ = k_ref.shape
    copies = [pltpu.make_async_copy(v_hbm.at[row], v_ref.at[row], sems.at[row]) for row in range(rows)]
    for copy in copies:
        copy.start()
    at = 0
    for ref in (own_q, other_q):
        for column in range(0, ref.shape[1], DH):
            if column != kv_column:
                q_scr[:, at, :] = DH**-0.5 * ref[:, column : column + DH].astype(jnp.float32)
                at += 1
    total_heads = at
    first = own_q[:, kv_column : kv_column + DH].astype(jnp.float32)
    second = other_q[:, kv_column : kv_column + DH].astype(jnp.float32)
    new_keys = jnp.where(core == 0, first, second)
    new_values = jnp.where(core == 0, second, first)
    shares = []
    for row in range(rows):
        query = q_scr[row]
        scores = lax.dot_general(
            query.astype(jnp.bfloat16),
            k_ref[row],
            (((1,), (1,)), ((), ())),
            preferred_element_type=jnp.float32,
        )
        self_score = jnp.sum(query * new_keys[row : row + 1], axis=1, keepdims=True)
        visible = lax.broadcasted_iota(jnp.int32, scores.shape, 1) < scalars_ref[1 + row]
        masked = jnp.where(visible, scores, jnp.float32(-1e30))
        peak = jnp.maximum(jnp.max(masked, axis=1, keepdims=True), self_score)
        raised = jnp.exp(masked - peak)
        self_raised = jnp.exp(self_score - peak)
        inverse = 1.0 / (jnp.sum(raised, axis=1, keepdims=True) + self_raised)
        weights = (raised * inverse).astype(jnp.bfloat16)
        self_weight = (self_raised * inverse).astype(jnp.bfloat16).astype(jnp.float32)
        shares.append((weights, self_weight))
    for copy in copies:
        copy.wait()
    for row, (weights, self_weight) in enumerate(shares):
        total = jnp.dot(weights, v_ref[row], preferred_element_type=jnp.float32)
        o_scr[row] = total + self_weight * new_values[row : row + 1]
    half = total_heads // 2
    for head in range(total_heads):
        ref = own_out if head < half else other_out
        column = (head % half) * DH
        ref[:, column : column + DH] = o_scr[:, head, :].astype(jnp.bfloat16)


def attend(core, lengths, own_q, other_q, kv_column, keys, values):
    rows, positions, _ = keys.shape
    heads = 2 * (own_q.shape[1] // DH - 1)
    out = jax.ShapeDtypeStruct((rows, heads * DH // 2), jnp.bfloat16)
    scalars = jnp.concatenate([core[None], lengths])
    return pl.pallas_call(
        functools.partial(attend_kernel, kv_column),
        out_shape=(out, out),
        in_specs=[SMEM] + [VMEM] * 3 + [HBM],
        out_specs=(VMEM, VMEM),
        scratch_shapes=[pltpu.VMEM(values.shape, values.dtype)]
        + [pltpu.VMEM((rows, heads, DH), jnp.float32)] * 2
        + [pltpu.SemaphoreType.DMA((rows,))],
        compiler_params=pltpu.CompilerParams(vmem_limit_bytes=49 * MIB),
        cost_estimate=pl.CostEstimate(
            flops=4 * rows * heads * positions * DH,
            bytes_accessed=4 * rows * positions * DH,
            transcendentals=rows * heads * positions,
        ),
        name="attend",
    )(scalars, own_q, other_q, keys, values)


def output_kernel(orders, rows, columns, pieces, after, ids_ref, *refs):
    count = 2 * len(orders)
    block_refs, w_refs = refs[:count], refs[count : count + len(pieces)]
    send_ref, keep_ref, xs_ref = refs[count + len(pieces) + after :]
    depth = block_refs[0].shape[1]
    me, core = ids_ref[0], ids_ref[1]
    n = len(orders[0])
    half = n // 2
    for group, (near_ref, far_ref) in enumerate(zip(block_refs[::2], block_refs[1::2])):
        for p, j in enumerate(orders[group]):
            block = jnp.bitwise_xor(me, j)
            place = block % half + jnp.where(block // half == core, half, 0)
            source = near_ref if p < half else far_ref
            at = (p % half) * rows
            xs_ref[
                pl.ds(pl.multiple_of(place * rows, rows), rows), group * depth : (group + 1) * depth
            ] = source[at : at + rows, :]
    cut = half * rows
    totals = {}
    for w_ref, ((first, tall), span) in zip(w_refs, pieces):
        part = jnp.dot(
            xs_ref[:, first : first + tall], w_ref[...], preferred_element_type=jnp.float32
        )
        totals[span] = totals[span] + part if span in totals else part
    for (column, width), total in totals.items():
        send_ref[:, column - columns[0] : column - columns[0] + width] = total[:cut]
        keep_ref[:, column - columns[0] : column - columns[0] + width] = total[cut:]


def project_out(orders, rows, ids, blocks, held, cuts, columns, after):
    chosen = [at for at, (_, (column, _)) in enumerate(cuts) if columns[0] <= column < sum(columns)]
    weights, pieces = [held[at] for at in chosen], [cuts[at] for at in chosen]
    pieces, weights = zip(*sorted(zip(pieces, weights), key=lambda pair: (pair[0][1], pair[0][0])))
    depth = len(orders) * blocks[0].shape[1]
    n = len(orders[0])
    out = jax.ShapeDtypeStruct((n * rows // 2, columns[1]), jnp.float32)
    return pl.pallas_call(
        functools.partial(output_kernel, orders, rows, columns, pieces, len(after)),
        out_shape=(out, out),
        in_specs=[SMEM] + [VMEM] * (len(blocks) + len(weights)) + [ANY] * len(after),
        out_specs=(VMEM, VMEM),
        scratch_shapes=[pltpu.VMEM((n * rows, depth), jnp.bfloat16)],
        compiler_params=pltpu.CompilerParams(vmem_limit_bytes=12 * MIB),
        cost_estimate=pl.CostEstimate(
            flops=2 * n * rows * depth * columns[1],
            bytes_accessed=2 * depth * columns[1] + 4 * n * rows * columns[1],
            transcendentals=0,
        ),
        name="project_out",
    )(ids, *blocks, *weights, *after)


def local(tokens, query_weight, kv_weight, out_weight, key_cache, value_cache, lengths):
    n = lax.axis_size("gx")
    me = lax.axis_index("gx").astype(jnp.int32)
    core = lax.axis_index("gy").astype(jnp.int32)
    ids = jnp.stack([me, core])
    own_rows = key_cache.shape[0]
    rows = 2 * own_rows
    bits = [1 << i for i in range(n.bit_length() - 1)]

    def swap(array):
        return lax.ppermute(array, "gy", [(0, 1), (1, 0)])

    def across(array, mask):
        return lax.ppermute(array, "gx", [(g, g ^ mask) for g in range(n)])

    other_tokens = swap(tokens)
    own_tokens = jnp.where(me < n, tokens, jnp.bfloat16(0))
    width = query_weight.shape[1] // 2

    y, z = bits[:1], bits[1:]
    unit = query_weight.shape[1] // 12
    plan = [(3 * unit, z[:1] + y + z[1:]), (5 * unit, y + z), (4 * unit, z + y)]
    state, first, after = [None] * len(plan), 0, []
    for group in ((2,), (0, 1)):
        chunks = [plan[i] for i in group]
        weight = kv_weight if 0 in group else None
        made = project(chunks, rows, ids, own_tokens, other_tokens, query_weight, weight, first, after)
        for i, pair in zip(group, made):
            state[i] = pair
        after = [made[0][0]]
        first += sum(columns for columns, _ in chunks)
    moving = [across(send, order[0]) for (send, _), (_, order) in zip(state, plan)]
    for step in range(len(bits)):
        for i in (2, 0, 1):
            columns, order = plan[i]
            total = state[i][1] + moving[i]
            if step + 1 < len(bits):
                cut = total.shape[0] // 2
                state[i] = (total[cut:], total[:cut])
                moving[i] = across(state[i][0], order[step + 1])
            else:
                state[i] = total
    kv_width = kv_weight.shape[1] // 2
    by_column = [i for group in ((2,), (0, 1)) for i in group]
    total = jnp.concatenate([state[i] for i in by_column], axis=1)
    mine = lax.dynamic_slice_in_dim(total, core * own_rows, own_rows, 0).astype(jnp.bfloat16)
    give = lax.dynamic_slice_in_dim(total, (1 - core) * own_rows, own_rows, 0).astype(jnp.bfloat16)
    kv_column = sum(plan[i][0] for i in by_column[: by_column.index(0)])
    own, other = attend(core, lengths, mine, swap(give), kv_column, key_cache, value_cache)
    got = swap(other)
    block = jnp.where(core == 0, jnp.concatenate([own, got]), jnp.concatenate([got, own]))

    near = [block[:, :width], block[:, width:]]
    far = [None, None]
    paths = [bits[::-1], bits[:1] + bits[:0:-1]]
    out_cuts, out_held = cuts_of(out_weight), []
    early = len(out_cuts) * 9 // 18
    for step in range(len(bits)):
        for i in range(2):
            if step:
                near[i] = jnp.concatenate([near[i], far[i]])
                if i == 0 and out_held:
                    near[i] = near[i] + zero.astype(jnp.bfloat16)
                if i == 1 and step + 2 >= len(bits):
                    part = out_cuts[early:] if out_held else out_cuts[:early]
                    held, zero = load([out_weight], [(0, cut) for cut in part], near, 36, width)
                    out_held += held
            far[i] = across(near[i], paths[i][step])
    orders = [order_of(path[::-1]) for path in paths]
    blocks = [b for pair in zip(near, far) for b in pair]
    send, keep = project_out(orders, rows, ids, blocks, out_held, out_cuts, (0, out_weight.shape[1]), [])
    return (keep + swap(send)).astype(jnp.bfloat16)


def solution(mesh):
    return jax.shard_map(
        local,
        mesh=mesh,
        in_specs=(
            P(("grp", "gy"), "gx"),
            P("gx", "gy"),
            P("gx", None),
            P("gy", "gx"),
            P(("grp", "gx", "gy"), None, None),
            P(("grp", "gx", "gy"), None, None),
            P(("grp", "gx", "gy")),
        ),
        out_specs=P(("grp", "gy"), "gx"),
        check_vma=False,
    )
```

```python
import functools

import jax
import jax.numpy as jnp
from jax import lax
from jax.experimental import pallas as pl
from jax.experimental.pallas import tpu as pltpu
from jax.sharding import PartitionSpec as P

H = 24
DH = 256
MIB = 1024 * 1024
HBM = pl.BlockSpec(memory_space=pltpu.HBM)
ANY = pl.BlockSpec(memory_space=pl.ANY)
VMEM = pl.BlockSpec(memory_space=pltpu.VMEM)
SMEM = pl.BlockSpec(memory_space=pltpu.SMEM)


class InOrder:
    def __init__(self, copies, ahead):
        self.copies, self.ahead = copies, ahead
        for copy in copies[:ahead]:
            copy.start()

    def wait(self, at):
        self.copies[at].wait()
        if at + self.ahead < len(self.copies):
            self.copies[at + self.ahead].start()


def order_of(bits):
    order = [0]
    for bit in reversed(bits):
        order = order + [j + bit for j in order]
    return order


def cuts_of(array):
    if len(array.shape) == 3:
        return [(at, None) for at in range(array.shape[0])]
    depth, columns = array.shape
    tall, wide = 512, (768 if columns % 768 == 0 else columns)
    return [
        ((at, tall), (column, wide)) for at in range(0, depth, tall) for column in range(0, columns, wide)
    ]


def piece_of(array, cut):
    if cut[1] is None:
        shape = array.shape[1:]
    else:
        shape = (cut[0][1], cut[1][1])
    return jax.ShapeDtypeStruct(shape, array.dtype)


def fetches(refs, cuts, targets, sems):
    copies = []
    for ref, cut in cuts:
        source = refs[ref]
        view = source.at[cut[0]] if cut[1] is None else source.at[pl.ds(*cut[0]), pl.ds(*cut[1])]
        copies.append(pltpu.make_async_copy(view, targets[len(copies)], sems.at[len(copies)]))
    return copies


def load_kernel(after, cuts, count, *refs):
    refs = refs[after:]
    in_refs, out_refs, zero_ref, sems = refs[:count], refs[count:-2], refs[-2], refs[-1]
    copies = fetches(in_refs, cuts, out_refs, sems)
    for copy in copies:
        copy.start()
    zero_ref[...] = jnp.zeros_like(zero_ref)
    for copy in copies:
        copy.wait()


def load(arrays, cuts, after, grant, zeros=128):
    shapes = [piece_of(arrays[at], cut) for at, cut in cuts]
    *held, zero = pl.pallas_call(
        functools.partial(load_kernel, len(after), cuts, len(arrays)),
        out_shape=(*shapes, jax.ShapeDtypeStruct((1, zeros), jnp.float32)),
        in_specs=[ANY] * len(after) + [HBM] * len(arrays),
        out_specs=[VMEM] * (len(cuts) + 1),
        scratch_shapes=[pltpu.SemaphoreType.DMA((len(cuts),))],
        compiler_params=pltpu.CompilerParams(vmem_limit_bytes=grant * MIB),
        cost_estimate=pl.CostEstimate(
            flops=0, bytes_accessed=sum(4 * s.shape[0] * s.shape[1] for s in shapes), transcendentals=0
        ),
        name="load",
    )(*after, *arrays)
    return held, zero


def spans_of(width):
    return [(at, min(512, width - at)) for at in range(0, width, 512)]


def project_kernel(orders, rows, first, widths, kv_width, after, ids_ref, own_ref, other_ref, w_ref, *refs):
    refs = list(refs)
    kv_ref = refs.pop(0) if kv_width else None
    outs, (xs_ref, ws_ref, w_sem) = refs[after:-3], refs[-3:]
    n = len(orders[0])
    half = n // 2
    me, core = ids_ref[0], ids_ref[1]
    features = xs_ref.shape[1]

    tiles, copies, at, source = [], [], 0, first
    depth = 768 if features % 768 == 0 else features

    def fetch(from_ref, column, width):
        for part in range(features // depth):
            span = pl.ds(part * depth, depth)
            copies.append(
                pltpu.make_async_copy(
                    from_ref.at[span, pl.ds(column, width)],
                    ws_ref.at[span, pl.ds(at, width)],
                    w_sem.at[len(copies)],
                )
            )

    for chunk, width in enumerate(widths):
        column = 0
        if kv_width and chunk == 0:
            fetch(kv_ref, pl.multiple_of(core * kv_width, kv_width), kv_width)
            tiles.append((chunk, 0, at, kv_width))
            at += kv_width
            column = kv_width
        for offset, tile in spans_of(width):
            fetch(w_ref, source, tile)
            tiles.append((chunk, column + offset, at, tile))
            at += tile
            source += tile
    per_tile = features // depth
    weights = InOrder(copies, 9)
    def place_rows(low_ref, high_ref):
        for j in range(n):
            block = jnp.bitwise_xor(me, j) % half
            source = low_ref if j < half else high_ref
            xs_ref[j * rows : (j + 1) * rows, :] = source[
                pl.ds(pl.multiple_of(block * rows, rows), rows), :
            ]

    low_mine = me // half == core

    @pl.when(low_mine)
    def _():
        place_rows(own_ref, other_ref)

    @pl.when(jnp.logical_not(low_mine))
    def _():
        place_rows(other_ref, own_ref)

    for t, (chunk, column, at, width) in enumerate(tiles):
        for part in range(per_tile):
            weights.wait(t * per_tile + part)
        total = jnp.dot(xs_ref[...], ws_ref[:, at : at + width], preferred_element_type=jnp.float32)
        span = slice(column, column + width)
        for p, j in enumerate(orders[chunk]):
            out = outs[2 * chunk + 1] if p < half else outs[2 * chunk]
            out[(p % half) * rows : (p % half + 1) * rows, span] = total[j * rows : (j + 1) * rows]


def project(plan, rows, ids, tokens, other, query_weight, kv_weight, first, after):
    features = tokens.shape[1]
    orders = [order_of(bits) for _, bits in plan]
    widths = [width for width, _ in plan]
    n = len(orders[0])
    kv_width = kv_weight.shape[1] // 2 if kv_weight is not None else 0
    columns = sum(widths) + kv_width
    outs = []
    for chunk, width in enumerate(widths):
        shape = (n * rows // 2, width + (0 if chunk else kv_width))
        outs += [jax.ShapeDtypeStruct(shape, jnp.float32)] * 2
    weights = [query_weight] + ([kv_weight] if kv_width else [])
    parts = features // 768 if features % 768 == 0 else 1
    copies = parts * (len(weights) - 1 + sum(len(spans_of(width)) for width in widths))
    outs = pl.pallas_call(
        functools.partial(project_kernel, orders, rows, first, widths, kv_width, len(after)),
        out_shape=outs,
        in_specs=[SMEM, VMEM, VMEM] + [HBM] * len(weights) + [ANY] * len(after),
        out_specs=[VMEM] * len(outs),
        scratch_shapes=[
            pltpu.VMEM((n * rows, features), tokens.dtype),
            pltpu.VMEM((features, columns), tokens.dtype),
            pltpu.SemaphoreType.DMA((copies,)),
        ],
        compiler_params=pltpu.CompilerParams(vmem_limit_bytes=46 * MIB),
        cost_estimate=pl.CostEstimate(
            flops=2 * n * rows * features * columns,
            bytes_accessed=2 * features * columns + 4 * n * rows * columns,
            transcendentals=0,
        ),
        name="project",
    )(ids, tokens, other, *weights, *after)
    return list(zip(outs[::2], outs[1::2]))


def attend_kernel(kv_column, scalars_ref, own_q, other_q, *refs):
    k_ref, v_hbm, own_out, other_out, v_ref, q_scr, o_scr, s_scr, sems = refs
    core = scalars_ref[0]
    rows, positions, _ = k_ref.shape
    copies = [pltpu.make_async_copy(v_hbm.at[row], v_ref.at[row], sems.at[row]) for row in range(rows)]
    for copy in copies:
        copy.start()
    at = 0
    for ref in (own_q, other_q):
        for column in range(0, ref.shape[1], DH):
            if column != kv_column:
                q_scr[:, at, :] = DH**-0.5 * ref[:, column : column + DH].astype(jnp.float32)
                at += 1
    total_heads = at
    first = own_q[:, kv_column : kv_column + DH].astype(jnp.float32)
    second = other_q[:, kv_column : kv_column + DH].astype(jnp.float32)
    new_keys = jnp.where(core == 0, first, second)
    new_values = jnp.where(core == 0, second, first)
    own_scores = []
    for row in range(rows):
        query = q_scr[row]
        scores = lax.dot_general(
            query.astype(jnp.bfloat16),
            k_ref[row],
            (((1,), (1,)), ((), ())),
            preferred_element_type=jnp.float32,
        )
        visible = lax.broadcasted_iota(jnp.int32, scores.shape, 1) < scalars_ref[1 + row]
        s_scr[row] = jnp.where(visible, scores, jnp.float32(-1e30))
        own_scores.append(jnp.sum(query * new_keys[row : row + 1], axis=1, keepdims=True))
    self_score = jnp.stack(own_scores)
    masked = s_scr[...]
    peak = jnp.maximum(jnp.max(masked, axis=2, keepdims=True), self_score)
    raised = jnp.exp(masked - peak)
    self_raised = jnp.exp(self_score - peak)
    inverse = 1.0 / (jnp.sum(raised, axis=2, keepdims=True) + self_raised)
    s_scr[...] = raised * inverse
    self_weight = (self_raised * inverse).astype(jnp.bfloat16).astype(jnp.float32)
    for copy in copies:
        copy.wait()
    for row in range(rows):
        weights = s_scr[row].astype(jnp.bfloat16)
        total = jnp.dot(weights, v_ref[row], preferred_element_type=jnp.float32)
        o_scr[row] = total + self_weight[row] * new_values[row : row + 1]
    half = total_heads // 2
    for head in range(total_heads):
        ref = own_out if head < half else other_out
        column = (head % half) * DH
        ref[:, column : column + DH] = o_scr[:, head, :].astype(jnp.bfloat16)


def attend(core, lengths, own_q, other_q, kv_column, keys, values):
    rows, positions, _ = keys.shape
    heads = 2 * (own_q.shape[1] // DH - 1)
    out = jax.ShapeDtypeStruct((rows, heads * DH // 2), jnp.bfloat16)
    scalars = jnp.concatenate([core[None], lengths])
    return pl.pallas_call(
        functools.partial(attend_kernel, kv_column),
        out_shape=(out, out),
        in_specs=[SMEM] + [VMEM] * 3 + [HBM],
        out_specs=(VMEM, VMEM),
        scratch_shapes=[pltpu.VMEM(values.shape, values.dtype)]
        + [pltpu.VMEM((rows, heads, DH), jnp.float32)] * 2
        + [pltpu.VMEM((rows, heads, positions), jnp.float32)]
        + [pltpu.SemaphoreType.DMA((rows,))],
        compiler_params=pltpu.CompilerParams(vmem_limit_bytes=49 * MIB),
        cost_estimate=pl.CostEstimate(
            flops=4 * rows * heads * positions * DH,
            bytes_accessed=4 * rows * positions * DH,
            transcendentals=rows * heads * positions,
        ),
        name="attend",
    )(scalars, own_q, other_q, keys, values)


def output_kernel(orders, rows, columns, pieces, after, ids_ref, *refs):
    count = 2 * len(orders)
    block_refs, w_refs = refs[:count], refs[count : count + len(pieces)]
    send_ref, keep_ref, xs_ref = refs[count + len(pieces) + after :]
    depth = block_refs[0].shape[1]
    me, core = ids_ref[0], ids_ref[1]
    n = len(orders[0])
    half = n // 2
    for group, (near_ref, far_ref) in enumerate(zip(block_refs[::2], block_refs[1::2])):
        for p, j in enumerate(orders[group]):
            block = jnp.bitwise_xor(me, j)
            place = block % half + jnp.where(block // half == core, half, 0)
            source = near_ref if p < half else far_ref
            at = (p % half) * rows
            xs_ref[
                pl.ds(pl.multiple_of(place * rows, rows), rows), group * depth : (group + 1) * depth
            ] = source[at : at + rows, :]
    cut = half * rows
    totals = {}
    for w_ref, ((first, tall), span) in zip(w_refs, pieces):
        part = jnp.dot(
            xs_ref[:, first : first + tall], w_ref[...], preferred_element_type=jnp.float32
        )
        totals[span] = totals[span] + part if span in totals else part
    for (column, width), total in totals.items():
        send_ref[:, column - columns[0] : column - columns[0] + width] = total[:cut]
        keep_ref[:, column - columns[0] : column - columns[0] + width] = total[cut:]


def project_out(orders, rows, ids, blocks, held, cuts, columns, after):
    chosen = [at for at, (_, (column, _)) in enumerate(cuts) if columns[0] <= column < sum(columns)]
    weights, pieces = [held[at] for at in chosen], [cuts[at] for at in chosen]
    pieces, weights = zip(*sorted(zip(pieces, weights), key=lambda pair: (pair[0][1], pair[0][0])))
    depth = len(orders) * blocks[0].shape[1]
    n = len(orders[0])
    out = jax.ShapeDtypeStruct((n * rows // 2, columns[1]), jnp.float32)
    return pl.pallas_call(
        functools.partial(output_kernel, orders, rows, columns, pieces, len(after)),
        out_shape=(out, out),
        in_specs=[SMEM] + [VMEM] * (len(blocks) + len(weights)) + [ANY] * len(after),
        out_specs=(VMEM, VMEM),
        scratch_shapes=[pltpu.VMEM((n * rows, depth), jnp.bfloat16)],
        compiler_params=pltpu.CompilerParams(vmem_limit_bytes=12 * MIB),
        cost_estimate=pl.CostEstimate(
            flops=2 * n * rows * depth * columns[1],
            bytes_accessed=2 * depth * columns[1] + 4 * n * rows * columns[1],
            transcendentals=0,
        ),
        name="project_out",
    )(ids, *blocks, *weights, *after)


def local(tokens, query_weight, kv_weight, out_weight, key_cache, value_cache, lengths):
    n = lax.axis_size("gx")
    me = lax.axis_index("gx").astype(jnp.int32)
    core = lax.axis_index("gy").astype(jnp.int32)
    ids = jnp.stack([me, core])
    own_rows = key_cache.shape[0]
    rows = 2 * own_rows
    bits = [1 << i for i in range(n.bit_length() - 1)]

    def swap(array):
        return lax.ppermute(array, "gy", [(0, 1), (1, 0)])

    def across(array, mask):
        return lax.ppermute(array, "gx", [(g, g ^ mask) for g in range(n)])

    other_tokens = swap(tokens)
    own_tokens = jnp.where(me < n, tokens, jnp.bfloat16(0))
    width = query_weight.shape[1] // 2

    y, z = bits[:1], bits[1:]
    unit = query_weight.shape[1] // 12
    plan = [(3 * unit, z[:1] + y + z[1:]), (5 * unit, y + z), (4 * unit, z + y)]
    state, first, after = [None] * len(plan), 0, []
    for group in ((2,), (0, 1)):
        chunks = [plan[i] for i in group]
        weight = kv_weight if 0 in group else None
        made = project(chunks, rows, ids, own_tokens, other_tokens, query_weight, weight, first, after)
        for i, pair in zip(group, made):
            state[i] = pair
        after = [made[0][0]]
        first += sum(columns for columns, _ in chunks)
    moving = [across(send, order[0]) for (send, _), (_, order) in zip(state, plan)]
    for step in range(len(bits)):
        for i in (2, 0, 1):
            columns, order = plan[i]
            total = state[i][1] + moving[i]
            if step + 1 < len(bits):
                cut = total.shape[0] // 2
                state[i] = (total[cut:], total[:cut])
                moving[i] = across(state[i][0], order[step + 1])
            else:
                state[i] = total
    kv_width = kv_weight.shape[1] // 2
    by_column = [i for group in ((2,), (0, 1)) for i in group]
    total = jnp.concatenate([state[i] for i in by_column], axis=1)
    mine = lax.dynamic_slice_in_dim(total, core * own_rows, own_rows, 0).astype(jnp.bfloat16)
    give = lax.dynamic_slice_in_dim(total, (1 - core) * own_rows, own_rows, 0).astype(jnp.bfloat16)
    kv_column = sum(plan[i][0] for i in by_column[: by_column.index(0)])
    own, other = attend(core, lengths, mine, swap(give), kv_column, key_cache, value_cache)
    got = swap(other)
    block = jnp.where(core == 0, jnp.concatenate([own, got]), jnp.concatenate([got, own]))

    near = [block[:, :width], block[:, width:]]
    far = [None, None]
    paths = [bits[::-1], bits[:1] + bits[:0:-1]]
    out_cuts, out_held = cuts_of(out_weight), []
    early = len(out_cuts) * 9 // 18
    for step in range(len(bits)):
        for i in range(2):
            if step:
                near[i] = jnp.concatenate([near[i], far[i]])
                if i == 0 and out_held:
                    near[i] = near[i] + zero.astype(jnp.bfloat16)
                if i == 1 and step + 2 >= len(bits):
                    part = out_cuts[early:] if out_held else out_cuts[:early]
                    held, zero = load([out_weight], [(0, cut) for cut in part], near, 36, width)
                    out_held += held
            far[i] = across(near[i], paths[i][step])
    orders = [order_of(path[::-1]) for path in paths]
    blocks = [b for pair in zip(near, far) for b in pair]
    send, keep = project_out(orders, rows, ids, blocks, out_held, out_cuts, (0, out_weight.shape[1]), [])
    return (keep + swap(send)).astype(jnp.bfloat16)


def solution(mesh):
    return jax.shard_map(
        local,
        mesh=mesh,
        in_specs=(
            P(("grp", "gy"), "gx"),
            P("gx", "gy"),
            P("gx", None),
            P("gy", "gx"),
            P(("grp", "gx", "gy"), None, None),
            P(("grp", "gx", "gy"), None, None),
            P(("grp", "gx", "gy")),
        ),
        out_specs=P(("grp", "gy"), "gx"),
        check_vma=False,
    )
```

```python
import functools

import jax
import jax.numpy as jnp
from jax import lax
from jax.experimental import pallas as pl
from jax.experimental.pallas import tpu as pltpu
from jax.sharding import PartitionSpec as P

H = 24
DH = 256
MIB = 1024 * 1024
HBM = pl.BlockSpec(memory_space=pltpu.HBM)
ANY = pl.BlockSpec(memory_space=pl.ANY)
VMEM = pl.BlockSpec(memory_space=pltpu.VMEM)
SMEM = pl.BlockSpec(memory_space=pltpu.SMEM)


class InOrder:
    def __init__(self, copies, ahead):
        self.copies, self.ahead = copies, ahead
        for copy in copies[:ahead]:
            copy.start()

    def wait(self, at):
        self.copies[at].wait()
        if at + self.ahead < len(self.copies):
            self.copies[at + self.ahead].start()


def order_of(bits):
    order = [0]
    for bit in reversed(bits):
        order = order + [j + bit for j in order]
    return order


def cuts_of(array):
    if len(array.shape) == 3:
        return [(at, None) for at in range(array.shape[0])]
    depth, columns = array.shape
    tall, wide = 512, (768 if columns % 768 == 0 else columns)
    return [
        ((at, tall), (column, wide)) for at in range(0, depth, tall) for column in range(0, columns, wide)
    ]


def piece_of(array, cut):
    if cut[1] is None:
        shape = array.shape[1:]
    else:
        shape = (cut[0][1], cut[1][1])
    return jax.ShapeDtypeStruct(shape, array.dtype)


def fetches(refs, cuts, targets, sems):
    copies = []
    for ref, cut in cuts:
        source = refs[ref]
        view = source.at[cut[0]] if cut[1] is None else source.at[pl.ds(*cut[0]), pl.ds(*cut[1])]
        copies.append(pltpu.make_async_copy(view, targets[len(copies)], sems.at[len(copies)]))
    return copies


def load_kernel(after, cuts, count, *refs):
    refs = refs[after:]
    in_refs, out_refs, zero_ref, sems = refs[:count], refs[count:-2], refs[-2], refs[-1]
    copies = fetches(in_refs, cuts, out_refs, sems)
    for copy in copies:
        copy.start()
    zero_ref[...] = jnp.zeros_like(zero_ref)
    for copy in copies:
        copy.wait()


def load(arrays, cuts, after, grant, zeros=128):
    shapes = [piece_of(arrays[at], cut) for at, cut in cuts]
    *held, zero = pl.pallas_call(
        functools.partial(load_kernel, len(after), cuts, len(arrays)),
        out_shape=(*shapes, jax.ShapeDtypeStruct((1, zeros), jnp.float32)),
        in_specs=[ANY] * len(after) + [HBM] * len(arrays),
        out_specs=[VMEM] * (len(cuts) + 1),
        scratch_shapes=[pltpu.SemaphoreType.DMA((len(cuts),))],
        compiler_params=pltpu.CompilerParams(vmem_limit_bytes=grant * MIB),
        cost_estimate=pl.CostEstimate(
            flops=0, bytes_accessed=sum(4 * s.shape[0] * s.shape[1] for s in shapes), transcendentals=0
        ),
        name="load",
    )(*after, *arrays)
    return held, zero


def spans_of(width):
    return [(at, min(512, width - at)) for at in range(0, width, 512)]


def project_kernel(orders, rows, first, widths, kv_width, after, ids_ref, own_ref, other_ref, w_ref, *refs):
    refs = list(refs)
    kv_ref = refs.pop(0) if kv_width else None
    outs, (xs_ref, ws_ref, w_sem) = refs[after:-3], refs[-3:]
    n = len(orders[0])
    half = n // 2
    me, core = ids_ref[0], ids_ref[1]
    features = xs_ref.shape[1]

    tiles, copies, at, source = [], [], 0, first
    depth = 768 if features % 768 == 0 else features

    def fetch(from_ref, column, width):
        for part in range(features // depth):
            span = pl.ds(part * depth, depth)
            copies.append(
                pltpu.make_async_copy(
                    from_ref.at[span, pl.ds(column, width)],
                    ws_ref.at[span, pl.ds(at, width)],
                    w_sem.at[len(copies)],
                )
            )

    for chunk, width in enumerate(widths):
        column = 0
        if kv_width and chunk == 0:
            fetch(kv_ref, pl.multiple_of(core * kv_width, kv_width), kv_width)
            tiles.append((chunk, 0, at, kv_width))
            at += kv_width
            column = kv_width
        for offset, tile in spans_of(width):
            fetch(w_ref, source, tile)
            tiles.append((chunk, column + offset, at, tile))
            at += tile
            source += tile
    per_tile = features // depth
    weights = InOrder(copies, 9)
    def place_rows(low_ref, high_ref):
        for j in range(n):
            block = jnp.bitwise_xor(me, j) % half
            source = low_ref if j < half else high_ref
            xs_ref[j * rows : (j + 1) * rows, :] = source[
                pl.ds(pl.multiple_of(block * rows, rows), rows), :
            ]

    low_mine = me // half == core

    @pl.when(low_mine)
    def _():
        place_rows(own_ref, other_ref)

    @pl.when(jnp.logical_not(low_mine))
    def _():
        place_rows(other_ref, own_ref)

    for t, (chunk, column, at, width) in enumerate(tiles):
        for part in range(per_tile):
            weights.wait(t * per_tile + part)
        total = jnp.dot(xs_ref[...], ws_ref[:, at : at + width], preferred_element_type=jnp.float32)
        span = slice(column, column + width)
        for p, j in enumerate(orders[chunk]):
            out = outs[2 * chunk + 1] if p < half else outs[2 * chunk]
            out[(p % half) * rows : (p % half + 1) * rows, span] = total[j * rows : (j + 1) * rows]


def project(plan, rows, ids, tokens, other, query_weight, kv_weight, first, after):
    features = tokens.shape[1]
    orders = [order_of(bits) for _, bits in plan]
    widths = [width for width, _ in plan]
    n = len(orders[0])
    kv_width = kv_weight.shape[1] // 2 if kv_weight is not None else 0
    columns = sum(widths) + kv_width
    outs = []
    for chunk, width in enumerate(widths):
        shape = (n * rows // 2, width + (0 if chunk else kv_width))
        outs += [jax.ShapeDtypeStruct(shape, jnp.float32)] * 2
    weights = [query_weight] + ([kv_weight] if kv_width else [])
    parts = features // 768 if features % 768 == 0 else 1
    copies = parts * (len(weights) - 1 + sum(len(spans_of(width)) for width in widths))
    outs = pl.pallas_call(
        functools.partial(project_kernel, orders, rows, first, widths, kv_width, len(after)),
        out_shape=outs,
        in_specs=[SMEM, VMEM, VMEM] + [HBM] * len(weights) + [ANY] * len(after),
        out_specs=[VMEM] * len(outs),
        scratch_shapes=[
            pltpu.VMEM((n * rows, features), tokens.dtype),
            pltpu.VMEM((features, columns), tokens.dtype),
            pltpu.SemaphoreType.DMA((copies,)),
        ],
        compiler_params=pltpu.CompilerParams(vmem_limit_bytes=46 * MIB),
        cost_estimate=pl.CostEstimate(
            flops=2 * n * rows * features * columns,
            bytes_accessed=2 * features * columns + 4 * n * rows * columns,
            transcendentals=0,
        ),
        name="project",
    )(ids, tokens, other, *weights, *after)
    return list(zip(outs[::2], outs[1::2]))


def attend_kernel(kv_column, scalars_ref, own_q, other_q, *refs):
    k_ref, v_hbm, own_out, other_out, v_ref, q_scr, o_scr, sems = refs
    core = scalars_ref[0]
    rows, positions, _ = k_ref.shape
    copies = [pltpu.make_async_copy(v_hbm.at[row], v_ref.at[row], sems.at[row]) for row in range(rows)]
    for copy in copies:
        copy.start()
    at = 0
    for ref in (own_q, other_q):
        for column in range(0, ref.shape[1], DH):
            if column != kv_column:
                q_scr[:, at, :] = DH**-0.5 * ref[:, column : column + DH].astype(jnp.float32)
                at += 1
    total_heads = at
    first = own_q[:, kv_column : kv_column + DH].astype(jnp.float32)
    second = other_q[:, kv_column : kv_column + DH].astype(jnp.float32)
    new_keys = jnp.where(core == 0, first, second)
    new_values = jnp.where(core == 0, second, first)
    group = max(g for g in range(1, rows + 1) if rows % g == 0 and g * total_heads <= 128)
    lane = lax.broadcasted_iota(jnp.int32, (1, 128), 1)
    place = lax.broadcasted_iota(jnp.int32, (positions, 128), 0)
    shares = []
    for base in range(0, rows, group):
        members = range(base, base + group)
        queries = jnp.concatenate(
            [q_scr[row] for row in members]
            + [jnp.zeros((128 - group * total_heads, DH), jnp.float32)] * (group * total_heads < 128)
        ).T
        columns, lengths = [], jnp.zeros((1, 128), jnp.int32)
        for at, row in enumerate(members):
            own = (lane >= at * total_heads) & (lane < (at + 1) * total_heads)
            columns.append(jnp.where(own, queries, 0.0).astype(jnp.bfloat16))
            lengths = jnp.where(own, scalars_ref[1 + row], lengths)
        columns = jnp.concatenate(columns)
        keys = jnp.concatenate([k_ref[row] for row in members], axis=1)
        scores = jnp.dot(keys, columns, preferred_element_type=jnp.float32)
        fresh = jnp.concatenate([new_keys[row : row + 1] for row in members], axis=1).astype(jnp.bfloat16)
        self_score = jnp.dot(
            jnp.broadcast_to(fresh, (16, group * DH)), columns, preferred_element_type=jnp.float32
        )[:1]
        masked = jnp.where(place < lengths, scores, jnp.float32(-1e30))
        peak = jnp.maximum(jnp.max(masked, axis=0, keepdims=True), self_score)
        raised = jnp.exp(masked - peak)
        self_raised = jnp.exp(self_score - peak)
        inverse = 1.0 / (jnp.sum(raised, axis=0, keepdims=True) + self_raised)
        weights = (raised * inverse).T
        self_weights = jnp.broadcast_to(self_raised * inverse, (128, 128)).T
        for at, row in enumerate(members):
            span = slice(at * total_heads, (at + 1) * total_heads)
            self_weight = self_weights[span, :1].astype(jnp.bfloat16).astype(jnp.float32)
            shares.append((weights[span].astype(jnp.bfloat16), self_weight))
    for copy in copies:
        copy.wait()
    for row, (weights, self_weight) in enumerate(shares):
        total = jnp.dot(weights, v_ref[row], preferred_element_type=jnp.float32)
        o_scr[row] = total + self_weight * new_values[row : row + 1]
    half = total_heads // 2
    for head in range(total_heads):
        ref = own_out if head < half else other_out
        column = (head % half) * DH
        ref[:, column : column + DH] = o_scr[:, head, :].astype(jnp.bfloat16)


def attend(core, lengths, own_q, other_q, kv_column, keys, values):
    rows, positions, _ = keys.shape
    heads = 2 * (own_q.shape[1] // DH - 1)
    out = jax.ShapeDtypeStruct((rows, heads * DH // 2), jnp.bfloat16)
    scalars = jnp.concatenate([core[None], lengths])
    return pl.pallas_call(
        functools.partial(attend_kernel, kv_column),
        out_shape=(out, out),
        in_specs=[SMEM] + [VMEM] * 3 + [HBM],
        out_specs=(VMEM, VMEM),
        scratch_shapes=[pltpu.VMEM(values.shape, values.dtype)]
        + [pltpu.VMEM((rows, heads, DH), jnp.float32)] * 2
        + [pltpu.SemaphoreType.DMA((rows,))],
        compiler_params=pltpu.CompilerParams(vmem_limit_bytes=49 * MIB),
        cost_estimate=pl.CostEstimate(
            flops=4 * rows * heads * positions * DH,
            bytes_accessed=4 * rows * positions * DH,
            transcendentals=rows * heads * positions,
        ),
        name="attend",
    )(scalars, own_q, other_q, keys, values)


def output_kernel(orders, rows, columns, pieces, after, ids_ref, *refs):
    count = 2 * len(orders)
    block_refs, w_refs = refs[:count], refs[count : count + len(pieces)]
    send_ref, keep_ref, xs_ref = refs[count + len(pieces) + after :]
    depth = block_refs[0].shape[1]
    me, core = ids_ref[0], ids_ref[1]
    n = len(orders[0])
    half = n // 2
    for group, (near_ref, far_ref) in enumerate(zip(block_refs[::2], block_refs[1::2])):
        for p, j in enumerate(orders[group]):
            block = jnp.bitwise_xor(me, j)
            place = block % half + jnp.where(block // half == core, half, 0)
            source = near_ref if p < half else far_ref
            at = (p % half) * rows
            xs_ref[
                pl.ds(pl.multiple_of(place * rows, rows), rows), group * depth : (group + 1) * depth
            ] = source[at : at + rows, :]
    cut = half * rows
    totals = {}
    for w_ref, ((first, tall), span) in zip(w_refs, pieces):
        part = jnp.dot(
            xs_ref[:, first : first + tall], w_ref[...], preferred_element_type=jnp.float32
        )
        totals[span] = totals[span] + part if span in totals else part
    for (column, width), total in totals.items():
        send_ref[:, column - columns[0] : column - columns[0] + width] = total[:cut]
        keep_ref[:, column - columns[0] : column - columns[0] + width] = total[cut:]


def project_out(orders, rows, ids, blocks, held, cuts, columns, after):
    chosen = [at for at, (_, (column, _)) in enumerate(cuts) if columns[0] <= column < sum(columns)]
    weights, pieces = [held[at] for at in chosen], [cuts[at] for at in chosen]
    pieces, weights = zip(*sorted(zip(pieces, weights), key=lambda pair: (pair[0][1], pair[0][0])))
    depth = len(orders) * blocks[0].shape[1]
    n = len(orders[0])
    out = jax.ShapeDtypeStruct((n * rows // 2, columns[1]), jnp.float32)
    return pl.pallas_call(
        functools.partial(output_kernel, orders, rows, columns, pieces, len(after)),
        out_shape=(out, out),
        in_specs=[SMEM] + [VMEM] * (len(blocks) + len(weights)) + [ANY] * len(after),
        out_specs=(VMEM, VMEM),
        scratch_shapes=[pltpu.VMEM((n * rows, depth), jnp.bfloat16)],
        compiler_params=pltpu.CompilerParams(vmem_limit_bytes=12 * MIB),
        cost_estimate=pl.CostEstimate(
            flops=2 * n * rows * depth * columns[1],
            bytes_accessed=2 * depth * columns[1] + 4 * n * rows * columns[1],
            transcendentals=0,
        ),
        name="project_out",
    )(ids, *blocks, *weights, *after)


def local(tokens, query_weight, kv_weight, out_weight, key_cache, value_cache, lengths):
    n = lax.axis_size("gx")
    me = lax.axis_index("gx").astype(jnp.int32)
    core = lax.axis_index("gy").astype(jnp.int32)
    ids = jnp.stack([me, core])
    own_rows = key_cache.shape[0]
    rows = 2 * own_rows
    bits = [1 << i for i in range(n.bit_length() - 1)]

    def swap(array):
        return lax.ppermute(array, "gy", [(0, 1), (1, 0)])

    def across(array, mask):
        return lax.ppermute(array, "gx", [(g, g ^ mask) for g in range(n)])

    other_tokens = swap(tokens)
    own_tokens = jnp.where(me < n, tokens, jnp.bfloat16(0))
    width = query_weight.shape[1] // 2

    y, z = bits[:1], bits[1:]
    unit = query_weight.shape[1] // 12
    plan = [(3 * unit, z[:1] + y + z[1:]), (5 * unit, y + z), (4 * unit, z + y)]
    state, first, after = [None] * len(plan), 0, []
    for group in ((2,), (0, 1)):
        chunks = [plan[i] for i in group]
        weight = kv_weight if 0 in group else None
        made = project(chunks, rows, ids, own_tokens, other_tokens, query_weight, weight, first, after)
        for i, pair in zip(group, made):
            state[i] = pair
        after = [made[0][0]]
        first += sum(columns for columns, _ in chunks)
    moving = [across(send, order[0]) for (send, _), (_, order) in zip(state, plan)]
    for step in range(len(bits)):
        for i in (2, 0, 1):
            columns, order = plan[i]
            total = state[i][1] + moving[i]
            if step + 1 < len(bits):
                cut = total.shape[0] // 2
                state[i] = (total[cut:], total[:cut])
                moving[i] = across(state[i][0], order[step + 1])
            else:
                state[i] = total
    kv_width = kv_weight.shape[1] // 2
    by_column = [i for group in ((2,), (0, 1)) for i in group]
    total = jnp.concatenate([state[i] for i in by_column], axis=1)
    mine = lax.dynamic_slice_in_dim(total, core * own_rows, own_rows, 0).astype(jnp.bfloat16)
    give = lax.dynamic_slice_in_dim(total, (1 - core) * own_rows, own_rows, 0).astype(jnp.bfloat16)
    kv_column = sum(plan[i][0] for i in by_column[: by_column.index(0)])
    own, other = attend(core, lengths, mine, swap(give), kv_column, key_cache, value_cache)
    got = swap(other)
    block = jnp.where(core == 0, jnp.concatenate([own, got]), jnp.concatenate([got, own]))

    near = [block[:, :width], block[:, width:]]
    far = [None, None]
    paths = [bits[::-1], bits[:1] + bits[:0:-1]]
    out_cuts, out_held = cuts_of(out_weight), []
    early = len(out_cuts) * 9 // 18
    for step in range(len(bits)):
        for i in range(2):
            if step:
                near[i] = jnp.concatenate([near[i], far[i]])
                if i == 0 and out_held:
                    near[i] = near[i] + zero.astype(jnp.bfloat16)
                if i == 1 and step + 2 >= len(bits):
                    part = out_cuts[early:] if out_held else out_cuts[:early]
                    held, zero = load([out_weight], [(0, cut) for cut in part], near, 36, width)
                    out_held += held
            far[i] = across(near[i], paths[i][step])
    orders = [order_of(path[::-1]) for path in paths]
    blocks = [b for pair in zip(near, far) for b in pair]
    send, keep = project_out(orders, rows, ids, blocks, out_held, out_cuts, (0, out_weight.shape[1]), [])
    return (keep + swap(send)).astype(jnp.bfloat16)


def solution(mesh):
    return jax.shard_map(
        local,
        mesh=mesh,
        in_specs=(
            P(("grp", "gy"), "gx"),
            P("gx", "gy"),
            P("gx", None),
            P("gy", "gx"),
            P(("grp", "gx", "gy"), None, None),
            P(("grp", "gx", "gy"), None, None),
            P(("grp", "gx", "gy")),
        ),
        out_specs=P(("grp", "gy"), "gx"),
        check_vma=False,
    )
```

```python
import functools

import jax
import jax.numpy as jnp
from jax import lax
from jax.experimental import pallas as pl
from jax.experimental.pallas import tpu as pltpu
from jax.sharding import PartitionSpec as P

H = 24
DH = 256
MIB = 1024 * 1024
HBM = pl.BlockSpec(memory_space=pltpu.HBM)
ANY = pl.BlockSpec(memory_space=pl.ANY)
VMEM = pl.BlockSpec(memory_space=pltpu.VMEM)
SMEM = pl.BlockSpec(memory_space=pltpu.SMEM)


class InOrder:
    def __init__(self, copies, ahead):
        self.copies, self.ahead = copies, ahead
        for copy in copies[:ahead]:
            copy.start()

    def wait(self, at):
        self.copies[at].wait()
        if at + self.ahead < len(self.copies):
            self.copies[at + self.ahead].start()


def order_of(bits):
    order = [0]
    for bit in reversed(bits):
        order = order + [j + bit for j in order]
    return order


def cuts_of(array):
    if len(array.shape) == 3:
        return [(at, None) for at in range(array.shape[0])]
    depth, columns = array.shape
    tall, wide = 512, (768 if columns % 768 == 0 else columns)
    return [
        ((at, tall), (column, wide)) for at in range(0, depth, tall) for column in range(0, columns, wide)
    ]


def piece_of(array, cut):
    if cut[1] is None:
        shape = array.shape[1:]
    else:
        shape = (cut[0][1], cut[1][1])
    return jax.ShapeDtypeStruct(shape, array.dtype)


def fetches(refs, cuts, targets, sems):
    copies = []
    for ref, cut in cuts:
        source = refs[ref]
        view = source.at[cut[0]] if cut[1] is None else source.at[pl.ds(*cut[0]), pl.ds(*cut[1])]
        copies.append(pltpu.make_async_copy(view, targets[len(copies)], sems.at[len(copies)]))
    return copies


def load_kernel(after, cuts, count, *refs):
    refs = refs[after:]
    in_refs, out_refs, zero_ref, sems = refs[:count], refs[count:-2], refs[-2], refs[-1]
    copies = fetches(in_refs, cuts, out_refs, sems)
    for copy in copies:
        copy.start()
    zero_ref[...] = jnp.zeros_like(zero_ref)
    for copy in copies:
        copy.wait()


def load(arrays, cuts, after, grant, zeros=128):
    shapes = [piece_of(arrays[at], cut) for at, cut in cuts]
    *held, zero = pl.pallas_call(
        functools.partial(load_kernel, len(after), cuts, len(arrays)),
        out_shape=(*shapes, jax.ShapeDtypeStruct((1, zeros), jnp.float32)),
        in_specs=[ANY] * len(after) + [HBM] * len(arrays),
        out_specs=[VMEM] * (len(cuts) + 1),
        scratch_shapes=[pltpu.SemaphoreType.DMA((len(cuts),))],
        compiler_params=pltpu.CompilerParams(vmem_limit_bytes=grant * MIB),
        cost_estimate=pl.CostEstimate(
            flops=0, bytes_accessed=sum(4 * s.shape[0] * s.shape[1] for s in shapes), transcendentals=0
        ),
        name="load",
    )(*after, *arrays)
    return held, zero


def spans_of(width):
    return [(at, min(512, width - at)) for at in range(0, width, 512)]


def project_kernel(orders, rows, first, widths, kv_width, after, ids_ref, own_ref, other_ref, w_ref, *refs):
    refs = list(refs)
    kv_ref = refs.pop(0) if kv_width else None
    outs, (xs_ref, ws_ref, w_sem) = refs[after:-3], refs[-3:]
    n = len(orders[0])
    half = n // 2
    me, core = ids_ref[0], ids_ref[1]
    features = xs_ref.shape[1]

    tiles, copies, at, source = [], [], 0, first
    depth = 768 if features % 768 == 0 else features

    def fetch(from_ref, column, width):
        for part in range(features // depth):
            span = pl.ds(part * depth, depth)
            copies.append(
                pltpu.make_async_copy(
                    from_ref.at[span, pl.ds(column, width)],
                    ws_ref.at[span, pl.ds(at, width)],
                    w_sem.at[len(copies)],
                )
            )

    for chunk, width in enumerate(widths):
        column = 0
        if kv_width and chunk == 0:
            fetch(kv_ref, pl.multiple_of(core * kv_width, kv_width), kv_width)
            tiles.append((chunk, 0, at, kv_width))
            at += kv_width
            column = kv_width
        for offset, tile in spans_of(width):
            fetch(w_ref, source, tile)
            tiles.append((chunk, column + offset, at, tile))
            at += tile
            source += tile
    per_tile = features // depth
    weights = InOrder(copies, 9)
    def place_rows(low_ref, high_ref):
        for j in range(n):
            block = jnp.bitwise_xor(me, j) % half
            source = low_ref if j < half else high_ref
            xs_ref[j * rows : (j + 1) * rows, :] = source[
                pl.ds(pl.multiple_of(block * rows, rows), rows), :
            ]

    low_mine = me // half == core

    @pl.when(low_mine)
    def _():
        place_rows(own_ref, other_ref)

    @pl.when(jnp.logical_not(low_mine))
    def _():
        place_rows(other_ref, own_ref)

    for t, (chunk, column, at, width) in enumerate(tiles):
        for part in range(per_tile):
            weights.wait(t * per_tile + part)
        total = jnp.dot(xs_ref[...], ws_ref[:, at : at + width], preferred_element_type=jnp.float32)
        span = slice(column, column + width)
        for p, j in enumerate(orders[chunk]):
            out = outs[2 * chunk + 1] if p < half else outs[2 * chunk]
            out[(p % half) * rows : (p % half + 1) * rows, span] = total[j * rows : (j + 1) * rows]


def project(plan, rows, ids, tokens, other, query_weight, kv_weight, first, after):
    features = tokens.shape[1]
    orders = [order_of(bits) for _, bits in plan]
    widths = [width for width, _ in plan]
    n = len(orders[0])
    kv_width = kv_weight.shape[1] // 2 if kv_weight is not None else 0
    columns = sum(widths) + kv_width
    outs = []
    for chunk, width in enumerate(widths):
        shape = (n * rows // 2, width + (0 if chunk else kv_width))
        outs += [jax.ShapeDtypeStruct(shape, jnp.float32)] * 2
    weights = [query_weight] + ([kv_weight] if kv_width else [])
    parts = features // 768 if features % 768 == 0 else 1
    copies = parts * (len(weights) - 1 + sum(len(spans_of(width)) for width in widths))
    outs = pl.pallas_call(
        functools.partial(project_kernel, orders, rows, first, widths, kv_width, len(after)),
        out_shape=outs,
        in_specs=[SMEM, VMEM, VMEM] + [HBM] * len(weights) + [ANY] * len(after),
        out_specs=[VMEM] * len(outs),
        scratch_shapes=[
            pltpu.VMEM((n * rows, features), tokens.dtype),
            pltpu.VMEM((features, columns), tokens.dtype),
            pltpu.SemaphoreType.DMA((copies,)),
        ],
        compiler_params=pltpu.CompilerParams(vmem_limit_bytes=46 * MIB),
        cost_estimate=pl.CostEstimate(
            flops=2 * n * rows * features * columns,
            bytes_accessed=2 * features * columns + 4 * n * rows * columns,
            transcendentals=0,
        ),
        name="project",
    )(ids, tokens, other, *weights, *after)
    return list(zip(outs[::2], outs[1::2]))


def attend_kernel(kv_column, scalars_ref, own_q, other_q, *refs):
    k_ref, refs = refs[0], refs[1:]
    v_refs, (own_out, other_out, q_scr, o_scr) = refs[:-4], refs[-4:]
    core = scalars_ref[0]
    rows, positions, _ = k_ref.shape
    at = 0
    for ref in (own_q, other_q):
        for column in range(0, ref.shape[1], DH):
            if column != kv_column:
                q_scr[:, at, :] = DH**-0.5 * ref[:, column : column + DH].astype(jnp.float32)
                at += 1
    total_heads = at
    first = own_q[:, kv_column : kv_column + DH].astype(jnp.float32)
    second = other_q[:, kv_column : kv_column + DH].astype(jnp.float32)
    new_keys = jnp.where(core == 0, first, second)
    new_values = jnp.where(core == 0, second, first)
    group = max(g for g in range(1, rows + 1) if rows % g == 0 and g * total_heads <= 128)
    lane = lax.broadcasted_iota(jnp.int32, (1, 128), 1)
    place = lax.broadcasted_iota(jnp.int32, (positions, 128), 0)
    shares = []
    for base in range(0, rows, group):
        members = range(base, base + group)
        queries = jnp.concatenate(
            [q_scr[row] for row in members]
            + [jnp.zeros((128 - group * total_heads, DH), jnp.float32)] * (group * total_heads < 128)
        ).T
        columns, lengths = [], jnp.zeros((1, 128), jnp.int32)
        for at, row in enumerate(members):
            own = (lane >= at * total_heads) & (lane < (at + 1) * total_heads)
            columns.append(jnp.where(own, queries, 0.0).astype(jnp.bfloat16))
            lengths = jnp.where(own, scalars_ref[1 + row], lengths)
        columns = jnp.concatenate(columns)
        keys = jnp.concatenate([k_ref[row] for row in members], axis=1)
        scores = jnp.dot(keys, columns, preferred_element_type=jnp.float32)
        fresh = jnp.concatenate([new_keys[row : row + 1] for row in members], axis=1).astype(jnp.bfloat16)
        self_score = jnp.dot(
            jnp.broadcast_to(fresh, (16, group * DH)), columns, preferred_element_type=jnp.float32
        )[:1]
        masked = jnp.where(place < lengths, scores, jnp.float32(-1e30))
        peak = jnp.maximum(jnp.max(masked, axis=0, keepdims=True), self_score)
        raised = jnp.exp(masked - peak)
        self_raised = jnp.exp(self_score - peak)
        inverse = 1.0 / (jnp.sum(raised, axis=0, keepdims=True) + self_raised)
        weights = (raised * inverse).T
        self_weights = jnp.broadcast_to(self_raised * inverse, (128, 128)).T
        for at, row in enumerate(members):
            span = slice(at * total_heads, (at + 1) * total_heads)
            self_weight = self_weights[span, :1].astype(jnp.bfloat16).astype(jnp.float32)
            shares.append((weights[span].astype(jnp.bfloat16), self_weight))
    for row, (weights, self_weight) in enumerate(shares):
        total = jnp.dot(weights, v_refs[row][...], preferred_element_type=jnp.float32)
        o_scr[row] = total + self_weight * new_values[row : row + 1]
    half = total_heads // 2
    for head in range(total_heads):
        ref = own_out if head < half else other_out
        column = (head % half) * DH
        ref[:, column : column + DH] = o_scr[:, head, :].astype(jnp.bfloat16)


def attend(core, lengths, own_q, other_q, kv_column, keys, values):
    rows, positions, _ = keys.shape
    heads = 2 * (own_q.shape[1] // DH - 1)
    out = jax.ShapeDtypeStruct((rows, heads * DH // 2), jnp.bfloat16)
    scalars = jnp.concatenate([core[None], lengths])
    return pl.pallas_call(
        functools.partial(attend_kernel, kv_column),
        out_shape=(out, out),
        in_specs=[SMEM] + [VMEM] * (3 + rows),
        out_specs=(VMEM, VMEM),
        scratch_shapes=[pltpu.VMEM((rows, heads, DH), jnp.float32)] * 2,
        compiler_params=pltpu.CompilerParams(vmem_limit_bytes=44 * MIB),
        cost_estimate=pl.CostEstimate(
            flops=4 * rows * heads * positions * DH,
            bytes_accessed=4 * rows * positions * DH,
            transcendentals=rows * heads * positions,
        ),
        name="attend",
    )(scalars, own_q, other_q, keys, *values)


def output_kernel(orders, rows, columns, pieces, after, ids_ref, *refs):
    count = 2 * len(orders)
    block_refs, w_refs = refs[:count], refs[count : count + len(pieces)]
    send_ref, keep_ref, xs_ref = refs[count + len(pieces) + after :]
    depth = block_refs[0].shape[1]
    me, core = ids_ref[0], ids_ref[1]
    n = len(orders[0])
    half = n // 2
    for group, (near_ref, far_ref) in enumerate(zip(block_refs[::2], block_refs[1::2])):
        for p, j in enumerate(orders[group]):
            block = jnp.bitwise_xor(me, j)
            place = block % half + jnp.where(block // half == core, half, 0)
            source = near_ref if p < half else far_ref
            at = (p % half) * rows
            xs_ref[
                pl.ds(pl.multiple_of(place * rows, rows), rows), group * depth : (group + 1) * depth
            ] = source[at : at + rows, :]
    cut = half * rows
    totals = {}
    for w_ref, ((first, tall), span) in zip(w_refs, pieces):
        part = jnp.dot(
            xs_ref[:, first : first + tall], w_ref[...], preferred_element_type=jnp.float32
        )
        totals[span] = totals[span] + part if span in totals else part
    for (column, width), total in totals.items():
        send_ref[:, column - columns[0] : column - columns[0] + width] = total[:cut]
        keep_ref[:, column - columns[0] : column - columns[0] + width] = total[cut:]


def project_out(orders, rows, ids, blocks, held, cuts, columns, after):
    chosen = [at for at, (_, (column, _)) in enumerate(cuts) if columns[0] <= column < sum(columns)]
    weights, pieces = [held[at] for at in chosen], [cuts[at] for at in chosen]
    pieces, weights = zip(*sorted(zip(pieces, weights), key=lambda pair: (pair[0][1], pair[0][0])))
    depth = len(orders) * blocks[0].shape[1]
    n = len(orders[0])
    out = jax.ShapeDtypeStruct((n * rows // 2, columns[1]), jnp.float32)
    return pl.pallas_call(
        functools.partial(output_kernel, orders, rows, columns, pieces, len(after)),
        out_shape=(out, out),
        in_specs=[SMEM] + [VMEM] * (len(blocks) + len(weights)) + [ANY] * len(after),
        out_specs=(VMEM, VMEM),
        scratch_shapes=[pltpu.VMEM((n * rows, depth), jnp.bfloat16)],
        compiler_params=pltpu.CompilerParams(vmem_limit_bytes=12 * MIB),
        cost_estimate=pl.CostEstimate(
            flops=2 * n * rows * depth * columns[1],
            bytes_accessed=2 * depth * columns[1] + 4 * n * rows * columns[1],
            transcendentals=0,
        ),
        name="project_out",
    )(ids, *blocks, *weights, *after)


def local(tokens, query_weight, kv_weight, out_weight, key_cache, value_cache, lengths):
    n = lax.axis_size("gx")
    me = lax.axis_index("gx").astype(jnp.int32)
    core = lax.axis_index("gy").astype(jnp.int32)
    ids = jnp.stack([me, core])
    own_rows = key_cache.shape[0]
    rows = 2 * own_rows
    bits = [1 << i for i in range(n.bit_length() - 1)]

    def swap(array):
        return lax.ppermute(array, "gy", [(0, 1), (1, 0)])

    def across(array, mask):
        return lax.ppermute(array, "gx", [(g, g ^ mask) for g in range(n)])

    other_tokens = swap(tokens)
    own_tokens = jnp.where(me < n, tokens, jnp.bfloat16(0))
    width = query_weight.shape[1] // 2

    y, z = bits[:1], bits[1:]
    unit = query_weight.shape[1] // 12
    plan = [(3 * unit, z[:1] + y + z[1:]), (5 * unit, y + z), (4 * unit, z + y)]
    state, first, after = [None] * len(plan), 0, []
    for group in ((2,), (0, 1)):
        chunks = [plan[i] for i in group]
        weight = kv_weight if 0 in group else None
        made = project(chunks, rows, ids, own_tokens, other_tokens, query_weight, weight, first, after)
        for i, pair in zip(group, made):
            state[i] = pair
        after = [made[0][0]]
        first += sum(columns for columns, _ in chunks)
    moving = [across(send, order[0]) for (send, _), (_, order) in zip(state, plan)]
    for step in range(len(bits)):
        for i in (2, 0, 1):
            columns, order = plan[i]
            total = state[i][1] + moving[i]
            if i == 0 and step == 0:
                cuts = [(0, cut) for cut in cuts_of(value_cache)]
                values, zero = load([value_cache], cuts, [state[2][0]], 46, total.shape[1])
                total = total + zero
            if step + 1 < len(bits):
                cut = total.shape[0] // 2
                state[i] = (total[cut:], total[:cut])
                moving[i] = across(state[i][0], order[step + 1])
            else:
                state[i] = total
    kv_width = kv_weight.shape[1] // 2
    by_column = [i for group in ((2,), (0, 1)) for i in group]
    total = jnp.concatenate([state[i] for i in by_column], axis=1)
    mine = lax.dynamic_slice_in_dim(total, core * own_rows, own_rows, 0).astype(jnp.bfloat16)
    give = lax.dynamic_slice_in_dim(total, (1 - core) * own_rows, own_rows, 0).astype(jnp.bfloat16)
    kv_column = sum(plan[i][0] for i in by_column[: by_column.index(0)])
    own, other = attend(core, lengths, mine, swap(give), kv_column, key_cache, values)
    got = swap(other)
    block = jnp.where(core == 0, jnp.concatenate([own, got]), jnp.concatenate([got, own]))

    near = [block[:, :width], block[:, width:]]
    far = [None, None]
    paths = [bits[::-1], bits[:1] + bits[:0:-1]]
    out_cuts, out_held = cuts_of(out_weight), []
    early = len(out_cuts) * 9 // 18
    for step in range(len(bits)):
        for i in range(2):
            if step:
                near[i] = jnp.concatenate([near[i], far[i]])
                if i == 0 and out_held:
                    near[i] = near[i] + zero.astype(jnp.bfloat16)
                if i == 1 and step + 2 >= len(bits):
                    part = out_cuts[early:] if out_held else out_cuts[:early]
                    held, zero = load([out_weight], [(0, cut) for cut in part], near, 36, width)
                    out_held += held
            far[i] = across(near[i], paths[i][step])
    orders = [order_of(path[::-1]) for path in paths]
    blocks = [b for pair in zip(near, far) for b in pair]
    send, keep = project_out(orders, rows, ids, blocks, out_held, out_cuts, (0, out_weight.shape[1]), [])
    return (keep + swap(send)).astype(jnp.bfloat16)


def solution(mesh):
    return jax.shard_map(
        local,
        mesh=mesh,
        in_specs=(
            P(("grp", "gy"), "gx"),
            P("gx", "gy"),
            P("gx", None),
            P("gy", "gx"),
            P(("grp", "gx", "gy"), None, None),
            P(("grp", "gx", "gy"), None, None),
            P(("grp", "gx", "gy")),
        ),
        out_specs=P(("grp", "gy"), "gx"),
        check_vma=False,
    )
```

```python
import functools

import jax
import jax.numpy as jnp
from jax import lax
from jax.experimental import pallas as pl
from jax.experimental.pallas import tpu as pltpu
from jax.sharding import PartitionSpec as P

H = 24
DH = 256
MIB = 1024 * 1024
HBM = pl.BlockSpec(memory_space=pltpu.HBM)
ANY = pl.BlockSpec(memory_space=pl.ANY)
VMEM = pl.BlockSpec(memory_space=pltpu.VMEM)
SMEM = pl.BlockSpec(memory_space=pltpu.SMEM)


class InOrder:
    def __init__(self, copies, ahead):
        self.copies, self.ahead = copies, ahead
        for copy in copies[:ahead]:
            copy.start()

    def wait(self, at):
        self.copies[at].wait()
        if at + self.ahead < len(self.copies):
            self.copies[at + self.ahead].start()


def order_of(bits):
    order = [0]
    for bit in reversed(bits):
        order = order + [j + bit for j in order]
    return order


def cuts_of(array):
    if len(array.shape) == 3:
        return [(at, None) for at in range(array.shape[0])]
    depth, columns = array.shape
    tall, wide = 512, (768 if columns % 768 == 0 else columns)
    return [
        ((at, tall), (column, wide)) for at in range(0, depth, tall) for column in range(0, columns, wide)
    ]


def piece_of(array, cut):
    if cut[1] is None:
        shape = array.shape[1:]
    else:
        shape = (cut[0][1], cut[1][1])
    return jax.ShapeDtypeStruct(shape, array.dtype)


def fetches(refs, cuts, targets, sems):
    copies = []
    for ref, cut in cuts:
        source = refs[ref]
        view = source.at[cut[0]] if cut[1] is None else source.at[pl.ds(*cut[0]), pl.ds(*cut[1])]
        copies.append(pltpu.make_async_copy(view, targets[len(copies)], sems.at[len(copies)]))
    return copies


def load_kernel(after, cuts, count, *refs):
    refs = refs[after:]
    in_refs, out_refs, zero_ref, sems = refs[:count], refs[count:-2], refs[-2], refs[-1]
    copies = fetches(in_refs, cuts, out_refs, sems)
    for copy in copies:
        copy.start()
    zero_ref[...] = jnp.zeros_like(zero_ref)
    for copy in copies:
        copy.wait()


def load(arrays, cuts, after, grant, zeros=128):
    shapes = [piece_of(arrays[at], cut) for at, cut in cuts]
    *held, zero = pl.pallas_call(
        functools.partial(load_kernel, len(after), cuts, len(arrays)),
        out_shape=(*shapes, jax.ShapeDtypeStruct((1, zeros), jnp.float32)),
        in_specs=[ANY] * len(after) + [HBM] * len(arrays),
        out_specs=[VMEM] * (len(cuts) + 1),
        scratch_shapes=[pltpu.SemaphoreType.DMA((len(cuts),))],
        compiler_params=pltpu.CompilerParams(vmem_limit_bytes=grant * MIB),
        cost_estimate=pl.CostEstimate(
            flops=0, bytes_accessed=sum(4 * s.shape[0] * s.shape[1] for s in shapes), transcendentals=0
        ),
        name="load",
    )(*after, *arrays)
    return held, zero


def spans_of(width):
    return [(at, min(512, width - at)) for at in range(0, width, 512)]


def project_kernel(orders, rows, first, widths, kv_width, after, ids_ref, own_ref, other_ref, w_ref, *refs):
    refs = list(refs)
    kv_ref = refs.pop(0) if kv_width else None
    outs, (xs_ref, ws_ref, w_sem) = refs[after:-3], refs[-3:]
    n = len(orders[0])
    half = n // 2
    me, core = ids_ref[0], ids_ref[1]
    features = xs_ref.shape[1]

    tiles, copies, at, source = [], [], 0, first
    depth = 768 if features % 768 == 0 else features

    def fetch(from_ref, column, width):
        for part in range(features // depth):
            span = pl.ds(part * depth, depth)
            copies.append(
                pltpu.make_async_copy(
                    from_ref.at[span, pl.ds(column, width)],
                    ws_ref.at[span, pl.ds(at, width)],
                    w_sem.at[len(copies)],
                )
            )

    for chunk, width in enumerate(widths):
        column = 0
        if kv_width and chunk == 0:
            fetch(kv_ref, pl.multiple_of(core * kv_width, kv_width), kv_width)
            tiles.append((chunk, 0, at, kv_width))
            at += kv_width
            column = kv_width
        for offset, tile in spans_of(width):
            fetch(w_ref, source, tile)
            tiles.append((chunk, column + offset, at, tile))
            at += tile
            source += tile
    per_tile = features // depth
    weights = InOrder(copies, 9)
    def place_rows(low_ref, high_ref):
        for j in range(n):
            block = jnp.bitwise_xor(me, j) % half
            source = low_ref if j < half else high_ref
            xs_ref[j * rows : (j + 1) * rows, :] = source[
                pl.ds(pl.multiple_of(block * rows, rows), rows), :
            ]

    low_mine = me // half == core

    @pl.when(low_mine)
    def _():
        place_rows(own_ref, other_ref)

    @pl.when(jnp.logical_not(low_mine))
    def _():
        place_rows(other_ref, own_ref)

    for t, (chunk, column, at, width) in enumerate(tiles):
        for part in range(per_tile):
            weights.wait(t * per_tile + part)
        total = jnp.dot(xs_ref[...], ws_ref[:, at : at + width], preferred_element_type=jnp.float32)
        span = slice(column, column + width)
        for p, j in enumerate(orders[chunk]):
            out = outs[2 * chunk + 1] if p < half else outs[2 * chunk]
            out[(p % half) * rows : (p % half + 1) * rows, span] = total[j * rows : (j + 1) * rows]


def project(plan, rows, ids, tokens, other, query_weight, kv_weight, first, after):
    features = tokens.shape[1]
    orders = [order_of(bits) for _, bits in plan]
    widths = [width for width, _ in plan]
    n = len(orders[0])
    kv_width = kv_weight.shape[1] // 2 if kv_weight is not None else 0
    columns = sum(widths) + kv_width
    outs = []
    for chunk, width in enumerate(widths):
        shape = (n * rows // 2, width + (0 if chunk else kv_width))
        outs += [jax.ShapeDtypeStruct(shape, jnp.float32)] * 2
    weights = [query_weight] + ([kv_weight] if kv_width else [])
    parts = features // 768 if features % 768 == 0 else 1
    copies = parts * (len(weights) - 1 + sum(len(spans_of(width)) for width in widths))
    outs = pl.pallas_call(
        functools.partial(project_kernel, orders, rows, first, widths, kv_width, len(after)),
        out_shape=outs,
        in_specs=[SMEM, VMEM, VMEM] + [HBM] * len(weights) + [ANY] * len(after),
        out_specs=[VMEM] * len(outs),
        scratch_shapes=[
            pltpu.VMEM((n * rows, features), tokens.dtype),
            pltpu.VMEM((features, columns), tokens.dtype),
            pltpu.SemaphoreType.DMA((copies,)),
        ],
        compiler_params=pltpu.CompilerParams(vmem_limit_bytes=46 * MIB),
        cost_estimate=pl.CostEstimate(
            flops=2 * n * rows * features * columns,
            bytes_accessed=2 * features * columns + 4 * n * rows * columns,
            transcendentals=0,
        ),
        name="project",
    )(ids, tokens, other, *weights, *after)
    return list(zip(outs[::2], outs[1::2]))


def attend_kernel(kv_column, scalars_ref, own_q, other_q, *refs):
    k_ref, refs = refs[0], refs[1:]
    v_refs, (own_out, other_out, q_scr, o_scr, s_scr) = refs[:-5], refs[-5:]
    core = scalars_ref[0]
    rows, positions, _ = k_ref.shape
    at = 0
    for ref in (own_q, other_q):
        for column in range(0, ref.shape[1], DH):
            if column != kv_column:
                q_scr[:, at, :] = DH**-0.5 * ref[:, column : column + DH].astype(jnp.float32)
                at += 1
    total_heads = at
    first = own_q[:, kv_column : kv_column + DH].astype(jnp.float32)
    second = other_q[:, kv_column : kv_column + DH].astype(jnp.float32)
    new_keys = jnp.where(core == 0, first, second)
    new_values = jnp.where(core == 0, second, first)
    own_scores = []
    for row in range(rows):
        query = q_scr[row]
        scores = lax.dot_general(
            query.astype(jnp.bfloat16),
            k_ref[row],
            (((1,), (1,)), ((), ())),
            preferred_element_type=jnp.float32,
        )
        visible = lax.broadcasted_iota(jnp.int32, scores.shape, 1) < scalars_ref[1 + row]
        s_scr[row] = jnp.where(visible, scores, jnp.float32(-1e30))
        own_scores.append(jnp.sum(query * new_keys[row : row + 1], axis=1, keepdims=True))
    self_score = jnp.stack(own_scores)
    masked = s_scr[...]
    peak = jnp.maximum(jnp.max(masked, axis=2, keepdims=True), self_score)
    raised = jnp.exp(masked - peak)
    self_raised = jnp.exp(self_score - peak)
    inverse = 1.0 / (jnp.sum(raised, axis=2, keepdims=True) + self_raised)
    s_scr[...] = raised * inverse
    self_weight = (self_raised * inverse).astype(jnp.bfloat16).astype(jnp.float32)
    for row in range(rows):
        weights = s_scr[row].astype(jnp.bfloat16)
        total = jnp.dot(weights, v_refs[row][...], preferred_element_type=jnp.float32)
        o_scr[row] = total + self_weight[row] * new_values[row : row + 1]
    half = total_heads // 2
    for head in range(total_heads):
        ref = own_out if head < half else other_out
        column = (head % half) * DH
        ref[:, column : column + DH] = o_scr[:, head, :].astype(jnp.bfloat16)


def attend(core, lengths, own_q, other_q, kv_column, keys, values):
    rows, positions, _ = keys.shape
    heads = 2 * (own_q.shape[1] // DH - 1)
    out = jax.ShapeDtypeStruct((rows, heads * DH // 2), jnp.bfloat16)
    scalars = jnp.concatenate([core[None], lengths])
    return pl.pallas_call(
        functools.partial(attend_kernel, kv_column),
        out_shape=(out, out),
        in_specs=[SMEM] + [VMEM] * (3 + rows),
        out_specs=(VMEM, VMEM),
        scratch_shapes=[pltpu.VMEM((rows, heads, DH), jnp.float32)] * 2
        + [pltpu.VMEM((rows, heads, positions), jnp.float32)],
        compiler_params=pltpu.CompilerParams(vmem_limit_bytes=44 * MIB),
        cost_estimate=pl.CostEstimate(
            flops=4 * rows * heads * positions * DH,
            bytes_accessed=4 * rows * positions * DH,
            transcendentals=rows * heads * positions,
        ),
        name="attend",
    )(scalars, own_q, other_q, keys, *values)


def output_kernel(orders, rows, columns, pieces, after, ids_ref, *refs):
    count = 2 * len(orders)
    block_refs, w_refs = refs[:count], refs[count : count + len(pieces)]
    send_ref, keep_ref, xs_ref = refs[count + len(pieces) + after :]
    depth = block_refs[0].shape[1]
    me, core = ids_ref[0], ids_ref[1]
    n = len(orders[0])
    half = n // 2
    for group, (near_ref, far_ref) in enumerate(zip(block_refs[::2], block_refs[1::2])):
        for p, j in enumerate(orders[group]):
            block = jnp.bitwise_xor(me, j)
            place = block % half + jnp.where(block // half == core, half, 0)
            source = near_ref if p < half else far_ref
            at = (p % half) * rows
            xs_ref[
                pl.ds(pl.multiple_of(place * rows, rows), rows), group * depth : (group + 1) * depth
            ] = source[at : at + rows, :]
    cut = half * rows
    totals = {}
    for w_ref, ((first, tall), span) in zip(w_refs, pieces):
        part = jnp.dot(
            xs_ref[:, first : first + tall], w_ref[...], preferred_element_type=jnp.float32
        )
        totals[span] = totals[span] + part if span in totals else part
    for (column, width), total in totals.items():
        send_ref[:, column - columns[0] : column - columns[0] + width] = total[:cut]
        keep_ref[:, column - columns[0] : column - columns[0] + width] = total[cut:]


def project_out(orders, rows, ids, blocks, held, cuts, columns, after):
    chosen = [at for at, (_, (column, _)) in enumerate(cuts) if columns[0] <= column < sum(columns)]
    weights, pieces = [held[at] for at in chosen], [cuts[at] for at in chosen]
    pieces, weights = zip(*sorted(zip(pieces, weights), key=lambda pair: (pair[0][1], pair[0][0])))
    depth = len(orders) * blocks[0].shape[1]
    n = len(orders[0])
    out = jax.ShapeDtypeStruct((n * rows // 2, columns[1]), jnp.float32)
    return pl.pallas_call(
        functools.partial(output_kernel, orders, rows, columns, pieces, len(after)),
        out_shape=(out, out),
        in_specs=[SMEM] + [VMEM] * (len(blocks) + len(weights)) + [ANY] * len(after),
        out_specs=(VMEM, VMEM),
        scratch_shapes=[pltpu.VMEM((n * rows, depth), jnp.bfloat16)],
        compiler_params=pltpu.CompilerParams(vmem_limit_bytes=12 * MIB),
        cost_estimate=pl.CostEstimate(
            flops=2 * n * rows * depth * columns[1],
            bytes_accessed=2 * depth * columns[1] + 4 * n * rows * columns[1],
            transcendentals=0,
        ),
        name="project_out",
    )(ids, *blocks, *weights, *after)


def local(tokens, query_weight, kv_weight, out_weight, key_cache, value_cache, lengths):
    n = lax.axis_size("gx")
    me = lax.axis_index("gx").astype(jnp.int32)
    core = lax.axis_index("gy").astype(jnp.int32)
    ids = jnp.stack([me, core])
    own_rows = key_cache.shape[0]
    rows = 2 * own_rows
    bits = [1 << i for i in range(n.bit_length() - 1)]

    def swap(array):
        return lax.ppermute(array, "gy", [(0, 1), (1, 0)])

    def across(array, mask):
        return lax.ppermute(array, "gx", [(g, g ^ mask) for g in range(n)])

    other_tokens = swap(tokens)
    own_tokens = jnp.where(me < n, tokens, jnp.bfloat16(0))
    width = query_weight.shape[1] // 2

    y, z = bits[:1], bits[1:]
    unit = query_weight.shape[1] // 12
    plan = [(3 * unit, z[:1] + y + z[1:]), (5 * unit, y + z), (4 * unit, z + y)]
    state, first, after = [None] * len(plan), 0, []
    for group in ((2,), (0, 1)):
        chunks = [plan[i] for i in group]
        weight = kv_weight if 0 in group else None
        made = project(chunks, rows, ids, own_tokens, other_tokens, query_weight, weight, first, after)
        for i, pair in zip(group, made):
            state[i] = pair
        after = [made[0][0]]
        first += sum(columns for columns, _ in chunks)
    moving = [across(send, order[0]) for (send, _), (_, order) in zip(state, plan)]
    for step in range(len(bits)):
        for i in (2, 0, 1):
            columns, order = plan[i]
            total = state[i][1] + moving[i]
            if i == 0 and step == 0:
                cuts = [(0, cut) for cut in cuts_of(value_cache)]
                values, zero = load([value_cache], cuts, [state[2][0]], 46, total.shape[1])
                total = total + zero
            if step + 1 < len(bits):
                cut = total.shape[0] // 2
                state[i] = (total[cut:], total[:cut])
                moving[i] = across(state[i][0], order[step + 1])
            else:
                state[i] = total
    kv_width = kv_weight.shape[1] // 2
    by_column = [i for group in ((2,), (0, 1)) for i in group]
    total = jnp.concatenate([state[i] for i in by_column], axis=1)
    mine = lax.dynamic_slice_in_dim(total, core * own_rows, own_rows, 0).astype(jnp.bfloat16)
    give = lax.dynamic_slice_in_dim(total, (1 - core) * own_rows, own_rows, 0).astype(jnp.bfloat16)
    kv_column = sum(plan[i][0] for i in by_column[: by_column.index(0)])
    own, other = attend(core, lengths, mine, swap(give), kv_column, key_cache, values)
    got = swap(other)
    block = jnp.where(core == 0, jnp.concatenate([own, got]), jnp.concatenate([got, own]))

    near = [block[:, :width], block[:, width:]]
    far = [None, None]
    paths = [bits[::-1], bits[:1] + bits[:0:-1]]
    out_cuts, out_held = cuts_of(out_weight), []
    early = len(out_cuts) * 9 // 18
    for step in range(len(bits)):
        for i in range(2):
            if step:
                near[i] = jnp.concatenate([near[i], far[i]])
                if i == 0 and out_held:
                    near[i] = near[i] + zero.astype(jnp.bfloat16)
                if i == 1 and step + 2 >= len(bits):
                    part = out_cuts[early:] if out_held else out_cuts[:early]
                    held, zero = load([out_weight], [(0, cut) for cut in part], near, 36, width)
                    out_held += held
            far[i] = across(near[i], paths[i][step])
    orders = [order_of(path[::-1]) for path in paths]
    blocks = [b for pair in zip(near, far) for b in pair]
    send, keep = project_out(orders, rows, ids, blocks, out_held, out_cuts, (0, out_weight.shape[1]), [])
    return (keep + swap(send)).astype(jnp.bfloat16)


def solution(mesh):
    return jax.shard_map(
        local,
        mesh=mesh,
        in_specs=(
            P(("grp", "gy"), "gx"),
            P("gx", "gy"),
            P("gx", None),
            P("gy", "gx"),
            P(("grp", "gx", "gy"), None, None),
            P(("grp", "gx", "gy"), None, None),
            P(("grp", "gx", "gy")),
        ),
        out_specs=P(("grp", "gy"), "gx"),
        check_vma=False,
    )
```

```python
import functools

import jax
import jax.numpy as jnp
from jax import lax
from jax.experimental import pallas as pl
from jax.experimental.pallas import tpu as pltpu
from jax.sharding import PartitionSpec as P

H = 24
DH = 256
MIB = 1024 * 1024
HBM = pl.BlockSpec(memory_space=pltpu.HBM)
ANY = pl.BlockSpec(memory_space=pl.ANY)
VMEM = pl.BlockSpec(memory_space=pltpu.VMEM)
SMEM = pl.BlockSpec(memory_space=pltpu.SMEM)


class InOrder:
    def __init__(self, copies, ahead):
        self.copies, self.ahead = copies, ahead
        for copy in copies[:ahead]:
            copy.start()

    def wait(self, at):
        self.copies[at].wait()
        if at + self.ahead < len(self.copies):
            self.copies[at + self.ahead].start()


def order_of(bits):
    order = [0]
    for bit in reversed(bits):
        order = order + [j + bit for j in order]
    return order


def cuts_of(array):
    if len(array.shape) == 3:
        return [(at, None) for at in range(array.shape[0])]
    depth, columns = array.shape
    tall, wide = 512, (768 if columns % 768 == 0 else columns)
    return [
        ((at, tall), (column, wide)) for at in range(0, depth, tall) for column in range(0, columns, wide)
    ]


def piece_of(array, cut):
    if cut[1] is None:
        shape = array.shape[1:]
    else:
        shape = (cut[0][1], cut[1][1])
    return jax.ShapeDtypeStruct(shape, array.dtype)


def fetches(refs, cuts, targets, sems):
    copies = []
    for ref, cut in cuts:
        source = refs[ref]
        view = source.at[cut[0]] if cut[1] is None else source.at[pl.ds(*cut[0]), pl.ds(*cut[1])]
        copies.append(pltpu.make_async_copy(view, targets[len(copies)], sems.at[len(copies)]))
    return copies


def load_kernel(after, cuts, count, *refs):
    refs = refs[after:]
    in_refs, out_refs, zero_ref, sems = refs[:count], refs[count:-2], refs[-2], refs[-1]
    copies = fetches(in_refs, cuts, out_refs, sems)
    for copy in copies:
        copy.start()
    zero_ref[...] = jnp.zeros_like(zero_ref)
    for copy in copies:
        copy.wait()


def load(arrays, cuts, after, grant, zeros=128):
    shapes = [piece_of(arrays[at], cut) for at, cut in cuts]
    *held, zero = pl.pallas_call(
        functools.partial(load_kernel, len(after), cuts, len(arrays)),
        out_shape=(*shapes, jax.ShapeDtypeStruct((1, zeros), jnp.float32)),
        in_specs=[ANY] * len(after) + [HBM] * len(arrays),
        out_specs=[VMEM] * (len(cuts) + 1),
        scratch_shapes=[pltpu.SemaphoreType.DMA((len(cuts),))],
        compiler_params=pltpu.CompilerParams(vmem_limit_bytes=grant * MIB),
        cost_estimate=pl.CostEstimate(
            flops=0, bytes_accessed=sum(4 * s.shape[0] * s.shape[1] for s in shapes), transcendentals=0
        ),
        name="load",
    )(*after, *arrays)
    return held, zero


def spans_of(width):
    return [(at, min(768, width - at)) for at in range(0, width, 768)]


def project_kernel(orders, rows, first, widths, kv_width, after, ids_ref, own_ref, other_ref, w_ref, *refs):
    refs = list(refs)
    kv_ref = refs.pop(0) if kv_width else None
    outs, (xs_ref, ws_ref, w_sem) = refs[after:-3], refs[-3:]
    n = len(orders[0])
    half = n // 2
    me, core = ids_ref[0], ids_ref[1]
    features = xs_ref.shape[1]

    tiles, copies, at, source = [], [], 0, first
    depth = 768 if features % 768 == 0 else features

    def fetch(from_ref, column, width):
        for part in range(features // depth):
            span = pl.ds(part * depth, depth)
            copies.append(
                pltpu.make_async_copy(
                    from_ref.at[span, pl.ds(column, width)],
                    ws_ref.at[span, pl.ds(at, width)],
                    w_sem.at[len(copies)],
                )
            )

    for chunk, width in enumerate(widths):
        column = 0
        if kv_width and chunk == 0:
            fetch(kv_ref, pl.multiple_of(core * kv_width, kv_width), kv_width)
            tiles.append((chunk, 0, at, kv_width))
            at += kv_width
            column = kv_width
        for offset, tile in spans_of(width):
            fetch(w_ref, source, tile)
            tiles.append((chunk, column + offset, at, tile))
            at += tile
            source += tile
    per_tile = features // depth
    weights = InOrder(copies, 9)
    def place_rows(low_ref, high_ref):
        for j in range(n):
            block = jnp.bitwise_xor(me, j) % half
            source = low_ref if j < half else high_ref
            xs_ref[j * rows : (j + 1) * rows, :] = source[
                pl.ds(pl.multiple_of(block * rows, rows), rows), :
            ]

    low_mine = me // half == core

    @pl.when(low_mine)
    def _():
        place_rows(own_ref, other_ref)

    @pl.when(jnp.logical_not(low_mine))
    def _():
        place_rows(other_ref, own_ref)

    for t, (chunk, column, at, width) in enumerate(tiles):
        for part in range(per_tile):
            weights.wait(t * per_tile + part)
        total = jnp.dot(xs_ref[...], ws_ref[:, at : at + width], preferred_element_type=jnp.float32)
        span = slice(column, column + width)
        for p, j in enumerate(orders[chunk]):
            out = outs[2 * chunk + 1] if p < half else outs[2 * chunk]
            out[(p % half) * rows : (p % half + 1) * rows, span] = total[j * rows : (j + 1) * rows]


def project(plan, rows, ids, tokens, other, query_weight, kv_weight, first, after):
    features = tokens.shape[1]
    orders = [order_of(bits) for _, bits in plan]
    widths = [width for width, _ in plan]
    n = len(orders[0])
    kv_width = kv_weight.shape[1] // 2 if kv_weight is not None else 0
    columns = sum(widths) + kv_width
    outs = []
    for chunk, width in enumerate(widths):
        shape = (n * rows // 2, width + (0 if chunk else kv_width))
        outs += [jax.ShapeDtypeStruct(shape, jnp.float32)] * 2
    weights = [query_weight] + ([kv_weight] if kv_width else [])
    parts = features // 768 if features % 768 == 0 else 1
    copies = parts * (len(weights) - 1 + sum(len(spans_of(width)) for width in widths))
    outs = pl.pallas_call(
        functools.partial(project_kernel, orders, rows, first, widths, kv_width, len(after)),
        out_shape=outs,
        in_specs=[SMEM, VMEM, VMEM] + [HBM] * len(weights) + [ANY] * len(after),
        out_specs=[VMEM] * len(outs),
        scratch_shapes=[
            pltpu.VMEM((n * rows, features), tokens.dtype),
            pltpu.VMEM((features, columns), tokens.dtype),
            pltpu.SemaphoreType.DMA((copies,)),
        ],
        compiler_params=pltpu.CompilerParams(vmem_limit_bytes=46 * MIB),
        cost_estimate=pl.CostEstimate(
            flops=2 * n * rows * features * columns,
            bytes_accessed=2 * features * columns + 4 * n * rows * columns,
            transcendentals=0,
        ),
        name="project",
    )(ids, tokens, other, *weights, *after)
    return list(zip(outs[::2], outs[1::2]))


def attend_kernel(kv_column, scalars_ref, own_q, other_q, *refs):
    k_ref, refs = refs[0], refs[1:]
    v_refs, (own_out, other_out, q_scr, o_scr, s_scr) = refs[:-5], refs[-5:]
    core = scalars_ref[0]
    rows, positions, _ = k_ref.shape
    at = 0
    for ref in (own_q, other_q):
        for column in range(0, ref.shape[1], DH):
            if column != kv_column:
                q_scr[:, at, :] = DH**-0.5 * ref[:, column : column + DH].astype(jnp.float32)
                at += 1
    total_heads = at
    first = own_q[:, kv_column : kv_column + DH].astype(jnp.float32)
    second = other_q[:, kv_column : kv_column + DH].astype(jnp.float32)
    new_keys = jnp.where(core == 0, first, second)
    new_values = jnp.where(core == 0, second, first)
    own_scores = []
    for row in range(rows):
        query = q_scr[row]
        scores = lax.dot_general(
            query.astype(jnp.bfloat16),
            k_ref[row],
            (((1,), (1,)), ((), ())),
            preferred_element_type=jnp.float32,
        )
        visible = lax.broadcasted_iota(jnp.int32, scores.shape, 1) < scalars_ref[1 + row]
        s_scr[row] = jnp.where(visible, scores, jnp.float32(-1e30))
        own_scores.append(jnp.sum(query * new_keys[row : row + 1], axis=1, keepdims=True))
    self_score = jnp.stack(own_scores)
    masked = s_scr[...]
    peak = jnp.maximum(jnp.max(masked, axis=2, keepdims=True), self_score)
    raised = jnp.exp(masked - peak)
    self_raised = jnp.exp(self_score - peak)
    inverse = 1.0 / (jnp.sum(raised, axis=2, keepdims=True) + self_raised)
    s_scr[...] = raised * inverse
    self_weight = (self_raised * inverse).astype(jnp.bfloat16).astype(jnp.float32)
    for row in range(rows):
        weights = s_scr[row].astype(jnp.bfloat16)
        total = jnp.dot(weights, v_refs[row][...], preferred_element_type=jnp.float32)
        o_scr[row] = total + self_weight[row] * new_values[row : row + 1]
    half = total_heads // 2
    for head in range(total_heads):
        ref = own_out if head < half else other_out
        column = (head % half) * DH
        ref[:, column : column + DH] = o_scr[:, head, :].astype(jnp.bfloat16)


def attend(core, lengths, own_q, other_q, kv_column, keys, values):
    rows, positions, _ = keys.shape
    heads = 2 * (own_q.shape[1] // DH - 1)
    out = jax.ShapeDtypeStruct((rows, heads * DH // 2), jnp.bfloat16)
    scalars = jnp.concatenate([core[None], lengths])
    return pl.pallas_call(
        functools.partial(attend_kernel, kv_column),
        out_shape=(out, out),
        in_specs=[SMEM] + [VMEM] * (3 + rows),
        out_specs=(VMEM, VMEM),
        scratch_shapes=[pltpu.VMEM((rows, heads, DH), jnp.float32)] * 2
        + [pltpu.VMEM((rows, heads, positions), jnp.float32)],
        compiler_params=pltpu.CompilerParams(vmem_limit_bytes=44 * MIB),
        cost_estimate=pl.CostEstimate(
            flops=4 * rows * heads * positions * DH,
            bytes_accessed=4 * rows * positions * DH,
            transcendentals=rows * heads * positions,
        ),
        name="attend",
    )(scalars, own_q, other_q, keys, *values)


def output_kernel(orders, rows, columns, pieces, after, ids_ref, *refs):
    count = 2 * len(orders)
    block_refs, w_refs = refs[:count], refs[count : count + len(pieces)]
    send_ref, keep_ref, xs_ref = refs[count + len(pieces) + after :]
    depth = block_refs[0].shape[1]
    me, core = ids_ref[0], ids_ref[1]
    n = len(orders[0])
    half = n // 2
    for group, (near_ref, far_ref) in enumerate(zip(block_refs[::2], block_refs[1::2])):
        for p, j in enumerate(orders[group]):
            block = jnp.bitwise_xor(me, j)
            place = block % half + jnp.where(block // half == core, half, 0)
            source = near_ref if p < half else far_ref
            at = (p % half) * rows
            xs_ref[
                pl.ds(pl.multiple_of(place * rows, rows), rows), group * depth : (group + 1) * depth
            ] = source[at : at + rows, :]
    cut = half * rows
    totals = {}
    for w_ref, ((first, tall), span) in zip(w_refs, pieces):
        part = jnp.dot(
            xs_ref[:, first : first + tall], w_ref[...], preferred_element_type=jnp.float32
        )
        totals[span] = totals[span] + part if span in totals else part
    for (column, width), total in totals.items():
        send_ref[:, column - columns[0] : column - columns[0] + width] = total[:cut]
        keep_ref[:, column - columns[0] : column - columns[0] + width] = total[cut:]


def project_out(orders, rows, ids, blocks, held, cuts, columns, after):
    chosen = [at for at, (_, (column, _)) in enumerate(cuts) if columns[0] <= column < sum(columns)]
    weights, pieces = [held[at] for at in chosen], [cuts[at] for at in chosen]
    pieces, weights = zip(*sorted(zip(pieces, weights), key=lambda pair: (pair[0][1], pair[0][0])))
    depth = len(orders) * blocks[0].shape[1]
    n = len(orders[0])
    out = jax.ShapeDtypeStruct((n * rows // 2, columns[1]), jnp.float32)
    return pl.pallas_call(
        functools.partial(output_kernel, orders, rows, columns, pieces, len(after)),
        out_shape=(out, out),
        in_specs=[SMEM] + [VMEM] * (len(blocks) + len(weights)) + [ANY] * len(after),
        out_specs=(VMEM, VMEM),
        scratch_shapes=[pltpu.VMEM((n * rows, depth), jnp.bfloat16)],
        compiler_params=pltpu.CompilerParams(vmem_limit_bytes=12 * MIB),
        cost_estimate=pl.CostEstimate(
            flops=2 * n * rows * depth * columns[1],
            bytes_accessed=2 * depth * columns[1] + 4 * n * rows * columns[1],
            transcendentals=0,
        ),
        name="project_out",
    )(ids, *blocks, *weights, *after)


def local(tokens, query_weight, kv_weight, out_weight, key_cache, value_cache, lengths):
    n = lax.axis_size("gx")
    me = lax.axis_index("gx").astype(jnp.int32)
    core = lax.axis_index("gy").astype(jnp.int32)
    ids = jnp.stack([me, core])
    own_rows = key_cache.shape[0]
    rows = 2 * own_rows
    bits = [1 << i for i in range(n.bit_length() - 1)]

    def swap(array):
        return lax.ppermute(array, "gy", [(0, 1), (1, 0)])

    def across(array, mask):
        return lax.ppermute(array, "gx", [(g, g ^ mask) for g in range(n)])

    other_tokens = swap(tokens)
    own_tokens = jnp.where(me < n, tokens, jnp.bfloat16(0))
    width = query_weight.shape[1] // 2

    y, z = bits[:1], bits[1:]
    unit = query_weight.shape[1] // 12
    plan = [(3 * unit, z[:1] + y + z[1:]), (5 * unit, y + z), (4 * unit, z + y)]
    state, first, after = [None] * len(plan), 0, []
    for group in ((2,), (0, 1)):
        chunks = [plan[i] for i in group]
        weight = kv_weight if 0 in group else None
        made = project(chunks, rows, ids, own_tokens, other_tokens, query_weight, weight, first, after)
        for i, pair in zip(group, made):
            state[i] = pair
        after = [made[0][0]]
        first += sum(columns for columns, _ in chunks)
    moving = [across(send, order[0]) for (send, _), (_, order) in zip(state, plan)]
    for step in range(len(bits)):
        for i in (2, 0, 1):
            columns, order = plan[i]
            total = state[i][1] + moving[i]
            if i == 0 and step == 0:
                cuts = [(0, cut) for cut in cuts_of(value_cache)]
                values, zero = load([value_cache], cuts, [state[2][0]], 46, total.shape[1])
                total = total + zero
            if step + 1 < len(bits):
                cut = total.shape[0] // 2
                state[i] = (total[cut:], total[:cut])
                moving[i] = across(state[i][0], order[step + 1])
            else:
                state[i] = total
    kv_width = kv_weight.shape[1] // 2
    by_column = [i for group in ((2,), (0, 1)) for i in group]
    total = jnp.concatenate([state[i] for i in by_column], axis=1)
    mine = lax.dynamic_slice_in_dim(total, core * own_rows, own_rows, 0).astype(jnp.bfloat16)
    give = lax.dynamic_slice_in_dim(total, (1 - core) * own_rows, own_rows, 0).astype(jnp.bfloat16)
    kv_column = sum(plan[i][0] for i in by_column[: by_column.index(0)])
    own, other = attend(core, lengths, mine, swap(give), kv_column, key_cache, values)
    got = swap(other)
    block = jnp.where(core == 0, jnp.concatenate([own, got]), jnp.concatenate([got, own]))

    near = [block[:, :width], block[:, width:]]
    far = [None, None]
    paths = [bits[::-1], bits[:1] + bits[:0:-1]]
    out_cuts, out_held = cuts_of(out_weight), []
    early = len(out_cuts) * 9 // 18
    for step in range(len(bits)):
        for i in range(2):
            if step:
                near[i] = jnp.concatenate([near[i], far[i]])
                if i == 0 and out_held:
                    near[i] = near[i] + zero.astype(jnp.bfloat16)
                if i == 1 and step + 2 >= len(bits):
                    part = out_cuts[early:] if out_held else out_cuts[:early]
                    held, zero = load([out_weight], [(0, cut) for cut in part], near, 36, width)
                    out_held += held
            far[i] = across(near[i], paths[i][step])
    orders = [order_of(path[::-1]) for path in paths]
    blocks = [b for pair in zip(near, far) for b in pair]
    send, keep = project_out(orders, rows, ids, blocks, out_held, out_cuts, (0, out_weight.shape[1]), [])
    return (keep + swap(send)).astype(jnp.bfloat16)


def solution(mesh):
    return jax.shard_map(
        local,
        mesh=mesh,
        in_specs=(
            P(("grp", "gy"), "gx"),
            P("gx", "gy"),
            P("gx", None),
            P("gy", "gx"),
            P(("grp", "gx", "gy"), None, None),
            P(("grp", "gx", "gy"), None, None),
            P(("grp", "gx", "gy")),
        ),
        out_specs=P(("grp", "gy"), "gx"),
        check_vma=False,
    )
```

```python
import functools

import jax
import jax.numpy as jnp
from jax import lax
from jax.experimental import pallas as pl
from jax.experimental.pallas import tpu as pltpu
from jax.sharding import PartitionSpec as P

H = 24
DH = 256
MIB = 1024 * 1024
HBM = pl.BlockSpec(memory_space=pltpu.HBM)
ANY = pl.BlockSpec(memory_space=pl.ANY)
VMEM = pl.BlockSpec(memory_space=pltpu.VMEM)
SMEM = pl.BlockSpec(memory_space=pltpu.SMEM)


class InOrder:
    def __init__(self, copies, ahead):
        self.copies, self.ahead = copies, ahead
        for copy in copies[:ahead]:
            copy.start()

    def wait(self, at):
        self.copies[at].wait()
        if at + self.ahead < len(self.copies):
            self.copies[at + self.ahead].start()


def order_of(bits):
    order = [0]
    for bit in reversed(bits):
        order = order + [j + bit for j in order]
    return order


def cuts_of(array):
    if len(array.shape) == 3:
        return [(at, None) for at in range(array.shape[0])]
    depth, columns = array.shape
    tall, wide = 512, (768 if columns % 768 == 0 else columns)
    return [
        ((at, tall), (column, wide)) for at in range(0, depth, tall) for column in range(0, columns, wide)
    ]


def piece_of(array, cut):
    if cut[1] is None:
        shape = array.shape[1:]
    else:
        shape = (cut[0][1], cut[1][1])
    return jax.ShapeDtypeStruct(shape, array.dtype)


def fetches(refs, cuts, targets, sems):
    copies = []
    for ref, cut in cuts:
        source = refs[ref]
        view = source.at[cut[0]] if cut[1] is None else source.at[pl.ds(*cut[0]), pl.ds(*cut[1])]
        copies.append(pltpu.make_async_copy(view, targets[len(copies)], sems.at[len(copies)]))
    return copies


def load_kernel(after, cuts, count, *refs):
    refs = refs[after:]
    in_refs, out_refs, zero_ref, sems = refs[:count], refs[count:-2], refs[-2], refs[-1]
    copies = fetches(in_refs, cuts, out_refs, sems)
    for copy in copies:
        copy.start()
    zero_ref[...] = jnp.zeros_like(zero_ref)
    for copy in copies:
        copy.wait()


def load(arrays, cuts, after, grant, zeros=128):
    shapes = [piece_of(arrays[at], cut) for at, cut in cuts]
    *held, zero = pl.pallas_call(
        functools.partial(load_kernel, len(after), cuts, len(arrays)),
        out_shape=(*shapes, jax.ShapeDtypeStruct((1, zeros), jnp.float32)),
        in_specs=[ANY] * len(after) + [HBM] * len(arrays),
        out_specs=[VMEM] * (len(cuts) + 1),
        scratch_shapes=[pltpu.SemaphoreType.DMA((len(cuts),))],
        compiler_params=pltpu.CompilerParams(vmem_limit_bytes=grant * MIB),
        cost_estimate=pl.CostEstimate(
            flops=0, bytes_accessed=sum(4 * s.shape[0] * s.shape[1] for s in shapes), transcendentals=0
        ),
        name="load",
    )(*after, *arrays)
    return held, zero


def spans_of(width, tile):
    return [(at, min(tile, width - at)) for at in range(0, width, tile)]


def project_kernel(orders, rows, first, widths, kv_width, after, ids_ref, own_ref, other_ref, w_ref, *refs):
    refs = list(refs)
    kv_ref = refs.pop(0) if kv_width else None
    outs, (xs_ref, ws_ref, w_sem) = refs[after:-3], refs[-3:]
    n = len(orders[0])
    half = n // 2
    me, core = ids_ref[0], ids_ref[1]
    features = xs_ref.shape[1]

    tiles, copies, at, source = [], [], 0, first
    wide = 512 if len(widths) == 1 else 768
    depth = 768 if features % 768 == 0 else features

    def fetch(from_ref, column, width):
        for part in range(features // depth):
            span = pl.ds(part * depth, depth)
            copies.append(
                pltpu.make_async_copy(
                    from_ref.at[span, pl.ds(column, width)],
                    ws_ref.at[span, pl.ds(at, width)],
                    w_sem.at[len(copies)],
                )
            )

    for chunk, width in enumerate(widths):
        column = 0
        if kv_width and chunk == 0:
            fetch(kv_ref, pl.multiple_of(core * kv_width, kv_width), kv_width)
            tiles.append((chunk, 0, at, kv_width))
            at += kv_width
            column = kv_width
        for offset, tile in spans_of(width, wide):
            fetch(w_ref, source, tile)
            tiles.append((chunk, column + offset, at, tile))
            at += tile
            source += tile
    per_tile = features // depth
    weights = InOrder(copies, 9)
    def place_rows(low_ref, high_ref):
        for j in range(n):
            block = jnp.bitwise_xor(me, j) % half
            source = low_ref if j < half else high_ref
            xs_ref[j * rows : (j + 1) * rows, :] = source[
                pl.ds(pl.multiple_of(block * rows, rows), rows), :
            ]

    low_mine = me // half == core

    @pl.when(low_mine)
    def _():
        place_rows(own_ref, other_ref)

    @pl.when(jnp.logical_not(low_mine))
    def _():
        place_rows(other_ref, own_ref)

    for t, (chunk, column, at, width) in enumerate(tiles):
        for part in range(per_tile):
            weights.wait(t * per_tile + part)
        total = jnp.dot(xs_ref[...], ws_ref[:, at : at + width], preferred_element_type=jnp.float32)
        span = slice(column, column + width)
        for p, j in enumerate(orders[chunk]):
            out = outs[2 * chunk + 1] if p < half else outs[2 * chunk]
            out[(p % half) * rows : (p % half + 1) * rows, span] = total[j * rows : (j + 1) * rows]


def project(plan, rows, ids, tokens, other, query_weight, kv_weight, first, after):
    features = tokens.shape[1]
    orders = [order_of(bits) for _, bits in plan]
    widths = [width for width, _ in plan]
    n = len(orders[0])
    kv_width = kv_weight.shape[1] // 2 if kv_weight is not None else 0
    columns = sum(widths) + kv_width
    outs = []
    for chunk, width in enumerate(widths):
        shape = (n * rows // 2, width + (0 if chunk else kv_width))
        outs += [jax.ShapeDtypeStruct(shape, jnp.float32)] * 2
    weights = [query_weight] + ([kv_weight] if kv_width else [])
    parts = features // 768 if features % 768 == 0 else 1
    copies = parts * (len(weights) - 1 + sum(len(spans_of(width, 512)) for width in widths))
    outs = pl.pallas_call(
        functools.partial(project_kernel, orders, rows, first, widths, kv_width, len(after)),
        out_shape=outs,
        in_specs=[SMEM, VMEM, VMEM] + [HBM] * len(weights) + [ANY] * len(after),
        out_specs=[VMEM] * len(outs),
        scratch_shapes=[
            pltpu.VMEM((n * rows, features), tokens.dtype),
            pltpu.VMEM((features, columns), tokens.dtype),
            pltpu.SemaphoreType.DMA((copies,)),
        ],
        compiler_params=pltpu.CompilerParams(vmem_limit_bytes=46 * MIB),
        cost_estimate=pl.CostEstimate(
            flops=2 * n * rows * features * columns,
            bytes_accessed=2 * features * columns + 4 * n * rows * columns,
            transcendentals=0,
        ),
        name="project",
    )(ids, tokens, other, *weights, *after)
    return list(zip(outs[::2], outs[1::2]))


def attend_kernel(kv_column, scalars_ref, own_q, other_q, *refs):
    k_ref, refs = refs[0], refs[1:]
    v_refs, (own_out, other_out, q_scr, o_scr, s_scr) = refs[:-5], refs[-5:]
    core = scalars_ref[0]
    rows, positions, _ = k_ref.shape
    at = 0
    for ref in (own_q, other_q):
        for column in range(0, ref.shape[1], DH):
            if column != kv_column:
                q_scr[:, at, :] = DH**-0.5 * ref[:, column : column + DH].astype(jnp.float32)
                at += 1
    total_heads = at
    first = own_q[:, kv_column : kv_column + DH].astype(jnp.float32)
    second = other_q[:, kv_column : kv_column + DH].astype(jnp.float32)
    new_keys = jnp.where(core == 0, first, second)
    new_values = jnp.where(core == 0, second, first)
    own_scores = []
    for row in range(rows):
        query = q_scr[row]
        scores = lax.dot_general(
            query.astype(jnp.bfloat16),
            k_ref[row],
            (((1,), (1,)), ((), ())),
            preferred_element_type=jnp.float32,
        )
        visible = lax.broadcasted_iota(jnp.int32, scores.shape, 1) < scalars_ref[1 + row]
        s_scr[row] = jnp.where(visible, scores, jnp.float32(-1e30))
        own_scores.append(jnp.sum(query * new_keys[row : row + 1], axis=1, keepdims=True))
    self_score = jnp.stack(own_scores)
    masked = s_scr[...]
    peak = jnp.maximum(jnp.max(masked, axis=2, keepdims=True), self_score)
    raised = jnp.exp(masked - peak)
    self_raised = jnp.exp(self_score - peak)
    inverse = 1.0 / (jnp.sum(raised, axis=2, keepdims=True) + self_raised)
    s_scr[...] = raised * inverse
    self_weight = (self_raised * inverse).astype(jnp.bfloat16).astype(jnp.float32)
    for row in range(rows):
        weights = s_scr[row].astype(jnp.bfloat16)
        total = jnp.dot(weights, v_refs[row][...], preferred_element_type=jnp.float32)
        o_scr[row] = total + self_weight[row] * new_values[row : row + 1]
    half = total_heads // 2
    for head in range(total_heads):
        ref = own_out if head < half else other_out
        column = (head % half) * DH
        ref[:, column : column + DH] = o_scr[:, head, :].astype(jnp.bfloat16)


def attend(core, lengths, own_q, other_q, kv_column, keys, values):
    rows, positions, _ = keys.shape
    heads = 2 * (own_q.shape[1] // DH - 1)
    out = jax.ShapeDtypeStruct((rows, heads * DH // 2), jnp.bfloat16)
    scalars = jnp.concatenate([core[None], lengths])
    return pl.pallas_call(
        functools.partial(attend_kernel, kv_column),
        out_shape=(out, out),
        in_specs=[SMEM] + [VMEM] * (3 + rows),
        out_specs=(VMEM, VMEM),
        scratch_shapes=[pltpu.VMEM((rows, heads, DH), jnp.float32)] * 2
        + [pltpu.VMEM((rows, heads, positions), jnp.float32)],
        compiler_params=pltpu.CompilerParams(vmem_limit_bytes=44 * MIB),
        cost_estimate=pl.CostEstimate(
            flops=4 * rows * heads * positions * DH,
            bytes_accessed=4 * rows * positions * DH,
            transcendentals=rows * heads * positions,
        ),
        name="attend",
    )(scalars, own_q, other_q, keys, *values)


def output_kernel(orders, rows, columns, pieces, after, ids_ref, *refs):
    count = 2 * len(orders)
    block_refs, w_refs = refs[:count], refs[count : count + len(pieces)]
    send_ref, keep_ref, xs_ref = refs[count + len(pieces) + after :]
    depth = block_refs[0].shape[1]
    me, core = ids_ref[0], ids_ref[1]
    n = len(orders[0])
    half = n // 2
    for group, (near_ref, far_ref) in enumerate(zip(block_refs[::2], block_refs[1::2])):
        for p, j in enumerate(orders[group]):
            block = jnp.bitwise_xor(me, j)
            place = block % half + jnp.where(block // half == core, half, 0)
            source = near_ref if p < half else far_ref
            at = (p % half) * rows
            xs_ref[
                pl.ds(pl.multiple_of(place * rows, rows), rows), group * depth : (group + 1) * depth
            ] = source[at : at + rows, :]
    cut = half * rows
    totals = {}
    for w_ref, ((first, tall), span) in zip(w_refs, pieces):
        part = jnp.dot(
            xs_ref[:, first : first + tall], w_ref[...], preferred_element_type=jnp.float32
        )
        totals[span] = totals[span] + part if span in totals else part
    for (column, width), total in totals.items():
        send_ref[:, column - columns[0] : column - columns[0] + width] = total[:cut]
        keep_ref[:, column - columns[0] : column - columns[0] + width] = total[cut:]


def project_out(orders, rows, ids, blocks, held, cuts, columns, after):
    chosen = [at for at, (_, (column, _)) in enumerate(cuts) if columns[0] <= column < sum(columns)]
    weights, pieces = [held[at] for at in chosen], [cuts[at] for at in chosen]
    pieces, weights = zip(*sorted(zip(pieces, weights), key=lambda pair: (pair[0][1], pair[0][0])))
    depth = len(orders) * blocks[0].shape[1]
    n = len(orders[0])
    out = jax.ShapeDtypeStruct((n * rows // 2, columns[1]), jnp.float32)
    return pl.pallas_call(
        functools.partial(output_kernel, orders, rows, columns, pieces, len(after)),
        out_shape=(out, out),
        in_specs=[SMEM] + [VMEM] * (len(blocks) + len(weights)) + [ANY] * len(after),
        out_specs=(VMEM, VMEM),
        scratch_shapes=[pltpu.VMEM((n * rows, depth), jnp.bfloat16)],
        compiler_params=pltpu.CompilerParams(vmem_limit_bytes=12 * MIB),
        cost_estimate=pl.CostEstimate(
            flops=2 * n * rows * depth * columns[1],
            bytes_accessed=2 * depth * columns[1] + 4 * n * rows * columns[1],
            transcendentals=0,
        ),
        name="project_out",
    )(ids, *blocks, *weights, *after)


def local(tokens, query_weight, kv_weight, out_weight, key_cache, value_cache, lengths):
    n = lax.axis_size("gx")
    me = lax.axis_index("gx").astype(jnp.int32)
    core = lax.axis_index("gy").astype(jnp.int32)
    ids = jnp.stack([me, core])
    own_rows = key_cache.shape[0]
    rows = 2 * own_rows
    bits = [1 << i for i in range(n.bit_length() - 1)]

    def swap(array):
        return lax.ppermute(array, "gy", [(0, 1), (1, 0)])

    def across(array, mask):
        return lax.ppermute(array, "gx", [(g, g ^ mask) for g in range(n)])

    other_tokens = swap(tokens)
    own_tokens = jnp.where(me < n, tokens, jnp.bfloat16(0))
    width = query_weight.shape[1] // 2

    y, z = bits[:1], bits[1:]
    unit = query_weight.shape[1] // 12
    plan = [(3 * unit, z[:1] + y + z[1:]), (5 * unit, y + z), (4 * unit, z + y)]
    state, first, after = [None] * len(plan), 0, []
    for group in ((2,), (0, 1)):
        chunks = [plan[i] for i in group]
        weight = kv_weight if 0 in group else None
        made = project(chunks, rows, ids, own_tokens, other_tokens, query_weight, weight, first, after)
        for i, pair in zip(group, made):
            state[i] = pair
        after = [made[0][0]]
        first += sum(columns for columns, _ in chunks)
    moving = [across(send, order[0]) for (send, _), (_, order) in zip(state, plan)]
    for step in range(len(bits)):
        for i in (2, 0, 1):
            columns, order = plan[i]
            total = state[i][1] + moving[i]
            if i == 0 and step == 0:
                cuts = [(0, cut) for cut in cuts_of(value_cache)]
                values, zero = load([value_cache], cuts, [state[2][0]], 46, total.shape[1])
                total = total + zero
            if step + 1 < len(bits):
                cut = total.shape[0] // 2
                state[i] = (total[cut:], total[:cut])
                moving[i] = across(state[i][0], order[step + 1])
            else:
                state[i] = total
    kv_width = kv_weight.shape[1] // 2
    by_column = [i for group in ((2,), (0, 1)) for i in group]
    total = jnp.concatenate([state[i] for i in by_column], axis=1)
    mine = lax.dynamic_slice_in_dim(total, core * own_rows, own_rows, 0).astype(jnp.bfloat16)
    give = lax.dynamic_slice_in_dim(total, (1 - core) * own_rows, own_rows, 0).astype(jnp.bfloat16)
    kv_column = sum(plan[i][0] for i in by_column[: by_column.index(0)])
    own, other = attend(core, lengths, mine, swap(give), kv_column, key_cache, values)
    got = swap(other)
    block = jnp.where(core == 0, jnp.concatenate([own, got]), jnp.concatenate([got, own]))

    near = [block[:, :width], block[:, width:]]
    far = [None, None]
    paths = [bits[::-1], bits[:1] + bits[:0:-1]]
    out_cuts, out_held = cuts_of(out_weight), []
    early = len(out_cuts) * 9 // 18
    for step in range(len(bits)):
        for i in range(2):
            if step:
                near[i] = jnp.concatenate([near[i], far[i]])
                if i == 0 and out_held:
                    near[i] = near[i] + zero.astype(jnp.bfloat16)
                if i == 1 and step + 2 >= len(bits):
                    part = out_cuts[early:] if out_held else out_cuts[:early]
                    held, zero = load([out_weight], [(0, cut) for cut in part], near, 36, width)
                    out_held += held
            far[i] = across(near[i], paths[i][step])
    orders = [order_of(path[::-1]) for path in paths]
    blocks = [b for pair in zip(near, far) for b in pair]
    send, keep = project_out(orders, rows, ids, blocks, out_held, out_cuts, (0, out_weight.shape[1]), [])
    return (keep + swap(send)).astype(jnp.bfloat16)


def solution(mesh):
    return jax.shard_map(
        local,
        mesh=mesh,
        in_specs=(
            P(("grp", "gy"), "gx"),
            P("gx", "gy"),
            P("gx", None),
            P("gy", "gx"),
            P(("grp", "gx", "gy"), None, None),
            P(("grp", "gx", "gy"), None, None),
            P(("grp", "gx", "gy")),
        ),
        out_specs=P(("grp", "gy"), "gx"),
        check_vma=False,
    )
```

```python
import functools

import jax
import jax.numpy as jnp
from jax import lax
from jax.experimental import pallas as pl
from jax.experimental.pallas import tpu as pltpu
from jax.sharding import PartitionSpec as P

H = 24
DH = 256
MIB = 1024 * 1024
HBM = pl.BlockSpec(memory_space=pltpu.HBM)
ANY = pl.BlockSpec(memory_space=pl.ANY)
VMEM = pl.BlockSpec(memory_space=pltpu.VMEM)
SMEM = pl.BlockSpec(memory_space=pltpu.SMEM)


class InOrder:
    def __init__(self, copies, ahead):
        self.copies, self.ahead = copies, ahead
        for copy in copies[:ahead]:
            copy.start()

    def wait(self, at):
        self.copies[at].wait()
        if at + self.ahead < len(self.copies):
            self.copies[at + self.ahead].start()


def order_of(bits):
    order = [0]
    for bit in reversed(bits):
        order = order + [j + bit for j in order]
    return order


def cuts_of(array):
    if len(array.shape) == 3:
        return [(at, None) for at in range(array.shape[0])]
    depth, columns = array.shape
    tall, wide = 512, (768 if columns % 768 == 0 else columns)
    return [
        ((at, tall), (column, wide)) for at in range(0, depth, tall) for column in range(0, columns, wide)
    ]


def piece_of(array, cut):
    if cut[1] is None:
        shape = array.shape[1:]
    else:
        shape = (cut[0][1], cut[1][1])
    return jax.ShapeDtypeStruct(shape, array.dtype)


def fetches(refs, cuts, targets, sems):
    copies = []
    for ref, cut in cuts:
        source = refs[ref]
        view = source.at[cut[0]] if cut[1] is None else source.at[pl.ds(*cut[0]), pl.ds(*cut[1])]
        copies.append(pltpu.make_async_copy(view, targets[len(copies)], sems.at[len(copies)]))
    return copies


def load_kernel(after, cuts, count, *refs):
    refs = refs[after:]
    in_refs, out_refs, zero_ref, sems = refs[:count], refs[count:-2], refs[-2], refs[-1]
    copies = fetches(in_refs, cuts, out_refs, sems)
    for copy in copies:
        copy.start()
    zero_ref[...] = jnp.zeros_like(zero_ref)
    for copy in copies:
        copy.wait()


def load(arrays, cuts, after, grant, zeros=128):
    shapes = [piece_of(arrays[at], cut) for at, cut in cuts]
    *held, zero = pl.pallas_call(
        functools.partial(load_kernel, len(after), cuts, len(arrays)),
        out_shape=(*shapes, jax.ShapeDtypeStruct((1, zeros), jnp.float32)),
        in_specs=[ANY] * len(after) + [HBM] * len(arrays),
        out_specs=[VMEM] * (len(cuts) + 1),
        scratch_shapes=[pltpu.SemaphoreType.DMA((len(cuts),))],
        compiler_params=pltpu.CompilerParams(vmem_limit_bytes=grant * MIB),
        cost_estimate=pl.CostEstimate(
            flops=0, bytes_accessed=sum(4 * s.shape[0] * s.shape[1] for s in shapes), transcendentals=0
        ),
        name="load",
    )(*after, *arrays)
    return held, zero


def spans_of(width):
    return [(at, min(768, width - at)) for at in range(0, width, 768)]


def project_kernel(orders, rows, first, widths, kv_width, after, ids_ref, own_ref, other_ref, w_ref, *refs):
    refs = list(refs)
    kv_ref = refs.pop(0) if kv_width else None
    outs, (xs_ref, ws_ref, w_sem) = refs[after:-3], refs[-3:]
    n = len(orders[0])
    half = n // 2
    me, core = ids_ref[0], ids_ref[1]
    features = xs_ref.shape[1]

    tiles, copies, at, source = [], [], 0, first
    depth = 768 if features % 768 == 0 else features

    def fetch(from_ref, column, width):
        for part in range(features // depth):
            span = pl.ds(part * depth, depth)
            copies.append(
                pltpu.make_async_copy(
                    from_ref.at[span, pl.ds(column, width)],
                    ws_ref.at[span, pl.ds(at, width)],
                    w_sem.at[len(copies)],
                )
            )

    for chunk, width in enumerate(widths):
        column = 0
        if kv_width and chunk == 0:
            fetch(kv_ref, pl.multiple_of(core * kv_width, kv_width), kv_width)
            tiles.append((chunk, 0, at, kv_width))
            at += kv_width
            column = kv_width
        for offset, tile in spans_of(width):
            fetch(w_ref, source, tile)
            tiles.append((chunk, column + offset, at, tile))
            at += tile
            source += tile
    per_tile = features // depth
    weights = InOrder(copies, 9)
    def place_rows(low_ref, high_ref):
        for j in range(n):
            block = jnp.bitwise_xor(me, j) % half
            source = low_ref if j < half else high_ref
            xs_ref[j * rows : (j + 1) * rows, :] = source[
                pl.ds(pl.multiple_of(block * rows, rows), rows), :
            ]

    low_mine = me // half == core

    @pl.when(low_mine)
    def _():
        place_rows(own_ref, other_ref)

    @pl.when(jnp.logical_not(low_mine))
    def _():
        place_rows(other_ref, own_ref)

    for t, (chunk, column, at, width) in enumerate(tiles):
        for part in range(per_tile):
            weights.wait(t * per_tile + part)
        total = jnp.dot(xs_ref[...], ws_ref[:, at : at + width], preferred_element_type=jnp.float32)
        span = slice(column, column + width)
        for p, j in enumerate(orders[chunk]):
            out = outs[2 * chunk + 1] if p < half else outs[2 * chunk]
            out[(p % half) * rows : (p % half + 1) * rows, span] = total[j * rows : (j + 1) * rows]


def project(plan, rows, ids, tokens, other, query_weight, kv_weight, first, after):
    features = tokens.shape[1]
    orders = [order_of(bits) for _, bits in plan]
    widths = [width for width, _ in plan]
    n = len(orders[0])
    kv_width = kv_weight.shape[1] // 2 if kv_weight is not None else 0
    columns = sum(widths) + kv_width
    outs = []
    for chunk, width in enumerate(widths):
        shape = (n * rows // 2, width + (0 if chunk else kv_width))
        outs += [jax.ShapeDtypeStruct(shape, jnp.float32)] * 2
    weights = [query_weight] + ([kv_weight] if kv_width else [])
    parts = features // 768 if features % 768 == 0 else 1
    copies = parts * (len(weights) - 1 + sum(len(spans_of(width)) for width in widths))
    outs = pl.pallas_call(
        functools.partial(project_kernel, orders, rows, first, widths, kv_width, len(after)),
        out_shape=outs,
        in_specs=[SMEM, VMEM, VMEM] + [HBM] * len(weights) + [ANY] * len(after),
        out_specs=[VMEM] * len(outs),
        scratch_shapes=[
            pltpu.VMEM((n * rows, features), tokens.dtype),
            pltpu.VMEM((features, columns), tokens.dtype),
            pltpu.SemaphoreType.DMA((copies,)),
        ],
        compiler_params=pltpu.CompilerParams(vmem_limit_bytes=46 * MIB),
        cost_estimate=pl.CostEstimate(
            flops=2 * n * rows * features * columns,
            bytes_accessed=2 * features * columns + 4 * n * rows * columns,
            transcendentals=0,
        ),
        name="project",
    )(ids, tokens, other, *weights, *after)
    return list(zip(outs[::2], outs[1::2]))


def attend_kernel(kv_column, scalars_ref, own_q, other_q, *refs):
    k_ref, refs = refs[0], refs[1:]
    v_refs, (own_out, other_out, q_scr, o_scr) = refs[:-4], refs[-4:]
    core = scalars_ref[0]
    rows, positions, _ = k_ref.shape
    at = 0
    for ref in (own_q, other_q):
        for column in range(0, ref.shape[1], DH):
            if column != kv_column:
                q_scr[:, at, :] = DH**-0.5 * ref[:, column : column + DH].astype(jnp.float32)
                at += 1
    total_heads = at
    first = own_q[:, kv_column : kv_column + DH].astype(jnp.float32)
    second = other_q[:, kv_column : kv_column + DH].astype(jnp.float32)
    new_keys = jnp.where(core == 0, first, second)
    new_values = jnp.where(core == 0, second, first)
    for row in range(rows):
        query = q_scr[row]
        scores = lax.dot_general(
            query.astype(jnp.bfloat16),
            k_ref[row],
            (((1,), (1,)), ((), ())),
            preferred_element_type=jnp.float32,
        )
        self_score = jnp.sum(query * new_keys[row : row + 1], axis=1, keepdims=True)
        visible = lax.broadcasted_iota(jnp.int32, scores.shape, 1) < scalars_ref[1 + row]
        masked = jnp.where(visible, scores, jnp.float32(-1e30))
        peak = jnp.maximum(jnp.max(masked, axis=1, keepdims=True), self_score)
        raised = jnp.exp(masked - peak)
        self_raised = jnp.exp(self_score - peak)
        inverse = 1.0 / (jnp.sum(raised, axis=1, keepdims=True) + self_raised)
        weights = (raised * inverse).astype(jnp.bfloat16)
        self_weight = (self_raised * inverse).astype(jnp.bfloat16).astype(jnp.float32)
        total = jnp.dot(weights, v_refs[row][...], preferred_element_type=jnp.float32)
        o_scr[row] = total + self_weight * new_values[row : row + 1]
    half = total_heads // 2
    for head in range(total_heads):
        ref = own_out if head < half else other_out
        column = (head % half) * DH
        ref[:, column : column + DH] = o_scr[:, head, :].astype(jnp.bfloat16)


def attend(core, lengths, own_q, other_q, kv_column, keys, values):
    rows, positions, _ = keys.shape
    heads = 2 * (own_q.shape[1] // DH - 1)
    out = jax.ShapeDtypeStruct((rows, heads * DH // 2), jnp.bfloat16)
    scalars = jnp.concatenate([core[None], lengths])
    return pl.pallas_call(
        functools.partial(attend_kernel, kv_column),
        out_shape=(out, out),
        in_specs=[SMEM] + [VMEM] * (3 + rows),
        out_specs=(VMEM, VMEM),
        scratch_shapes=[pltpu.VMEM((rows, heads, DH), jnp.float32)] * 2,
        compiler_params=pltpu.CompilerParams(vmem_limit_bytes=44 * MIB),
        cost_estimate=pl.CostEstimate(
            flops=4 * rows * heads * positions * DH,
            bytes_accessed=4 * rows * positions * DH,
            transcendentals=rows * heads * positions,
        ),
        name="attend",
    )(scalars, own_q, other_q, keys, *values)


def output_kernel(orders, rows, columns, pieces, after, ids_ref, *refs):
    count = 2 * len(orders)
    block_refs, w_refs = refs[:count], refs[count : count + len(pieces)]
    send_ref, keep_ref, xs_ref = refs[count + len(pieces) + after :]
    depth = block_refs[0].shape[1]
    me, core = ids_ref[0], ids_ref[1]
    n = len(orders[0])
    half = n // 2
    for group, (near_ref, far_ref) in enumerate(zip(block_refs[::2], block_refs[1::2])):
        for p, j in enumerate(orders[group]):
            block = jnp.bitwise_xor(me, j)
            place = block % half + jnp.where(block // half == core, half, 0)
            source = near_ref if p < half else far_ref
            at = (p % half) * rows
            xs_ref[
                pl.ds(pl.multiple_of(place * rows, rows), rows), group * depth : (group + 1) * depth
            ] = source[at : at + rows, :]
    cut = half * rows
    totals = {}
    for w_ref, ((first, tall), span) in zip(w_refs, pieces):
        part = jnp.dot(
            xs_ref[:, first : first + tall], w_ref[...], preferred_element_type=jnp.float32
        )
        totals[span] = totals[span] + part if span in totals else part
    for (column, width), total in totals.items():
        send_ref[:, column - columns[0] : column - columns[0] + width] = total[:cut]
        keep_ref[:, column - columns[0] : column - columns[0] + width] = total[cut:]


def project_out(orders, rows, ids, blocks, held, cuts, columns, after):
    chosen = [at for at, (_, (column, _)) in enumerate(cuts) if columns[0] <= column < sum(columns)]
    weights, pieces = [held[at] for at in chosen], [cuts[at] for at in chosen]
    pieces, weights = zip(*sorted(zip(pieces, weights), key=lambda pair: (pair[0][1], pair[0][0])))
    depth = len(orders) * blocks[0].shape[1]
    n = len(orders[0])
    out = jax.ShapeDtypeStruct((n * rows // 2, columns[1]), jnp.float32)
    return pl.pallas_call(
        functools.partial(output_kernel, orders, rows, columns, pieces, len(after)),
        out_shape=(out, out),
        in_specs=[SMEM] + [VMEM] * (len(blocks) + len(weights)) + [ANY] * len(after),
        out_specs=(VMEM, VMEM),
        scratch_shapes=[pltpu.VMEM((n * rows, depth), jnp.bfloat16)],
        compiler_params=pltpu.CompilerParams(vmem_limit_bytes=12 * MIB),
        cost_estimate=pl.CostEstimate(
            flops=2 * n * rows * depth * columns[1],
            bytes_accessed=2 * depth * columns[1] + 4 * n * rows * columns[1],
            transcendentals=0,
        ),
        name="project_out",
    )(ids, *blocks, *weights, *after)


def local(tokens, query_weight, kv_weight, out_weight, key_cache, value_cache, lengths):
    n = lax.axis_size("gx")
    me = lax.axis_index("gx").astype(jnp.int32)
    core = lax.axis_index("gy").astype(jnp.int32)
    ids = jnp.stack([me, core])
    own_rows = key_cache.shape[0]
    rows = 2 * own_rows
    bits = [1 << i for i in range(n.bit_length() - 1)]

    def swap(array):
        return lax.ppermute(array, "gy", [(0, 1), (1, 0)])

    def across(array, mask):
        return lax.ppermute(array, "gx", [(g, g ^ mask) for g in range(n)])

    other_tokens = swap(tokens)
    own_tokens = jnp.where(me < n, tokens, jnp.bfloat16(0))
    width = query_weight.shape[1] // 2

    y, z = bits[:1], bits[1:]
    unit = query_weight.shape[1] // 12
    plan = [(3 * unit, z[:1] + y + z[1:]), (5 * unit, y + z), (4 * unit, z + y)]
    state, first, after = [None] * len(plan), 0, []
    for group in ((2,), (0, 1)):
        chunks = [plan[i] for i in group]
        weight = kv_weight if 0 in group else None
        made = project(chunks, rows, ids, own_tokens, other_tokens, query_weight, weight, first, after)
        for i, pair in zip(group, made):
            state[i] = pair
        after = [made[0][0]]
        first += sum(columns for columns, _ in chunks)
    moving = [across(send, order[0]) for (send, _), (_, order) in zip(state, plan)]
    for step in range(len(bits)):
        for i in (2, 0, 1):
            columns, order = plan[i]
            total = state[i][1] + moving[i]
            if i == 0 and step == 0:
                cuts = [(0, cut) for cut in cuts_of(value_cache)]
                values, zero = load([value_cache], cuts, [state[2][0]], 46, total.shape[1])
                total = total + zero
            if step + 1 < len(bits):
                cut = total.shape[0] // 2
                state[i] = (total[cut:], total[:cut])
                moving[i] = across(state[i][0], order[step + 1])
            else:
                state[i] = total
    kv_width = kv_weight.shape[1] // 2
    by_column = [i for group in ((2,), (0, 1)) for i in group]
    total = jnp.concatenate([state[i] for i in by_column], axis=1)
    mine = lax.dynamic_slice_in_dim(total, core * own_rows, own_rows, 0).astype(jnp.bfloat16)
    give = lax.dynamic_slice_in_dim(total, (1 - core) * own_rows, own_rows, 0).astype(jnp.bfloat16)
    kv_column = sum(plan[i][0] for i in by_column[: by_column.index(0)])
    own, other = attend(core, lengths, mine, swap(give), kv_column, key_cache, values)
    got = swap(other)
    block = jnp.where(core == 0, jnp.concatenate([own, got]), jnp.concatenate([got, own]))

    near = [block[:, :width], block[:, width:]]
    far = [None, None]
    paths = [bits[::-1], bits[:1] + bits[:0:-1]]
    out_cuts, out_held = cuts_of(out_weight), []
    early = len(out_cuts) * 9 // 18
    for step in range(len(bits)):
        for i in range(2):
            if step:
                near[i] = jnp.concatenate([near[i], far[i]])
                if i == 0 and out_held:
                    near[i] = near[i] + zero.astype(jnp.bfloat16)
                if i == 1 and step + 2 >= len(bits):
                    part = out_cuts[early:] if out_held else out_cuts[:early]
                    held, zero = load([out_weight], [(0, cut) for cut in part], near, 36, width)
                    out_held += held
            far[i] = across(near[i], paths[i][step])
    orders = [order_of(path[::-1]) for path in paths]
    blocks = [b for pair in zip(near, far) for b in pair]
    send, keep = project_out(orders, rows, ids, blocks, out_held, out_cuts, (0, out_weight.shape[1]), [])
    return (keep + swap(send)).astype(jnp.bfloat16)


def solution(mesh):
    return jax.shard_map(
        local,
        mesh=mesh,
        in_specs=(
            P(("grp", "gy"), "gx"),
            P("gx", "gy"),
            P("gx", None),
            P("gy", "gx"),
            P(("grp", "gx", "gy"), None, None),
            P(("grp", "gx", "gy"), None, None),
            P(("grp", "gx", "gy")),
        ),
        out_specs=P(("grp", "gy"), "gx"),
        check_vma=False,
    )
```
